256 devices in a mesh: slab: 32 (over x, y, core), grp: 8 (over z).
Axes of the slice: x: 4, y: 4, z: 8, core: 2. Of those that a mesh axis runs over, the one named last changes fastest.
Arguments:
- stay: float32 [7, 524288], P(None, ('slab', 'grp'))
- leave: float32 [7, 2097152], P(None, ('slab', 'grp'))
- stay_flag: int32 [524288], P(('slab', 'grp')), may hold values 0 or 1
- send_list: int32 [256, 32, 2], P(('slab', 'grp')), may hold values from 0 to 63, as said below
- send_count: int32 [256, 32], P(('slab', 'grp')), may hold values from 0 to 2, as said below
- wanted: int32 [256, 8, 4], P(('slab', 'grp')), may hold values from 0 to 79
- pair_tiles: int32 [256, 2, 256], P(('slab', 'grp')), may hold values from 0 to 79, as said below
- pair_count: int32 [256], P(('slab', 'grp')), may hold values from 64 to 256, as said below
Outputs:
- density: float32 [2621440], P(('slab', 'grp'))
- accel: float32 [3, 2621440], P(None, ('slab', 'grp'))
The draws below stay inside these ranges and needn't reach their ends.
Inputs may be any that keep to these rules, and one draw needn't show every extreme that they name: `send_list`: each device's lists, read in order, are a permutation of its candidate blocks 0 to 63. `send_count`: zero for the device's own slab; every device sends 2 blocks to the next slab (the last slab to the previous one). `pair_tiles`: row 0 names resident blocks below 80, row 1 neighbour blocks below 40; on every device slot 0 names one of the 4 blocks from the lower slab and slot 1 one of the 4 blocks from the upper slab. `pair_count`: some device fills all 256 slots.
All inputs are finite; a program needn't handle non-finite values. No bound on the sum of `stay_flag` on one device may be relied on, other than what follows from the above.
Results may differ from the reference program's by a relative error of at most 0.0003.
Values sent between devices are 32-bit elements; how exact they have to be, the bound alone decides.
A program may use at most 64 MiB of HBM per device.

```python
import math
import jax
import jax.numpy as jnp
from jax import lax

BLK = 128
NSTAY = 16
SM = 2
GH = 4
NEED = 4
PAIR_MAX = 256
BATCH = 32
RES = 80
NJ = 40
STAY_ROWS = 524288
LEAVE_ROWS = 2097152
N_SLAB = 32
N_GRP = 8


def particle_rows(key, count, normal_speed, mass_lo, mass_hi):
    keys = jax.random.split(key, 4)
    place = jax.random.uniform(keys[0], (3, count), jnp.float32, 2.5, 5.5)
    speed = normal_speed * jax.random.normal(keys[1], (3, count), jnp.float32)
    lograng = jax.random.uniform(keys[3], (1, count), jnp.float32, jnp.log(mass_lo), jnp.log(mass_hi))
    return jnp.concatenate([place, speed, jnp.exp(lograng)], 0)


def draw_stay(key, part):
    key = jax.random.fold_in(key, 11)
    return particle_rows(key, STAY_ROWS, 0.5, 0.1, 0.4)


def draw_leave(key, part):
    key = jax.random.fold_in(key, 12)
    return particle_rows(key, LEAVE_ROWS, 0.5, 0.1, 0.4)


def draw_send_list(key, part):
    key = jax.random.fold_in(key, 13)
    keys = jax.random.split(key, N_SLAB * N_GRP)
    orders = jax.vmap(lambda one: jax.random.permutation(one, N_SLAB * SM))(keys)
    return orders.reshape(N_SLAB * N_GRP, N_SLAB, SM).astype(jnp.int32)


def draw_send_count(key, part):
    key = jax.random.fold_in(key, 14)
    counts = jax.random.randint(key, (N_SLAB * N_GRP, N_SLAB), 0, SM + 1)
    slab_of = jnp.arange(N_SLAB * N_GRP) // N_GRP
    target = jnp.where(slab_of < N_SLAB - 1, slab_of + 1, slab_of - 1)
    column = jnp.arange(N_SLAB)[None, :]
    counts = jnp.where(column == target[:, None], SM, counts)
    counts = jnp.where(column == slab_of[:, None], 0, counts)
    return counts.astype(jnp.int32)


def draw_pair_tiles(key, part):
    key = jax.random.fold_in(key, 15)
    keys = jax.random.split(key, 4)
    left = jax.random.randint(keys[0], (N_SLAB * N_GRP, 1, PAIR_MAX), 0, RES)
    right = jax.random.randint(keys[1], (N_SLAB * N_GRP, 1, PAIR_MAX), 0, NJ)
    lower = N_GRP * NEED + jax.random.randint(keys[2], (N_SLAB * N_GRP,), 0, GH)
    upper = N_GRP * NEED + GH + jax.random.randint(keys[3], (N_SLAB * N_GRP,), 0, GH)
    slot = jnp.arange(PAIR_MAX)[None, :]
    flat_right = right[:, 0, :]
    flat_right = jnp.where(slot == 0, lower[:, None], flat_right)
    flat_right = jnp.where(slot == 1, upper[:, None], flat_right)
    return jnp.concatenate([left, flat_right[:, None, :]], 1).astype(jnp.int32)


def draw_pair_count(key, part):
    key = jax.random.fold_in(key, 16)
    keys = jax.random.split(key, 2)
    counts = jax.random.randint(keys[0], (N_SLAB * N_GRP,), PAIR_MAX // 4, PAIR_MAX + 1)
    fullest = jax.random.randint(keys[1], (), 0, N_SLAB * N_GRP)
    counts = jnp.where(jnp.arange(N_SLAB * N_GRP) == fullest, PAIR_MAX, counts)
    return counts.astype(jnp.int32)


def place_ends(result, own_key, low, high):
    extent = result.shape
    spot = [jax.random.randint(jax.random.fold_in(own_key, axis), (), 0, extent[axis]) for axis in range(len(extent))]
    result = result.at[tuple(spot)].set(low)
    longest = extent.index(max(extent))
    spot[longest] = (spot[longest] + 1) % extent[longest]
    return result.at[tuple(spot)].set(high)


def setup_inputs(seed: int = 0) -> dict:
    splits = jax.random.split(jax.random.key(seed), 9)
    stay = draw_stay(jax.random.fold_in(splits[8], 71), 0)
    leave = draw_leave(jax.random.fold_in(splits[8], 71), 0)
    stay_flag = place_ends((jax.random.randint(splits[2], (STAY_ROWS,), 0, 4) < 1).astype(jnp.int32), jax.random.fold_in(splits[2], 1), 0, 1)
    send_list = draw_send_list(jax.random.fold_in(splits[8], 71), 0)
    send_count = draw_send_count(jax.random.fold_in(splits[8], 71), 0)
    wanted = place_ends(jax.random.randint(splits[5], (N_SLAB * N_GRP, N_GRP, NEED), 0, RES), jax.random.fold_in(splits[5], 1), 0, RES - 1).astype(jnp.int32)
    pair_tiles = draw_pair_tiles(jax.random.fold_in(splits[8], 71), 0)
    pair_count = draw_pair_count(jax.random.fold_in(splits[8], 71), 0)
    return dict(stay=stay, leave=leave, stay_flag=stay_flag, send_list=send_list, send_count=send_count, wanted=wanted, pair_tiles=pair_tiles, pair_count=pair_count)


KERNEL_NORM = 21.0 / (16.0 * math.pi)
SMOOTH = 1.0
DENS_FLOOR = 0.5
STIFF = 0.02
VISCOUS = 0.1
GRAVITY = 1.0

def pair_geometry(left, right):
    offset = left[0:3, :, :, None] - right[0:3, :, None, :]
    radius2 = lax.optimization_barrier(jnp.sum(offset * offset, 0))
    ratio = jnp.sqrt(radius2) / SMOOTH
    shell = jnp.maximum(1.0 - 0.5 * ratio, 0.0)
    weight = KERNEL_NORM * shell ** 4 * (2.0 * ratio + 1.0)
    slope = -5.0 * KERNEL_NORM / (SMOOTH * SMOOTH) * shell ** 3
    return (offset, radius2, weight, slope)

def density_pass(resident3, neighbour, pairs, count, limit):

    def step(index, dens):
        start = index * BATCH
        left_idx = lax.dynamic_slice_in_dim(pairs[0], start, BATCH)
        right_idx = lax.dynamic_slice_in_dim(pairs[1], start, BATCH)
        valid = (start + jnp.arange(BATCH) < count).astype(jnp.float32)
        left = jnp.take(resident3, left_idx, axis=1)
        right = jnp.take(neighbour, right_idx, axis=1)
        offset, radius2, weight, slope = pair_geometry(left, right)
        contrib = lax.optimization_barrier(jnp.sum(weight * right[6][:, None, :], -1)) * valid[:, None]
        return dens.at[left_idx].add(contrib)
    start_dens = jnp.zeros((resident3.shape[1], resident3.shape[2]), jnp.float32)
    return lax.fori_loop(0, limit, step, start_dens)

def make_fields(dens, mass):
    inverse = 1.0 / jnp.maximum(dens, DENS_FLOOR)
    pressure = STIFF * (dens ** 7 - 1.0) * inverse * inverse
    return jnp.stack([pressure, mass * inverse], 0)

def force_pass(resident3, neighbour, own_fields, far_fields, pairs, count, limit):

    def step(index, acc):
        start = index * BATCH
        left_idx = lax.dynamic_slice_in_dim(pairs[0], start, BATCH)
        right_idx = lax.dynamic_slice_in_dim(pairs[1], start, BATCH)
        valid = (start + jnp.arange(BATCH) < count).astype(jnp.float32)
        left = jnp.take(resident3, left_idx, axis=1)
        right = jnp.take(neighbour, right_idx, axis=1)
        left_f = jnp.take(own_fields, left_idx, axis=1)
        right_f = jnp.take(far_fields, right_idx, axis=1)
        offset, radius2, weight, slope = pair_geometry(left, right)
        mass = right[6][:, None, :]
        press = -(left_f[0][:, :, None] + right_f[0][:, None, :]) * mass * slope
        visc = VISCOUS * mass * left_f[1][:, :, None] * right_f[1][:, None, :] * radius2 * slope / (radius2 + 0.01)
        dvel = left[3:6, :, :, None] - right[3:6, :, None, :]
        contrib = lax.optimization_barrier(jnp.sum(press[None] * offset + visc[None] * dvel, -1)) * valid[None, :, None]
        return acc.at[:, left_idx].add(contrib)
    start_acc = jnp.zeros((3, resident3.shape[1], resident3.shape[2]), jnp.float32)
    return lax.fori_loop(0, limit, step, start_acc)

def assemble(table, wanted):

    def one_slab(slab_rows, want):
        return jax.vmap(lambda names: slab_rows[jnp.arange(N_GRP)[:, None], names])(want)
    members = jax.vmap(one_slab)(table, wanted)
    shape = members.shape
    members = members.reshape(shape[0], shape[1], N_GRP * NEED, shape[4], shape[5])
    blank = jnp.zeros_like(table[:1])
    padded = jnp.concatenate([blank, table, blank], 0)
    left = padded[:-2, :, NSTAY - GH:NSTAY]
    right = padded[2:, :, :GH]
    return jnp.concatenate([members, left, right], 2)

def reference(stay, leave, stay_flag, send_list, send_count, wanted, pair_tiles, pair_count):
    devices = N_SLAB * N_GRP
    staying = stay.reshape(7, devices, NSTAY, BLK).transpose(1, 2, 0, 3)
    leaving = leave.reshape(7, devices, N_SLAB * SM, BLK).transpose(1, 2, 0, 3)
    picked = jax.vmap(lambda rows, names: rows[names])(leaving, send_list)
    live = jnp.arange(SM)[None, None, :] < send_count[:, :, None]
    outgoing = jnp.where(live[:, :, :, None, None], picked, 0.0)
    outgoing = outgoing.reshape(N_SLAB, N_GRP, N_SLAB, SM, 7, BLK)
    arrived = outgoing.transpose(2, 1, 0, 3, 4, 5).reshape(N_SLAB, N_GRP, N_SLAB * SM, 7, BLK)
    resident = jnp.concatenate([staying.reshape(N_SLAB, N_GRP, NSTAY, 7, BLK), arrived], 2)
    want = wanted.reshape(N_SLAB, N_GRP, N_GRP, NEED)
    neighbour = assemble(resident, want)
    res_flat = resident.reshape(devices, RES, 7, BLK).transpose(0, 2, 1, 3)
    nb_flat = neighbour.reshape(devices, NJ, 7, BLK).transpose(0, 2, 1, 3)
    limit = PAIR_MAX // BATCH

    def dens_one(items):
        return density_pass(items[0], items[1], items[2], items[3], limit)
    dens = lax.map(dens_one, (res_flat, nb_flat, pair_tiles, pair_count))
    fields = jax.vmap(make_fields)(dens, res_flat[:, 6])
    field_table = fields.transpose(0, 2, 1, 3).reshape(N_SLAB, N_GRP, RES, 2, BLK)
    far = assemble(field_table, want).reshape(devices, NJ, 2, BLK).transpose(0, 2, 1, 3)

    def force_one(items):
        return force_pass(items[0], items[1], items[2], items[3], items[4], items[5], limit)
    force = lax.map(force_one, (res_flat, nb_flat, fields, far, pair_tiles, pair_count))
    flags = stay_flag.reshape(devices, NSTAY * BLK).astype(jnp.float32)
    fluid = jnp.concatenate([1.0 - flags, jnp.ones((devices, N_SLAB * SM * BLK), jnp.float32)], 1)
    gravity = jnp.array([0.0, 0.0, -GRAVITY], jnp.float32)
    accel = (force.reshape(devices, 3, RES * BLK) + gravity[None, :, None]) * fluid[:, None, :]
    return (dens.reshape(-1), accel.transpose(1, 0, 2).reshape(3, -1))
```

```python
import functools
import math

import jax
import jax.numpy as jnp
from jax import lax
from jax.experimental import pallas as pl
from jax.experimental.pallas import tpu as pltpu
from jax.sharding import PartitionSpec as P

BLK = 128
SM = 2
GH = 4
NEED = 4
PAIR_MAX = 256
NSTAY = 16
RES = 80
NJ = 40
GROUPS = BLK // 8

KERNEL_NORM = 21.0 / (16.0 * math.pi)
SMOOTH = 1.0
HALF = 0.5 / SMOOTH
DENS_FLOOR = 0.5
STIFF = 0.02
VISCOUS = 0.1
GRAVITY = 1.0
TINY = 1e-30
SOFT = 0.01 * HALF * HALF
PRESS_SCALE = 5.0 * KERNEL_NORM / (SMOOTH * SMOOTH) / HALF
VISC_SCALE = -VISCOUS * 5.0 * KERNEL_NORM / (SMOOTH * SMOOTH)

VMEM = pl.BlockSpec(memory_space=pltpu.VMEM)
SMEM = pl.BlockSpec(memory_space=pltpu.SMEM)
LIMIT = 56 * 1024 * 1024


def pack_kernel(lists, counts, leave, out):
    for slab in range(lists.shape[1]):
        count = counts[0, slab]
        for k in range(SM):
            start = pl.multiple_of(lists[0, slab, k] * BLK, BLK)
            live = (count > k).astype(jnp.float32)
            keep = jnp.broadcast_to(live, (1, BLK))
            tile = leave[:, pl.ds(start, BLK)]
            out[slab * SM + k, 0:7, :] = jnp.where(keep > 0.5, tile, 0.0)
            out[slab * SM + k, 7:8, :] = keep


def shell_of(radius2):
    ratio = radius2 * lax.rsqrt(jnp.maximum(radius2, TINY))
    return jnp.maximum(1.0 - ratio, 0.0)


def weight_of(shell):
    square = shell * shell
    return square * square * (5.0 - 4.0 * shell)


def write_lists(count, pairs, res, nb, out):
    left = pairs[0:1, :]
    right = pairs[1:2, :]
    lane = lax.broadcasted_iota(jnp.int32, (1, PAIR_MAX), 1)
    res_live = res[:, 7, :]
    nb_live = nb[:, 7, :]
    res_live = jnp.concatenate([res_live, res_live], 1)
    nb_live = jnp.concatenate([nb_live, nb_live], 1)
    hit = lax.broadcasted_iota(jnp.int32, (RES, PAIR_MAX), 0) == left
    live_left = jnp.sum(jnp.where(hit, res_live, 0.0), 0, keepdims=True)
    hit = lax.broadcasted_iota(jnp.int32, (NJ, PAIR_MAX), 0) == right
    live_right = jnp.sum(jnp.where(hit, nb_live, 0.0), 0, keepdims=True)
    valid = jnp.where(lane < count, live_right, 0.0)
    heavy = valid * live_left
    light = valid * (1.0 - live_left)
    before = lax.broadcasted_iota(jnp.int32, (PAIR_MAX, PAIR_MAX), 0) < lax.broadcasted_iota(
        jnp.int32, (PAIR_MAX, PAIR_MAX), 1
    )
    blank = jnp.zeros((6, PAIR_MAX), jnp.float32)
    kinds = jnp.concatenate([heavy, light, blank], 0).astype(jnp.bfloat16)
    spots = jnp.dot(kinds, jnp.where(before, 1.0, 0.0).astype(jnp.bfloat16), preferred_element_type=jnp.float32)
    names = jnp.concatenate([left.astype(jnp.float32), right.astype(jnp.float32), blank], 0).astype(jnp.bfloat16)
    row = lax.broadcasted_iota(jnp.int32, (PAIR_MAX, PAIR_MAX), 0).astype(jnp.float32)
    sums = jnp.sum(jnp.concatenate([heavy, light, blank], 0), 1, keepdims=True)
    for kind, member in ((0, heavy), (1, light)):
        target = jnp.where(member > 0.5, spots[kind : kind + 1, :], -1.0)
        chosen = jnp.where(row == target, 1.0, 0.0).astype(jnp.bfloat16)
        packed = lax.dot_general(names, chosen, (((1,), (1,)), ((), ())), preferred_element_type=jnp.float32)
        amount = jnp.broadcast_to(sums[kind : kind + 1, :], (1, PAIR_MAX))
        filled = lane.astype(jnp.float32) < amount
        out[2 * kind : 2 * kind + 1, :] = jnp.where(filled, packed[0:1, :], float(RES)).astype(jnp.int32)
        out[2 * kind + 1 : 2 * kind + 2, :] = packed[1:2, :].astype(jnp.int32)
        out[4 + kind : 5 + kind, :] = amount.astype(jnp.int32)
    out[6:8, :] = jnp.zeros((2, PAIR_MAX), jnp.int32)


def write_columns(nb, table, fields):
    def one(j, carry):
        tile = nb[j]
        turned = jnp.transpose(tile, (1, 0))
        for spot, field in enumerate(fields):
            column = turned[:, field : field + 1]
            if field < 3:
                column = column * HALF
            table[j, spot] = jnp.broadcast_to(column, (BLK, BLK))
        return carry

    lax.fori_loop(0, NJ, one, 0)


def density_kernel(count, pairs, res, nb, dens_out, field_out, list_out, table, acc, origin, lists, sem):
    write_lists(count[0], pairs, res, nb, list_out)
    copy = pltpu.make_async_copy(list_out, lists, sem)
    copy.start()
    write_columns(nb, table, (0, 1, 2, 6))
    x, y, z = (nb[:, f, :] * HALF for f in range(3))
    alone = jnp.sum(weight_of(shell_of(x * x + y * y + z * z)) * nb[:, 6, :], 1, keepdims=True)
    origin[...] = jnp.zeros_like(origin)
    origin[:, 0, :] = jnp.broadcast_to(alone, (NJ, BLK))
    acc[...] = jnp.zeros_like(acc)
    copy.wait()

    def whole(step, carry):
        for u in range(2):
            i = lists[0, 2 * step + u]
            j = lists[1, 2 * step + u]
            ax, ay, az = (res[jnp.minimum(i, RES - 1), f : f + 1, :] * HALF for f in range(3))
            ax, ay, az = (jnp.broadcast_to(a, (8, BLK)) for a in (ax, ay, az))
            total = jnp.zeros((8, BLK), jnp.float32)
            for g in range(GROUPS):
                rows = pl.ds(8 * g, 8)
                dx = ax - table[j, 0, rows, :]
                dy = ay - table[j, 1, rows, :]
                dz = az - table[j, 2, rows, :]
                shell = shell_of(dx * dx + dy * dy + dz * dz)
                total = total + weight_of(shell) * table[j, 3, rows, :]
            acc[i] = acc[i] + total
        return carry

    lax.fori_loop(0, (lists[4, 0] + 1) // 2, whole, 0)

    def blank(n, carry):
        i = lists[2, n]
        acc[i] = acc[i] + origin[lists[3, n]]
        return carry

    lax.fori_loop(0, lists[5, 0], blank, 0)
    dens = jnp.sum(acc[0:RES], 1) * KERNEL_NORM
    dens_out[...] = dens
    inverse = 1.0 / jnp.maximum(dens, DENS_FLOOR)
    cube = dens * dens * dens
    field_out[:, 0, :] = STIFF * (cube * cube * dens - 1.0) * inverse * inverse
    field_out[:, 1, :] = res[:, 6, :] * inverse


def pieces(value):
    high = value.astype(jnp.bfloat16)
    rest = value - high.astype(jnp.float32)
    mid = rest.astype(jnp.bfloat16)
    low = (rest - mid.astype(jnp.float32)).astype(jnp.bfloat16)
    return high, mid, low


def two_pieces(value):
    high = value.astype(jnp.bfloat16)
    return high, (value - high.astype(jnp.float32)).astype(jnp.bfloat16)


def write_factors(nb, far, factors, centre):
    row = lax.broadcasted_iota(jnp.int32, (8, BLK), 0)
    upper = row < 3
    lower = (row >= 3) & (row < 6)
    scale = jnp.where(upper, HALF, 1.0)

    def one(j, carry):
        tile = nb[j]
        mass = jnp.broadcast_to(tile[6:7, :], (8, BLK))
        mid_of = jnp.where(upper, jnp.broadcast_to(tile[:, 0:1] * HALF, (8, BLK)), 0.0)
        centre[j] = mid_of
        place = tile * scale - mid_of
        q = jnp.broadcast_to(far[j, 0:1, :], (8, BLK))
        s = jnp.broadcast_to(far[j, 1:2, :], (8, BLK))
        m0 = jnp.where(upper, mass, jnp.where(lower, mass * s, 0.0))
        n0 = jnp.where(upper, mass * q, 0.0)
        parts = [pieces(v) for v in (m0, m0 * place, n0, n0 * place)]
        for p in range(3):
            for h in range(2):
                pair = jnp.concatenate(
                    [parts[2 * h][p].astype(jnp.float32), parts[2 * h + 1][p].astype(jnp.float32)], 0
                )
                top = jnp.concatenate([upper, upper], 0)
                first = jnp.where(top, pair, 0.0).astype(jnp.bfloat16)
                second = jnp.where(top, 0.0, pair).astype(jnp.bfloat16)
                rows = pl.ds(32 * p + 16 * h, 16)
                factors[j, rows, 0:BLK] = first
                factors[j, rows, BLK : 2 * BLK] = first
                factors[j, rows, 2 * BLK : 3 * BLK] = second
                factors[j, rows, 3 * BLK : 4 * BLK] = second
        return carry

    lax.fori_loop(0, NJ, one, 0)


def force_kernel(lists, res, nb, field, far, flag, out, table, acc, origin, factors, centre):
    write_columns(nb, table, (0, 1, 2))
    write_factors(nb, far, factors, centre)
    acc[...] = jnp.zeros_like(acc)
    row = lax.broadcasted_iota(jnp.int32, (8, BLK), 0)
    upper = row < 3
    lower = (row >= 3) & (row < 6)
    scale = jnp.where(upper, HALF, 1.0)

    x, y, z = (nb[:, f, :] * HALF for f in range(3))
    radius2 = x * x + y * y + z * z
    shell = shell_of(radius2)
    cube = shell * shell * shell * nb[:, 6, :]
    damp = cube * radius2 / (radius2 + SOFT) * far[:, 1, :]
    press = cube * far[:, 0, :]
    origin[...] = jnp.zeros_like(origin)
    for f, place in enumerate((x, y, z)):
        origin[:, f, :] = jnp.broadcast_to(jnp.sum(cube * place, 1, keepdims=True), (NJ, BLK))
        origin[:, 8 + f, :] = jnp.broadcast_to(jnp.sum(press * place, 1, keepdims=True), (NJ, BLK))
        origin[:, 3 + f, :] = jnp.broadcast_to(jnp.sum(damp * nb[:, 3 + f, :], 1, keepdims=True), (NJ, BLK))

    def coefficients(i):
        q = jnp.broadcast_to(field[i, 0:1, :], (8, BLK))
        s = jnp.broadcast_to(field[i, 1:2, :], (8, BLK))
        return jnp.where(upper, q, jnp.where(lower, s, 0.0))

    def whole(step, carry):
        for u in range(2):
            i = lists[0, 2 * step + u]
            j = lists[1, 2 * step + u]
            held = jnp.minimum(i, RES - 1)
            ax, ay, az = (res[held, f : f + 1, :] * HALF for f in range(3))
            ax, ay, az = (jnp.broadcast_to(a, (16, BLK)) for a in (ax, ay, az))
            cubes = []
            damps = []
            for g in range(GROUPS // 2):
                rows = pl.ds(16 * g, 16)
                dx = ax - table[j, 0, rows, :]
                dy = ay - table[j, 1, rows, :]
                dz = az - table[j, 2, rows, :]
                radius2 = dx * dx + dy * dy + dz * dz
                shell = shell_of(radius2)
                cube = shell * shell * shell
                soft = lax.rsqrt(radius2 + SOFT)
                cubes.append(two_pieces(cube))
                damps.append(two_pieces(cube * (radius2 * (soft * soft))))
            right = jnp.concatenate(
                [c[0] for c in cubes] + [c[1] for c in cubes] + [d[0] for d in damps] + [d[1] for d in damps], 0
            )
            sums = jnp.dot(factors[j], right, preferred_element_type=jnp.float32)
            sums = sums[0:32] + (sums[32:64] + sums[64:96])
            place = res[held] * scale - centre[j]
            part = coefficients(held) * (place * sums[0:8] - sums[8:16]) + (place * sums[16:24] - sums[24:32])
            acc[i] = acc[i] + part
        return carry

    lax.fori_loop(0, (lists[4, 0] + 1) // 2, whole, 0)

    def blank(n, carry):
        i = lists[2, n]
        j = lists[3, n]
        acc[i] = acc[i] - (coefficients(i) * origin[j, 0:8, :] + origin[j, 8:16, :])
        return carry

    lax.fori_loop(0, lists[5, 0], blank, 0)
    gravity = jnp.where(lax.broadcasted_iota(jnp.int32, (3, BLK), 0) == 2, -GRAVITY, 0.0)
    for b in range(RES):
        total = acc[b, 0:3, :] * PRESS_SCALE + acc[b, 3:6, :] * VISC_SCALE + gravity
        if b < NSTAY:
            total = total * (1.0 - flag[b : b + 1, :].astype(jnp.float32))
        out[:, b * BLK : (b + 1) * BLK] = total


def density_call(count, pairs, resident, neighbour):
    return pl.pallas_call(
        density_kernel,
        out_shape=(
            jax.ShapeDtypeStruct((RES, BLK), jnp.float32),
            jax.ShapeDtypeStruct((RES, 2, BLK), jnp.float32),
            jax.ShapeDtypeStruct((8, PAIR_MAX), jnp.int32),
        ),
        in_specs=[SMEM, VMEM, VMEM, VMEM],
        out_specs=(VMEM, VMEM, VMEM),
        scratch_shapes=[
            pltpu.VMEM((NJ, 4, BLK, BLK), jnp.float32),
            pltpu.VMEM((RES + 1, 8, BLK), jnp.float32),
            pltpu.VMEM((NJ, 8, BLK), jnp.float32),
            pltpu.SMEM((8, PAIR_MAX), jnp.int32),
            pltpu.SemaphoreType.DMA,
        ],
        compiler_params=pltpu.CompilerParams(vmem_limit_bytes=LIMIT),
    )(count, pairs, resident, neighbour)


def force_call(lists, resident, neighbour, field, far, flag):
    return pl.pallas_call(
        force_kernel,
        out_shape=jax.ShapeDtypeStruct((3, RES * BLK), jnp.float32),
        in_specs=[SMEM, VMEM, VMEM, VMEM, VMEM, VMEM],
        out_specs=VMEM,
        scratch_shapes=[
            pltpu.VMEM((NJ, 3, BLK, BLK), jnp.float32),
            pltpu.VMEM((RES + 1, 8, BLK), jnp.float32),
            pltpu.VMEM((NJ, 16, BLK), jnp.float32),
            pltpu.VMEM((NJ, 96, 4 * BLK), jnp.bfloat16),
            pltpu.VMEM((NJ, 8, BLK), jnp.float32),
        ],
        compiler_params=pltpu.CompilerParams(vmem_limit_bytes=LIMIT),
    )(lists, resident, neighbour, field, far, flag)


def on_device(stay, leave, stay_flag, send_list, send_count, wanted, pair_tiles, pair_count):
    slabs = send_list.shape[1]
    f32 = jnp.float32
    params = pltpu.CompilerParams(vmem_limit_bytes=LIMIT)
    asked = lax.all_to_all(wanted[0], "grp", split_axis=0, concat_axis=0, tiled=True)
    outgoing = pl.pallas_call(
        pack_kernel,
        out_shape=jax.ShapeDtypeStruct((slabs * SM, 8, BLK), f32),
        in_specs=[SMEM, SMEM, VMEM],
        out_specs=VMEM,
        compiler_params=params,
    )(send_list, send_count, leave)
    arrived = lax.all_to_all(outgoing, "slab", split_axis=0, concat_axis=0, tiled=True)
    kept = jnp.concatenate([stay, jnp.ones((1, stay.shape[1]), f32)], 0)
    kept = kept.reshape(8, NSTAY, BLK).transpose(1, 0, 2)
    ends = slabs - 1
    up = [(i, i + 1) for i in range(ends)]
    down = [(i + 1, i) for i in range(ends)]
    below = lax.ppermute(kept[-GH:], "slab", up)
    above = lax.ppermute(kept[:GH], "slab", down)
    resident = jnp.concatenate([kept, arrived], 0)
    names = asked.reshape(-1)
    members = lax.all_to_all(jnp.take(resident, names, axis=0), "grp", split_axis=0, concat_axis=0, tiled=True)
    neighbour = jnp.concatenate([members, below, above], 0)
    dens, field, lists = density_call(pair_count, pair_tiles[0], resident, neighbour)
    far_below = lax.ppermute(field[NSTAY - GH : NSTAY], "slab", up)
    far_above = lax.ppermute(field[:GH], "slab", down)
    far_members = lax.all_to_all(jnp.take(field, names, axis=0), "grp", split_axis=0, concat_axis=0, tiled=True)
    far = jnp.concatenate([far_members, far_below, far_above], 0)
    accel = force_call(lists, resident, neighbour, field, far, stay_flag.reshape(NSTAY, BLK))
    return (dens.reshape(-1), accel)


def solution(mesh):
    in_specs = (
        P(None, ("slab", "grp")),
        P(None, ("slab", "grp")),
        P(("slab", "grp")),
        P(("slab", "grp"), None, None),
        P(("slab", "grp"), None),
        P(("slab", "grp"), None, None),
        P(("slab", "grp"), None, None),
        P(("slab", "grp")),
    )
    out_specs = (P(("slab", "grp")), P(None, ("slab", "grp")))
    return jax.shard_map(
        on_device, mesh=mesh, in_specs=in_specs, out_specs=out_specs, check_vma=False
    )
```

```python
import functools
import math

import jax
import jax.numpy as jnp
from jax import lax
from jax.experimental import pallas as pl
from jax.experimental.pallas import tpu as pltpu
from jax.sharding import PartitionSpec as P

BLK = 128
SM = 2
GH = 4
NEED = 4
PAIR_MAX = 256
NSTAY = 16
RES = 80
NJ = 40
GROUPS = BLK // 8

KERNEL_NORM = 21.0 / (16.0 * math.pi)
SMOOTH = 1.0
HALF = 0.5 / SMOOTH
DENS_FLOOR = 0.5
STIFF = 0.02
VISCOUS = 0.1
GRAVITY = 1.0
TINY = 1e-30
SOFT = 0.01 * HALF * HALF
PRESS_SCALE = 5.0 * KERNEL_NORM / (SMOOTH * SMOOTH) / HALF
VISC_SCALE = -VISCOUS * 5.0 * KERNEL_NORM / (SMOOTH * SMOOTH)

VMEM = pl.BlockSpec(memory_space=pltpu.VMEM)
SMEM = pl.BlockSpec(memory_space=pltpu.SMEM)
MESH = pl.DeviceIdType.MESH
LIMIT = 56 * 1024 * 1024


def migrate_kernel(
    slabs, members, lists, counts, wanted, leave, stay,
    res_out, nb_out, asked_out,
    packed, res, nb, request, asked, names, chosen,
    row_send, row_recv, ghost_send, ghost_recv, name_send, name_recv, near_send, near_recv, local_sem,
):
    slab = lax.axis_index("slab")
    grp = lax.axis_index("grp")
    ghosts = members * NEED
    barrier = pltpu.get_barrier_semaphore()

    def greet_slab(r, carry):
        pl.semaphore_signal(barrier, inc=1, device_id={"slab": (slab + r) % slabs}, device_id_type=MESH)
        return carry

    def greet_grp(r, carry):
        pl.semaphore_signal(barrier, inc=1, device_id={"grp": (grp + r) % members}, device_id_type=MESH)
        return carry

    lax.fori_loop(1, members, greet_grp, 0)
    lax.fori_loop(1, slabs, greet_slab, 0)

    row = lax.broadcasted_iota(jnp.int32, (8, BLK), 0)
    lane = lax.broadcasted_iota(jnp.int32, (8, BLK), 1)
    ask = jnp.zeros((8, BLK), jnp.int32)
    for p in range(members):
        for k in range(NEED):
            ask = jnp.where((row == p) & (lane == k), wanted[0, k, p], ask)
    request[...] = ask
    for b in range(NSTAY):
        res[b, 0:7, :] = stay[b]
        res[b, 7:8, :] = jnp.ones((1, BLK), jnp.float32)
    for t in range(slabs):
        count = counts[0, t]
        for k in range(SM):
            keep = jnp.broadcast_to(jnp.minimum(jnp.maximum(count - k, 0), 1), (1, BLK)).astype(jnp.float32)
            packed[t * SM + k, 0:7, :] = leave[lists[0, k, t]] * keep
            packed[t * SM + k, 7:8, :] = keep
    pl.semaphore_wait(barrier, slabs - 1 + members - 1)

    def name_copy(r):
        return pltpu.make_async_remote_copy(
            src_ref=request, dst_ref=asked.at[grp], send_sem=name_send.at[r], recv_sem=name_recv.at[r],
            device_id={"grp": (grp + r) % members}, device_id_type=MESH,
        )

    def row_copy(r):
        target = (slab + r) % slabs
        return pltpu.make_async_remote_copy(
            src_ref=packed.at[pl.ds(target * SM, SM)], dst_ref=res.at[pl.ds(NSTAY + slab * SM, SM)],
            send_sem=row_send.at[r], recv_sem=row_recv.at[r],
            device_id={"slab": target}, device_id_type=MESH,
        )

    def ghost_copy(side):
        first = NSTAY - GH if side == 0 else 0
        target = (slab + (1 if side == 0 else slabs - 1)) % slabs
        return pltpu.make_async_remote_copy(
            src_ref=res.at[pl.ds(first, GH)], dst_ref=nb.at[pl.ds(ghosts + side * GH, GH)],
            send_sem=ghost_send.at[side], recv_sem=ghost_recv.at[side],
            device_id={"slab": target}, device_id_type=MESH,
        )

    def near_copy(r):
        target = (grp + r) % members
        return pltpu.make_async_remote_copy(
            src_ref=chosen.at[target], dst_ref=nb.at[pl.ds(grp * NEED, NEED)],
            send_sem=near_send.at[r], recv_sem=near_recv.at[r],
            device_id={"grp": target}, device_id_type=MESH,
        )

    def each(first, last, step):
        def body(r, carry):
            step(r)
            return carry

        lax.fori_loop(first, last, body, 0)

    each(1, members, lambda r: name_copy(r).start())
    each(1, slabs, lambda r: row_copy(r).start())
    ghost_copy(0).start()
    ghost_copy(1).start()
    asked[grp] = request[...]
    mine = pl.ds(NSTAY + slab * SM, SM)
    res[mine] = packed[pl.ds(slab * SM, SM)]
    each(1, members, lambda r: name_copy(r).wait_recv())
    local = pltpu.make_async_copy(asked, names, local_sem)
    local.start()
    local.wait()
    each(1, slabs, lambda r: row_copy(r).wait_recv())
    for d in range(members):
        for k in range(NEED):
            chosen[d, k] = res[names[d, grp, k]]
    each(1, members, lambda r: near_copy(r).start())
    nb[pl.ds(grp * NEED, NEED)] = chosen[grp]
    res_out[...] = res[...]
    asked_out[...] = asked[...]
    ghost_copy(0).wait_recv()
    ghost_copy(1).wait_recv()
    inside = (slab > 0).astype(jnp.float32)
    nb_out[pl.ds(ghosts, GH)] = nb[pl.ds(ghosts, GH)] * inside
    inside = (slab < slabs - 1).astype(jnp.float32)
    nb_out[pl.ds(ghosts + GH, GH)] = nb[pl.ds(ghosts + GH, GH)] * inside
    each(1, members, lambda r: near_copy(r).wait_recv())
    nb_out[pl.ds(0, ghosts)] = nb[pl.ds(0, ghosts)]
    each(1, members, lambda r: name_copy(r).wait_send())
    each(1, slabs, lambda r: row_copy(r).wait_send())
    each(1, members, lambda r: near_copy(r).wait_send())
    ghost_copy(0).wait_send()
    ghost_copy(1).wait_send()


def migrate_call(slabs, members, lists, counts, wanted, leave, stay):
    blocks = NSTAY + slabs * SM
    near = members * NEED + 2 * GH
    f32 = jnp.float32
    dma = pltpu.SemaphoreType.DMA
    return pl.pallas_call(
        functools.partial(migrate_kernel, slabs, members),
        out_shape=(
            jax.ShapeDtypeStruct((blocks, 8, BLK), f32),
            jax.ShapeDtypeStruct((near, 8, BLK), f32),
            jax.ShapeDtypeStruct((members, 8, BLK), jnp.int32),
        ),
        in_specs=[SMEM, SMEM, SMEM, VMEM, VMEM],
        out_specs=(VMEM, VMEM, VMEM),
        scratch_shapes=[
            pltpu.VMEM((slabs * SM, 8, BLK), f32),
            pltpu.VMEM((blocks, 8, BLK), f32),
            pltpu.VMEM((near, 8, BLK), f32),
            pltpu.VMEM((8, BLK), jnp.int32),
            pltpu.VMEM((members, 8, BLK), jnp.int32),
            pltpu.SMEM((members, 8, BLK), jnp.int32),
            pltpu.VMEM((members, NEED, 8, BLK), f32),
            dma((slabs,)), dma((slabs,)), dma((2,)), dma((2,)),
            dma((members,)), dma((members,)), dma((members,)), dma((members,)), dma,
        ],
        compiler_params=pltpu.CompilerParams(collective_id=0, has_side_effects=True, vmem_limit_bytes=LIMIT),
    )(lists, counts, wanted, leave, stay)


def field_kernel(
    slabs, members, names, field, out, tiles, edges, far, near_send, near_recv, edge_send, edge_recv
):
    slab = lax.axis_index("slab")
    grp = lax.axis_index("grp")
    above = (slab + 1) % slabs
    below = (slab + slabs - 1) % slabs
    barrier = pltpu.get_barrier_semaphore()
    for r in range(1, members):
        pl.semaphore_signal(barrier, inc=1, device_id={"grp": (grp + r) % members}, device_id_type=MESH)
    for target in (above, below):
        pl.semaphore_signal(barrier, inc=1, device_id={"slab": target}, device_id_type=MESH)
    for d in range(members):
        for k in range(NEED):
            tiles[d, 2 * k : 2 * k + 2, :] = field[names[d, grp, k]]
    for k in range(GH):
        edges[0, 2 * k : 2 * k + 2, :] = field[NSTAY - GH + k]
        edges[1, 2 * k : 2 * k + 2, :] = field[k]
    pl.semaphore_wait(barrier, members + 1)

    def near_copy(r):
        target = (grp + r) % members
        return pltpu.make_async_remote_copy(
            src_ref=tiles.at[target], dst_ref=far.at[grp], send_sem=near_send.at[r], recv_sem=near_recv.at[r],
            device_id={"grp": target}, device_id_type=MESH,
        )

    def edge_copy(side):
        return pltpu.make_async_remote_copy(
            src_ref=edges.at[side], dst_ref=far.at[members + side],
            send_sem=edge_send.at[side], recv_sem=edge_recv.at[side],
            device_id={"slab": above if side == 0 else below}, device_id_type=MESH,
        )

    copies = [near_copy(r) for r in range(1, members)] + [edge_copy(0), edge_copy(1)]
    for copy in copies:
        copy.start()
    far[grp] = tiles[grp]
    for copy in copies:
        copy.wait_recv()
    out[0:members] = far[0:members]
    out[members] = far[members] * (slab > 0).astype(jnp.float32)
    out[members + 1] = far[members + 1] * (slab < slabs - 1).astype(jnp.float32)
    for copy in copies:
        copy.wait_send()


def field_call(slabs, members, names, field):
    f32 = jnp.float32
    dma = pltpu.SemaphoreType.DMA
    out = pl.pallas_call(
        functools.partial(field_kernel, slabs, members),
        out_shape=jax.ShapeDtypeStruct((members + 2, 8, BLK), f32),
        in_specs=[SMEM, VMEM],
        out_specs=VMEM,
        scratch_shapes=[
            pltpu.VMEM((members, 8, BLK), f32),
            pltpu.VMEM((2, 8, BLK), f32),
            pltpu.VMEM((members + 2, 8, BLK), f32),
            dma((members,)), dma((members,)), dma((2,)), dma((2,)),
        ],
        compiler_params=pltpu.CompilerParams(collective_id=1, has_side_effects=True, vmem_limit_bytes=LIMIT),
    )(names, field)
    return out.reshape(-1, BLK)


def shell_of(radius2):
    ratio = radius2 * lax.rsqrt(jnp.maximum(radius2, TINY))
    return jnp.maximum(1.0 - ratio, 0.0)


def weight_of(shell):
    square = shell * shell
    return square * square * (5.0 - 4.0 * shell)


def write_lists(count, pairs, res, nb, out):
    left = pairs[0:1, :]
    right = pairs[1:2, :]
    lane = lax.broadcasted_iota(jnp.int32, (1, PAIR_MAX), 1)
    res_live = res[:, 7, :]
    nb_live = nb[:, 7, :]
    res_live = jnp.concatenate([res_live, res_live], 1)
    nb_live = jnp.concatenate([nb_live, nb_live], 1)
    hit = lax.broadcasted_iota(jnp.int32, (RES, PAIR_MAX), 0) == left
    live_left = jnp.sum(jnp.where(hit, res_live, 0.0), 0, keepdims=True)
    hit = lax.broadcasted_iota(jnp.int32, (NJ, PAIR_MAX), 0) == right
    live_right = jnp.sum(jnp.where(hit, nb_live, 0.0), 0, keepdims=True)
    valid = jnp.where(lane < count, live_right, 0.0)
    heavy = valid * live_left
    light = valid * (1.0 - live_left)
    before = lax.broadcasted_iota(jnp.int32, (PAIR_MAX, PAIR_MAX), 0) < lax.broadcasted_iota(
        jnp.int32, (PAIR_MAX, PAIR_MAX), 1
    )
    blank = jnp.zeros((6, PAIR_MAX), jnp.float32)
    kinds = jnp.concatenate([heavy, light, blank], 0).astype(jnp.bfloat16)
    spots = jnp.dot(kinds, jnp.where(before, 1.0, 0.0).astype(jnp.bfloat16), preferred_element_type=jnp.float32)
    names = jnp.concatenate([left.astype(jnp.float32), right.astype(jnp.float32), blank], 0).astype(jnp.bfloat16)
    row = lax.broadcasted_iota(jnp.int32, (PAIR_MAX, PAIR_MAX), 0).astype(jnp.float32)
    sums = jnp.sum(jnp.concatenate([heavy, light, blank], 0), 1, keepdims=True)
    for kind, member in ((0, heavy), (1, light)):
        target = jnp.where(member > 0.5, spots[kind : kind + 1, :], -1.0)
        chosen = jnp.where(row == target, 1.0, 0.0).astype(jnp.bfloat16)
        packed = lax.dot_general(names, chosen, (((1,), (1,)), ((), ())), preferred_element_type=jnp.float32)
        amount = jnp.broadcast_to(sums[kind : kind + 1, :], (1, PAIR_MAX))
        filled = lane.astype(jnp.float32) < amount
        out[2 * kind : 2 * kind + 1, :] = jnp.where(filled, packed[0:1, :], float(RES)).astype(jnp.int32)
        out[2 * kind + 1 : 2 * kind + 2, :] = packed[1:2, :].astype(jnp.int32)
        out[4 + kind : 5 + kind, :] = amount.astype(jnp.int32)
    out[6:8, :] = jnp.zeros((2, PAIR_MAX), jnp.int32)


def write_columns(nb, table, fields):
    def one(j, carry):
        tile = nb[j]
        turned = jnp.transpose(tile, (1, 0))
        for spot, field in enumerate(fields):
            column = turned[:, field : field + 1]
            if field < 3:
                column = column * HALF
            table[j, spot] = jnp.broadcast_to(column, (BLK, BLK))
        return carry

    lax.fori_loop(0, NJ, one, 0)


def density_kernel(count, pairs, res, nb, dens_out, field_out, list_out, table, acc, origin, lists, sem):
    write_lists(count[0], pairs, res, nb, list_out)
    copy = pltpu.make_async_copy(list_out, lists, sem)
    copy.start()
    write_columns(nb, table, (0, 1, 2, 6))
    x, y, z = (nb[:, f, :] * HALF for f in range(3))
    alone = jnp.sum(weight_of(shell_of(x * x + y * y + z * z)) * nb[:, 6, :], 1, keepdims=True)
    origin[...] = jnp.zeros_like(origin)
    origin[:, 0, :] = jnp.broadcast_to(alone, (NJ, BLK))
    acc[...] = jnp.zeros_like(acc)
    copy.wait()

    def whole(step, carry):
        for u in range(2):
            i = lists[0, 2 * step + u]
            j = lists[1, 2 * step + u]
            ax, ay, az = (res[jnp.minimum(i, RES - 1), f : f + 1, :] * HALF for f in range(3))
            ax, ay, az = (jnp.broadcast_to(a, (8, BLK)) for a in (ax, ay, az))
            total = jnp.zeros((8, BLK), jnp.float32)
            for g in range(GROUPS):
                rows = pl.ds(8 * g, 8)
                dx = ax - table[j, 0, rows, :]
                dy = ay - table[j, 1, rows, :]
                dz = az - table[j, 2, rows, :]
                shell = shell_of(dx * dx + dy * dy + dz * dz)
                total = total + weight_of(shell) * table[j, 3, rows, :]
            acc[i] = acc[i] + total
        return carry

    lax.fori_loop(0, (lists[4, 0] + 1) // 2, whole, 0)

    def blank(n, carry):
        i = lists[2, n]
        acc[i] = acc[i] + origin[lists[3, n]]
        return carry

    lax.fori_loop(0, lists[5, 0], blank, 0)
    dens = jnp.sum(acc[0:RES], 1) * KERNEL_NORM
    dens_out[...] = dens
    inverse = 1.0 / jnp.maximum(dens, DENS_FLOOR)
    cube = dens * dens * dens
    field_out[:, 0, :] = STIFF * (cube * cube * dens - 1.0) * inverse * inverse
    field_out[:, 1, :] = res[:, 6, :] * inverse


def pieces(value):
    high = value.astype(jnp.bfloat16)
    rest = value - high.astype(jnp.float32)
    mid = rest.astype(jnp.bfloat16)
    low = (rest - mid.astype(jnp.float32)).astype(jnp.bfloat16)
    return high, mid, low


def two_pieces(value):
    high = value.astype(jnp.bfloat16)
    return high, (value - high.astype(jnp.float32)).astype(jnp.bfloat16)


def write_factors(nb, far, factors, centre):
    row = lax.broadcasted_iota(jnp.int32, (8, BLK), 0)
    upper = row < 3
    lower = (row >= 3) & (row < 6)
    scale = jnp.where(upper, HALF, 1.0)

    def one(j, carry):
        tile = nb[j]
        mass = jnp.broadcast_to(tile[6:7, :], (8, BLK))
        mid_of = jnp.where(upper, jnp.broadcast_to(tile[:, 0:1] * HALF, (8, BLK)), 0.0)
        centre[j] = mid_of
        place = tile * scale - mid_of
        q = jnp.broadcast_to(far[pl.ds(2 * j, 1), :], (8, BLK))
        s = jnp.broadcast_to(far[pl.ds(2 * j + 1, 1), :], (8, BLK))
        m0 = jnp.where(upper, mass, jnp.where(lower, mass * s, 0.0))
        n0 = jnp.where(upper, mass * q, 0.0)
        parts = [pieces(v) for v in (m0, m0 * place, n0, n0 * place)]
        for p in range(3):
            for h in range(2):
                pair = jnp.concatenate(
                    [parts[2 * h][p].astype(jnp.float32), parts[2 * h + 1][p].astype(jnp.float32)], 0
                )
                top = jnp.concatenate([upper, upper], 0)
                first = jnp.where(top, pair, 0.0).astype(jnp.bfloat16)
                second = jnp.where(top, 0.0, pair).astype(jnp.bfloat16)
                rows = pl.ds(32 * p + 16 * h, 16)
                factors[j, rows, 0:BLK] = first
                factors[j, rows, BLK : 2 * BLK] = first
                factors[j, rows, 2 * BLK : 3 * BLK] = second
                factors[j, rows, 3 * BLK : 4 * BLK] = second
        return carry

    lax.fori_loop(0, NJ, one, 0)


def force_kernel(lists, res, nb, field, far, flag, out, table, acc, origin, factors, centre):
    write_columns(nb, table, (0, 1, 2))
    write_factors(nb, far, factors, centre)
    acc[...] = jnp.zeros_like(acc)
    row = lax.broadcasted_iota(jnp.int32, (8, BLK), 0)
    upper = row < 3
    lower = (row >= 3) & (row < 6)
    scale = jnp.where(upper, HALF, 1.0)

    x, y, z = (nb[:, f, :] * HALF for f in range(3))
    radius2 = x * x + y * y + z * z
    shell = shell_of(radius2)
    cube = shell * shell * shell * nb[:, 6, :]
    damp = cube * radius2 / (radius2 + SOFT) * far[pl.ds(1, NJ, stride=2), :]
    press = cube * far[pl.ds(0, NJ, stride=2), :]
    origin[...] = jnp.zeros_like(origin)
    for f, place in enumerate((x, y, z)):
        origin[:, f, :] = jnp.broadcast_to(jnp.sum(cube * place, 1, keepdims=True), (NJ, BLK))
        origin[:, 8 + f, :] = jnp.broadcast_to(jnp.sum(press * place, 1, keepdims=True), (NJ, BLK))
        origin[:, 3 + f, :] = jnp.broadcast_to(jnp.sum(damp * nb[:, 3 + f, :], 1, keepdims=True), (NJ, BLK))

    def coefficients(i):
        q = jnp.broadcast_to(field[i, 0:1, :], (8, BLK))
        s = jnp.broadcast_to(field[i, 1:2, :], (8, BLK))
        return jnp.where(upper, q, jnp.where(lower, s, 0.0))

    def whole(step, carry):
        for u in range(2):
            i = lists[0, 2 * step + u]
            j = lists[1, 2 * step + u]
            held = jnp.minimum(i, RES - 1)
            ax, ay, az = (res[held, f : f + 1, :] * HALF for f in range(3))
            ax, ay, az = (jnp.broadcast_to(a, (16, BLK)) for a in (ax, ay, az))
            cubes = []
            damps = []
            for g in range(GROUPS // 2):
                rows = pl.ds(16 * g, 16)
                dx = ax - table[j, 0, rows, :]
                dy = ay - table[j, 1, rows, :]
                dz = az - table[j, 2, rows, :]
                radius2 = dx * dx + dy * dy + dz * dz
                shell = shell_of(radius2)
                cube = shell * shell * shell
                soft = lax.rsqrt(radius2 + SOFT)
                cubes.append(two_pieces(cube))
                damps.append(two_pieces(cube * (radius2 * (soft * soft))))
            right = jnp.concatenate(
                [c[0] for c in cubes] + [c[1] for c in cubes] + [d[0] for d in damps] + [d[1] for d in damps], 0
            )
            sums = jnp.dot(factors[j], right, preferred_element_type=jnp.float32)
            sums = sums[0:32] + (sums[32:64] + sums[64:96])
            place = res[held] * scale - centre[j]
            part = coefficients(held) * (place * sums[0:8] - sums[8:16]) + (place * sums[16:24] - sums[24:32])
            acc[i] = acc[i] + part
        return carry

    lax.fori_loop(0, (lists[4, 0] + 1) // 2, whole, 0)

    def blank(n, carry):
        i = lists[2, n]
        j = lists[3, n]
        acc[i] = acc[i] - (coefficients(i) * origin[j, 0:8, :] + origin[j, 8:16, :])
        return carry

    lax.fori_loop(0, lists[5, 0], blank, 0)
    gravity = jnp.where(lax.broadcasted_iota(jnp.int32, (3, BLK), 0) == 2, -GRAVITY, 0.0)
    for b in range(RES):
        total = acc[b, 0:3, :] * PRESS_SCALE + acc[b, 3:6, :] * VISC_SCALE + gravity
        if b < NSTAY:
            total = total * (1.0 - flag[b : b + 1, :].astype(jnp.float32))
        out[:, b * BLK : (b + 1) * BLK] = total


def density_call(count, pairs, resident, neighbour):
    return pl.pallas_call(
        density_kernel,
        out_shape=(
            jax.ShapeDtypeStruct((RES, BLK), jnp.float32),
            jax.ShapeDtypeStruct((RES, 2, BLK), jnp.float32),
            jax.ShapeDtypeStruct((8, PAIR_MAX), jnp.int32),
        ),
        in_specs=[SMEM, VMEM, VMEM, VMEM],
        out_specs=(VMEM, VMEM, VMEM),
        scratch_shapes=[
            pltpu.VMEM((NJ, 4, BLK, BLK), jnp.float32),
            pltpu.VMEM((RES + 1, 8, BLK), jnp.float32),
            pltpu.VMEM((NJ, 8, BLK), jnp.float32),
            pltpu.SMEM((8, PAIR_MAX), jnp.int32),
            pltpu.SemaphoreType.DMA,
        ],
        compiler_params=pltpu.CompilerParams(vmem_limit_bytes=LIMIT),
    )(count, pairs, resident, neighbour)


def force_call(lists, resident, neighbour, field, far, flag):
    return pl.pallas_call(
        force_kernel,
        out_shape=jax.ShapeDtypeStruct((3, RES * BLK), jnp.float32),
        in_specs=[SMEM, VMEM, VMEM, VMEM, VMEM, VMEM],
        out_specs=VMEM,
        scratch_shapes=[
            pltpu.VMEM((NJ, 3, BLK, BLK), jnp.float32),
            pltpu.VMEM((RES + 1, 8, BLK), jnp.float32),
            pltpu.VMEM((NJ, 16, BLK), jnp.float32),
            pltpu.VMEM((NJ, 96, 4 * BLK), jnp.bfloat16),
            pltpu.VMEM((NJ, 8, BLK), jnp.float32),
        ],
        compiler_params=pltpu.CompilerParams(vmem_limit_bytes=LIMIT),
    )(lists, resident, neighbour, field, far, flag)


def on_device(stay, leave, stay_flag, send_list, send_count, wanted, pair_tiles, pair_count):
    slabs = send_list.shape[1]
    members = wanted.shape[1]
    leaving = leave.reshape(7, slabs * SM, BLK).transpose(1, 0, 2)
    staying = stay.reshape(7, NSTAY, BLK).transpose(1, 0, 2)
    resident, neighbour, asked = migrate_call(
        slabs, members, send_list.transpose(0, 2, 1), send_count, wanted.transpose(0, 2, 1), leaving, staying
    )
    dens, field, lists = density_call(pair_count, pair_tiles[0], resident, neighbour)
    far = field_call(slabs, members, asked, field)
    accel = force_call(lists, resident, neighbour, field, far, stay_flag.reshape(NSTAY, BLK))
    return (dens.reshape(-1), accel)


def solution(mesh):
    in_specs = (
        P(None, ("slab", "grp")),
        P(None, ("slab", "grp")),
        P(("slab", "grp")),
        P(("slab", "grp"), None, None),
        P(("slab", "grp"), None),
        P(("slab", "grp"), None, None),
        P(("slab", "grp"), None, None),
        P(("slab", "grp")),
    )
    out_specs = (P(("slab", "grp")), P(None, ("slab", "grp")))
    return jax.shard_map(
        on_device, mesh=mesh, in_specs=in_specs, out_specs=out_specs, check_vma=False
    )
```

```python
import functools
import math

import jax
import jax.numpy as jnp
from jax import lax
from jax.experimental import pallas as pl
from jax.experimental.pallas import tpu as pltpu
from jax.sharding import PartitionSpec as P

BLK = 128
SM = 2
GH = 4
NEED = 4
PAIR_MAX = 256
NSTAY = 16
RES = 80
NJ = 40
GROUPS = BLK // 8
COLUMN_STEP = 8
STEP = 4
FACTOR_STEP = 4

KERNEL_NORM = 21.0 / (16.0 * math.pi)
SMOOTH = 1.0
HALF = 0.5 / SMOOTH
DENS_FLOOR = 0.5
STIFF = 0.02
VISCOUS = 0.1
GRAVITY = 1.0
TINY = 1e-30
SOFT = 0.01 * HALF * HALF
PRESS_SCALE = 5.0 * KERNEL_NORM / (SMOOTH * SMOOTH) / HALF
VISC_SCALE = -VISCOUS * 5.0 * KERNEL_NORM / (SMOOTH * SMOOTH)

VMEM = pl.BlockSpec(memory_space=pltpu.VMEM)
SMEM = pl.BlockSpec(memory_space=pltpu.SMEM)
MESH = pl.DeviceIdType.MESH
LIMIT = 56 * 1024 * 1024


def migrate_kernel(
    slabs, members, lists, counts, wanted, leave, stay,
    res_out, nb_out, asked_out,
    packed, res, nb, request, asked, names, chosen,
    row_send, row_recv, ghost_send, ghost_recv, name_send, name_recv, near_send, near_recv, local_sem,
):
    slab = lax.axis_index("slab")
    grp = lax.axis_index("grp")
    ghosts = members * NEED
    barrier = pltpu.get_barrier_semaphore()

    def greet_slab(r, carry):
        pl.semaphore_signal(barrier, inc=1, device_id={"slab": (slab + r) % slabs}, device_id_type=MESH)
        return carry

    def greet_grp(r, carry):
        pl.semaphore_signal(barrier, inc=1, device_id={"grp": (grp + r) % members}, device_id_type=MESH)
        return carry

    lax.fori_loop(1, members, greet_grp, 0)
    lax.fori_loop(1, slabs, greet_slab, 0)

    row = lax.broadcasted_iota(jnp.int32, (8, BLK), 0)
    lane = lax.broadcasted_iota(jnp.int32, (8, BLK), 1)
    ask = jnp.zeros((8, BLK), jnp.int32)
    for p in range(members):
        for k in range(NEED):
            ask = jnp.where((row == p) & (lane == k), wanted[0, k, p], ask)
    request[...] = ask
    for b in range(NSTAY):
        res[b, 0:7, :] = stay[b]
        res[b, 7:8, :] = jnp.ones((1, BLK), jnp.float32)
    for t in range(slabs):
        count = counts[0, t]
        for k in range(SM):
            keep = jnp.broadcast_to(jnp.minimum(jnp.maximum(count - k, 0), 1), (1, BLK)).astype(jnp.float32)
            packed[t * SM + k, 0:7, :] = leave[lists[0, k, t]] * keep
            packed[t * SM + k, 7:8, :] = keep
    pl.semaphore_wait(barrier, slabs - 1 + members - 1)

    def name_copy(r):
        return pltpu.make_async_remote_copy(
            src_ref=request, dst_ref=asked.at[grp], send_sem=name_send.at[r], recv_sem=name_recv.at[r],
            device_id={"grp": (grp + r) % members}, device_id_type=MESH,
        )

    def row_copy(r):
        target = (slab + r) % slabs
        return pltpu.make_async_remote_copy(
            src_ref=packed.at[pl.ds(target * SM, SM)], dst_ref=res.at[pl.ds(NSTAY + slab * SM, SM)],
            send_sem=row_send.at[r], recv_sem=row_recv.at[r],
            device_id={"slab": target}, device_id_type=MESH,
        )

    def ghost_copy(side):
        first = NSTAY - GH if side == 0 else 0
        target = (slab + (1 if side == 0 else slabs - 1)) % slabs
        return pltpu.make_async_remote_copy(
            src_ref=res.at[pl.ds(first, GH)], dst_ref=nb.at[pl.ds(ghosts + side * GH, GH)],
            send_sem=ghost_send.at[side], recv_sem=ghost_recv.at[side],
            device_id={"slab": target}, device_id_type=MESH,
        )

    def near_copy(r):
        target = (grp + r) % members
        return pltpu.make_async_remote_copy(
            src_ref=chosen.at[target], dst_ref=nb.at[pl.ds(grp * NEED, NEED)],
            send_sem=near_send.at[r], recv_sem=near_recv.at[r],
            device_id={"grp": target}, device_id_type=MESH,
        )

    def each(first, last, step):
        def body(r, carry):
            step(r)
            return carry

        lax.fori_loop(first, last, body, 0)

    each(1, members, lambda r: name_copy(r).start())
    each(1, slabs, lambda r: row_copy(r).start())
    ghost_copy(0).start()
    ghost_copy(1).start()
    asked[grp] = request[...]
    mine = pl.ds(NSTAY + slab * SM, SM)
    res[mine] = packed[pl.ds(slab * SM, SM)]
    each(1, members, lambda r: name_copy(r).wait_recv())
    local = pltpu.make_async_copy(asked, names, local_sem)
    local.start()
    local.wait()
    each(1, slabs, lambda r: row_copy(r).wait_recv())
    for d in range(members):
        for k in range(NEED):
            chosen[d, k] = res[names[d, grp, k]]
    each(1, members, lambda r: near_copy(r).start())
    nb[pl.ds(grp * NEED, NEED)] = chosen[grp]
    res_out[...] = res[...]
    asked_out[...] = asked[...]
    ghost_copy(0).wait_recv()
    ghost_copy(1).wait_recv()
    inside = (slab > 0).astype(jnp.float32)
    nb_out[pl.ds(ghosts, GH)] = nb[pl.ds(ghosts, GH)] * inside
    inside = (slab < slabs - 1).astype(jnp.float32)
    nb_out[pl.ds(ghosts + GH, GH)] = nb[pl.ds(ghosts + GH, GH)] * inside
    each(1, members, lambda r: near_copy(r).wait_recv())
    nb_out[pl.ds(0, ghosts)] = nb[pl.ds(0, ghosts)]
    each(1, members, lambda r: name_copy(r).wait_send())
    each(1, slabs, lambda r: row_copy(r).wait_send())
    each(1, members, lambda r: near_copy(r).wait_send())
    ghost_copy(0).wait_send()
    ghost_copy(1).wait_send()


def migrate_call(slabs, members, lists, counts, wanted, leave, stay):
    blocks = NSTAY + slabs * SM
    near = members * NEED + 2 * GH
    f32 = jnp.float32
    dma = pltpu.SemaphoreType.DMA
    return pl.pallas_call(
        functools.partial(migrate_kernel, slabs, members),
        out_shape=(
            jax.ShapeDtypeStruct((blocks, 8, BLK), f32),
            jax.ShapeDtypeStruct((near, 8, BLK), f32),
            jax.ShapeDtypeStruct((members, 8, BLK), jnp.int32),
        ),
        in_specs=[SMEM, SMEM, SMEM, VMEM, VMEM],
        out_specs=(VMEM, VMEM, VMEM),
        scratch_shapes=[
            pltpu.VMEM((slabs * SM, 8, BLK), f32),
            pltpu.VMEM((blocks, 8, BLK), f32),
            pltpu.VMEM((near, 8, BLK), f32),
            pltpu.VMEM((8, BLK), jnp.int32),
            pltpu.VMEM((members, 8, BLK), jnp.int32),
            pltpu.SMEM((members, 8, BLK), jnp.int32),
            pltpu.VMEM((members, NEED, 8, BLK), f32),
            dma((slabs,)), dma((slabs,)), dma((2,)), dma((2,)),
            dma((members,)), dma((members,)), dma((members,)), dma((members,)), dma,
        ],
        compiler_params=pltpu.CompilerParams(collective_id=0, has_side_effects=True, vmem_limit_bytes=LIMIT),
    )(lists, counts, wanted, leave, stay)


def field_kernel(
    slabs, members, names, field, out, tiles, edges, far, near_send, near_recv, edge_send, edge_recv
):
    slab = lax.axis_index("slab")
    grp = lax.axis_index("grp")
    above = (slab + 1) % slabs
    below = (slab + slabs - 1) % slabs
    barrier = pltpu.get_barrier_semaphore()
    for r in range(1, members):
        pl.semaphore_signal(barrier, inc=1, device_id={"grp": (grp + r) % members}, device_id_type=MESH)
    for target in (above, below):
        pl.semaphore_signal(barrier, inc=1, device_id={"slab": target}, device_id_type=MESH)
    for d in range(members):
        for k in range(NEED):
            tiles[d, 2 * k : 2 * k + 2, :] = field[names[d, grp, k]]
    for k in range(GH):
        edges[0, 2 * k : 2 * k + 2, :] = field[NSTAY - GH + k]
        edges[1, 2 * k : 2 * k + 2, :] = field[k]
    pl.semaphore_wait(barrier, members + 1)

    def near_copy(r):
        target = (grp + r) % members
        return pltpu.make_async_remote_copy(
            src_ref=tiles.at[target], dst_ref=far.at[grp], send_sem=near_send.at[r], recv_sem=near_recv.at[r],
            device_id={"grp": target}, device_id_type=MESH,
        )

    def edge_copy(side):
        return pltpu.make_async_remote_copy(
            src_ref=edges.at[side], dst_ref=far.at[members + side],
            send_sem=edge_send.at[side], recv_sem=edge_recv.at[side],
            device_id={"slab": above if side == 0 else below}, device_id_type=MESH,
        )

    copies = [near_copy(r) for r in range(1, members)] + [edge_copy(0), edge_copy(1)]
    for copy in copies:
        copy.start()
    far[grp] = tiles[grp]
    for copy in copies:
        copy.wait_recv()
    out[0:members] = far[0:members]
    out[members] = far[members] * (slab > 0).astype(jnp.float32)
    out[members + 1] = far[members + 1] * (slab < slabs - 1).astype(jnp.float32)
    for copy in copies:
        copy.wait_send()


def field_call(slabs, members, names, field):
    f32 = jnp.float32
    dma = pltpu.SemaphoreType.DMA
    out = pl.pallas_call(
        functools.partial(field_kernel, slabs, members),
        out_shape=jax.ShapeDtypeStruct((members + 2, 8, BLK), f32),
        in_specs=[SMEM, VMEM],
        out_specs=VMEM,
        scratch_shapes=[
            pltpu.VMEM((members, 8, BLK), f32),
            pltpu.VMEM((2, 8, BLK), f32),
            pltpu.VMEM((members + 2, 8, BLK), f32),
            dma((members,)), dma((members,)), dma((2,)), dma((2,)),
        ],
        compiler_params=pltpu.CompilerParams(collective_id=1, has_side_effects=True, vmem_limit_bytes=LIMIT),
    )(names, field)
    return out.reshape(-1, BLK)


def shell_of(radius2):
    ratio = radius2 * lax.rsqrt(jnp.maximum(radius2, TINY))
    return jnp.maximum(1.0 - ratio, 0.0)


def weight_of(shell):
    square = shell * shell
    return square * square * (1.25 - shell)


def write_lists(count, pairs, res, nb, out):
    left = pairs[0:1, :]
    right = pairs[1:2, :]
    lane = lax.broadcasted_iota(jnp.int32, (1, PAIR_MAX), 1)
    res_live = res[:, 7, :]
    nb_live = nb[:, 7, :]
    res_live = jnp.concatenate([res_live, res_live], 1)
    nb_live = jnp.concatenate([nb_live, nb_live], 1)
    hit = lax.broadcasted_iota(jnp.int32, (RES, PAIR_MAX), 0) == left
    live_left = jnp.sum(jnp.where(hit, res_live, 0.0), 0, keepdims=True)
    hit = lax.broadcasted_iota(jnp.int32, (NJ, PAIR_MAX), 0) == right
    live_right = jnp.sum(jnp.where(hit, nb_live, 0.0), 0, keepdims=True)
    valid = jnp.where(lane < count, live_right, 0.0)
    heavy = valid * live_left
    light = valid * (1.0 - live_left)
    before = lax.broadcasted_iota(jnp.int32, (PAIR_MAX, PAIR_MAX), 0) < lax.broadcasted_iota(
        jnp.int32, (PAIR_MAX, PAIR_MAX), 1
    )
    blank = jnp.zeros((6, PAIR_MAX), jnp.float32)
    kinds = jnp.concatenate([heavy, light, blank], 0).astype(jnp.bfloat16)
    spots = jnp.dot(kinds, jnp.where(before, 1.0, 0.0).astype(jnp.bfloat16), preferred_element_type=jnp.float32)
    names = jnp.concatenate([left.astype(jnp.float32), right.astype(jnp.float32), blank], 0).astype(jnp.bfloat16)
    row = lax.broadcasted_iota(jnp.int32, (PAIR_MAX, PAIR_MAX), 0).astype(jnp.float32)
    sums = jnp.sum(jnp.concatenate([heavy, light, blank], 0), 1, keepdims=True)
    for kind, member in ((0, heavy), (1, light)):
        target = jnp.where(member > 0.5, spots[kind : kind + 1, :], -1.0)
        chosen = jnp.where(row == target, 1.0, 0.0).astype(jnp.bfloat16)
        packed = lax.dot_general(names, chosen, (((1,), (1,)), ((), ())), preferred_element_type=jnp.float32)
        amount = jnp.broadcast_to(sums[kind : kind + 1, :], (1, PAIR_MAX))
        filled = lane.astype(jnp.float32) < amount
        out[2 * kind : 2 * kind + 1, :] = jnp.where(filled, packed[0:1, :], float(RES)).astype(jnp.int32)
        out[2 * kind + 1 : 2 * kind + 2, :] = packed[1:2, :].astype(jnp.int32)
        out[4 + kind : 5 + kind, :] = amount.astype(jnp.int32)
    out[6:8, :] = jnp.zeros((2, PAIR_MAX), jnp.int32)


def pieces(value):
    high = value.astype(jnp.bfloat16)
    rest = value - high.astype(jnp.float32)
    mid = rest.astype(jnp.bfloat16)
    low = (rest - mid.astype(jnp.float32)).astype(jnp.bfloat16)
    return high, mid, low


def write_columns(nb, table, fields):
    count = len(fields)
    row = lax.broadcasted_iota(jnp.int32, (32, count * BLK), 0)
    spot = lax.broadcasted_iota(jnp.int32, (32, count * BLK), 1) // BLK
    spread = jnp.zeros((32, count * BLK), jnp.float32)
    for n, (field, scale) in enumerate(fields):
        mine = (row == field) | (row == 8 + field) | (row == 16 + field)
        spread = jnp.where((spot == n) & mine, scale, spread)
    spread = spread.astype(jnp.bfloat16)

    def some(step, carry):
        for u in range(COLUMN_STEP):
            j = step * COLUMN_STEP + u
            high, mid, low = (p.astype(jnp.float32) for p in pieces(nb[j]))
            stacked = jnp.concatenate([high, mid, low, jnp.zeros((8, BLK), jnp.float32)], 0)
            turned = jnp.transpose(stacked, (1, 0)).astype(jnp.bfloat16)
            wide = jnp.dot(turned, spread, preferred_element_type=jnp.float32)
            for n in range(count):
                table[j, n] = wide[:, n * BLK : (n + 1) * BLK]
        return carry

    lax.fori_loop(0, NJ // COLUMN_STEP, some, 0)


def density_kernel(count, pairs, res, nb, dens_out, field_out, list_out, table, acc, origin, lists, sem):
    write_lists(count[0], pairs, res, nb, list_out)
    copy = pltpu.make_async_copy(list_out, lists, sem)
    copy.start()
    write_columns(nb, table, ((0, HALF), (1, HALF), (2, HALF), (6, 4.0)))
    x, y, z = (nb[:, f, :] * HALF for f in range(3))
    alone = jnp.sum(weight_of(shell_of(x * x + y * y + z * z)) * (4.0 * nb[:, 6, :]), 1, keepdims=True)
    origin[...] = jnp.zeros_like(origin)
    origin[:, 0, :] = jnp.broadcast_to(alone, (NJ, BLK))
    acc[...] = jnp.zeros_like(acc)
    copy.wait()

    def whole(step, carry):
        for u in range(STEP):
            i = lists[0, STEP * step + u]
            j = lists[1, STEP * step + u]
            ax, ay, az = (res[jnp.minimum(i, RES - 1), f : f + 1, :] * HALF for f in range(3))
            ax, ay, az = (jnp.broadcast_to(a, (8, BLK)) for a in (ax, ay, az))
            totals = [jnp.zeros((8, BLK), jnp.float32)] * 2
            for g in range(GROUPS):
                rows = pl.ds(8 * g, 8)
                dx = ax - table[j, 0, rows, :]
                dy = ay - table[j, 1, rows, :]
                dz = az - table[j, 2, rows, :]
                shell = shell_of(dx * dx + dy * dy + dz * dz)
                totals[g % 2] = totals[g % 2] + weight_of(shell) * table[j, 3, rows, :]
            acc[i] = acc[i] + (totals[0] + totals[1])
        return carry

    lax.fori_loop(0, (lists[4, 0] + STEP - 1) // STEP, whole, 0)

    def blank(n, carry):
        i = lists[2, n]
        acc[i] = acc[i] + origin[lists[3, n]]
        return carry

    lax.fori_loop(0, lists[5, 0], blank, 0)
    dens = jnp.sum(acc[0:RES], 1) * KERNEL_NORM
    dens_out[...] = dens
    inverse = 1.0 / jnp.maximum(dens, DENS_FLOOR)
    cube = dens * dens * dens
    field_out[:, 0, :] = STIFF * (cube * cube * dens - 1.0) * inverse * inverse
    field_out[:, 1, :] = res[:, 6, :] * inverse


def two_pieces(value):
    high = value.astype(jnp.bfloat16)
    return high, (value - high.astype(jnp.float32)).astype(jnp.bfloat16)


def write_factors(nb, far, press, damp, centre):
    row = lax.broadcasted_iota(jnp.int32, (8, BLK), 0)
    upper = row < 3
    lower = (row >= 3) & (row < 6)

    def store(ref, j, values):
        for p, some in enumerate(zip(*[pieces(v) for v in values])):
            for h in range(0, len(values), 2):
                pair = jnp.concatenate([some[h].astype(jnp.float32), some[h + 1].astype(jnp.float32)], 0)
                pair = pair.astype(jnp.bfloat16)
                rows = pl.ds(8 * (len(values) * p + h), 16)
                ref[j, rows, 0:BLK] = pair
                ref[j, rows, BLK : 2 * BLK] = pair

    def some(step, carry):
        for u in range(FACTOR_STEP):
            j = step * FACTOR_STEP + u
            tile = nb[j]
            mass = jnp.broadcast_to(tile[6:7, :], (8, BLK))
            scaled = tile * HALF
            middle = jnp.where(upper, jnp.broadcast_to(scaled[:, 0:1], (8, BLK)), 0.0)
            centre[j] = middle
            place = scaled - middle
            mass_q = mass * jnp.broadcast_to(far[pl.ds(2 * j, 1), :], (8, BLK))
            mass_s = jnp.where(lower, mass * jnp.broadcast_to(far[pl.ds(2 * j + 1, 1), :], (8, BLK)), 0.0)
            mass = jnp.where(upper, mass, 0.0)
            mass_q = jnp.where(upper, mass_q, 0.0)
            store(press, j, (mass, mass * place, mass_q, mass_q * place))
            store(damp, j, (mass_s, mass_s * tile))
        return carry

    lax.fori_loop(0, NJ // FACTOR_STEP, some, 0)


def force_kernel(
    lists, res, nb, field, far, flag, out, table, acc, origin, press, damp, centre, cubes, damps
):
    write_columns(nb, table, ((0, HALF), (1, HALF), (2, HALF)))
    write_factors(nb, far, press, damp, centre)
    acc[...] = jnp.zeros_like(acc)
    row = lax.broadcasted_iota(jnp.int32, (8, BLK), 0)
    upper = row < 3
    lower = (row >= 3) & (row < 6)
    scale = jnp.where(upper, HALF, 1.0)

    x, y, z = (nb[:, f, :] * HALF for f in range(3))
    radius2 = x * x + y * y + z * z
    shell = shell_of(radius2)
    cube = shell * shell * shell * nb[:, 6, :]
    drag = cube * radius2 / (radius2 + SOFT) * far[pl.ds(1, NJ, stride=2), :]
    push = cube * far[pl.ds(0, NJ, stride=2), :]
    origin[...] = jnp.zeros_like(origin)
    for f, place in enumerate((x, y, z)):
        origin[:, f, :] = jnp.broadcast_to(jnp.sum(cube * place, 1, keepdims=True), (NJ, BLK))
        origin[:, 8 + f, :] = jnp.broadcast_to(jnp.sum(push * place, 1, keepdims=True), (NJ, BLK))
        origin[:, 3 + f, :] = jnp.broadcast_to(jnp.sum(drag * nb[:, 3 + f, :], 1, keepdims=True), (NJ, BLK))

    def coefficients(i):
        q = jnp.broadcast_to(field[i, 0:1, :], (8, BLK))
        s = jnp.broadcast_to(field[i, 1:2, :], (8, BLK))
        return jnp.where(upper, q, jnp.where(lower, s, 0.0))

    def geometry(u, i, j):
        held = jnp.minimum(i, RES - 1)
        ax, ay, az = (res[held, f : f + 1, :] * HALF for f in range(3))
        ax, ay, az = (jnp.broadcast_to(a, (16, BLK)) for a in (ax, ay, az))
        for g in range(GROUPS // 2):
            rows = pl.ds(16 * g, 16)
            dx = ax - table[j, 0, rows, :]
            dy = ay - table[j, 1, rows, :]
            dz = az - table[j, 2, rows, :]
            radius2 = dx * dx + dy * dy + dz * dz
            shell = shell_of(radius2)
            cube = shell * shell * shell
            soft = lax.rsqrt(radius2 + SOFT)
            high, low = two_pieces(cube)
            cubes[u, rows, :] = high
            cubes[u, pl.ds(BLK + 16 * g, 16), :] = low
            high, low = two_pieces(cube * (radius2 * (soft * soft)))
            damps[u, rows, :] = high
            damps[u, pl.ds(BLK + 16 * g, 16), :] = low

    def sums_of(u, j):
        first = jnp.dot(press[j], cubes[u], preferred_element_type=jnp.float32)
        second = jnp.dot(damp[j], damps[u], preferred_element_type=jnp.float32)
        return first[0:32] + (first[32:64] + first[64:96]), second[0:16] + (second[16:32] + second[32:48])

    def whole(step, before):
        sums = [sums_of(u, j) for u, (i, j) in enumerate(before)]
        after = []
        for u in range(STEP):
            n = jnp.minimum(STEP * step + u, PAIR_MAX - 1)
            i = lists[0, n]
            j = lists[1, n]
            geometry(u, i, j)
            after.append((i, j))
        for u, (i, j) in enumerate(before):
            held = jnp.minimum(i, RES - 1)
            first, second = sums[u]
            place = res[held] * scale - centre[j]
            both = place * (first[0:8] + second[0:8]) - (first[8:16] + second[8:16])
            acc[i] = acc[i] + (coefficients(held) * both + (place * first[16:24] - first[24:32]))
        return tuple(after)

    cubes[...] = jnp.zeros_like(cubes)
    damps[...] = jnp.zeros_like(damps)
    nowhere = tuple((jnp.int32(RES), jnp.int32(0)) for _ in range(STEP))
    lax.fori_loop(0, (lists[4, 0] + STEP - 1) // STEP + 1, whole, nowhere)

    def blank(n, carry):
        i = lists[2, n]
        j = lists[3, n]
        acc[i] = acc[i] - (coefficients(i) * origin[j, 0:8, :] + origin[j, 8:16, :])
        return carry

    lax.fori_loop(0, lists[5, 0], blank, 0)
    gravity = jnp.where(lax.broadcasted_iota(jnp.int32, (3, BLK), 0) == 2, -GRAVITY, 0.0)
    for b in range(RES):
        total = acc[b, 0:3, :] * PRESS_SCALE + acc[b, 3:6, :] * VISC_SCALE + gravity
        if b < NSTAY:
            total = total * (1.0 - flag[b : b + 1, :].astype(jnp.float32))
        out[:, b * BLK : (b + 1) * BLK] = total


def density_call(count, pairs, resident, neighbour):
    return pl.pallas_call(
        density_kernel,
        out_shape=(
            jax.ShapeDtypeStruct((RES, BLK), jnp.float32),
            jax.ShapeDtypeStruct((RES, 2, BLK), jnp.float32),
            jax.ShapeDtypeStruct((8, PAIR_MAX), jnp.int32),
        ),
        in_specs=[SMEM, VMEM, VMEM, VMEM],
        out_specs=(VMEM, VMEM, VMEM),
        scratch_shapes=[
            pltpu.VMEM((NJ, 4, BLK, BLK), jnp.float32),
            pltpu.VMEM((RES + 1, 8, BLK), jnp.float32),
            pltpu.VMEM((NJ, 8, BLK), jnp.float32),
            pltpu.SMEM((8, PAIR_MAX), jnp.int32),
            pltpu.SemaphoreType.DMA,
        ],
        compiler_params=pltpu.CompilerParams(vmem_limit_bytes=LIMIT),
    )(count, pairs, resident, neighbour)


def force_call(lists, resident, neighbour, field, far, flag):
    return pl.pallas_call(
        force_kernel,
        out_shape=jax.ShapeDtypeStruct((3, RES * BLK), jnp.float32),
        in_specs=[SMEM, VMEM, VMEM, VMEM, VMEM, VMEM],
        out_specs=VMEM,
        scratch_shapes=[
            pltpu.VMEM((NJ, 3, BLK, BLK), jnp.float32),
            pltpu.VMEM((RES + 1, 8, BLK), jnp.float32),
            pltpu.VMEM((NJ, 16, BLK), jnp.float32),
            pltpu.VMEM((NJ, 96, 2 * BLK), jnp.bfloat16),
            pltpu.VMEM((NJ, 48, 2 * BLK), jnp.bfloat16),
            pltpu.VMEM((NJ, 8, BLK), jnp.float32),
            pltpu.VMEM((STEP, 2 * BLK, BLK), jnp.bfloat16),
            pltpu.VMEM((STEP, 2 * BLK, BLK), jnp.bfloat16),
        ],
        compiler_params=pltpu.CompilerParams(vmem_limit_bytes=LIMIT),
    )(lists, resident, neighbour, field, far, flag)


def on_device(stay, leave, stay_flag, send_list, send_count, wanted, pair_tiles, pair_count):
    slabs = send_list.shape[1]
    members = wanted.shape[1]
    leaving = leave.reshape(7, slabs * SM, BLK).transpose(1, 0, 2)
    staying = stay.reshape(7, NSTAY, BLK).transpose(1, 0, 2)
    resident, neighbour, asked = migrate_call(
        slabs, members, send_list.transpose(0, 2, 1), send_count, wanted.transpose(0, 2, 1), leaving, staying
    )
    dens, field, lists = density_call(pair_count, pair_tiles[0], resident, neighbour)
    far = field_call(slabs, members, asked, field)
    accel = force_call(lists, resident, neighbour, field, far, stay_flag.reshape(NSTAY, BLK))
    return (dens.reshape(-1), accel)


def solution(mesh):
    in_specs = (
        P(None, ("slab", "grp")),
        P(None, ("slab", "grp")),
        P(("slab", "grp")),
        P(("slab", "grp"), None, None),
        P(("slab", "grp"), None),
        P(("slab", "grp"), None, None),
        P(("slab", "grp"), None, None),
        P(("slab", "grp")),
    )
    out_specs = (P(("slab", "grp")), P(None, ("slab", "grp")))
    return jax.shard_map(
        on_device, mesh=mesh, in_specs=in_specs, out_specs=out_specs, check_vma=False
    )
```

```python
import functools
import math

import jax
import jax.numpy as jnp
from jax import lax
from jax.experimental import pallas as pl
from jax.experimental.pallas import tpu as pltpu
from jax.sharding import PartitionSpec as P

BLK = 128
SM = 2
GH = 4
NEED = 4
PAIR_MAX = 256
NSTAY = 16
RES = 80
NJ = 40
GROUPS = BLK // 8
COLUMN_STEP = 8
STEP = 4
WIDE = 8
FACTOR_STEP = 4

KERNEL_NORM = 21.0 / (16.0 * math.pi)
SMOOTH = 1.0
HALF = 0.5 / SMOOTH
DENS_FLOOR = 0.5
STIFF = 0.02
VISCOUS = 0.1
GRAVITY = 1.0
TINY = 1e-30
SOFT = 0.01 * HALF * HALF
PRESS_SCALE = 5.0 * KERNEL_NORM / (SMOOTH * SMOOTH) / HALF
VISC_SCALE = -VISCOUS * 5.0 * KERNEL_NORM / (SMOOTH * SMOOTH)

VMEM = pl.BlockSpec(memory_space=pltpu.VMEM)
SMEM = pl.BlockSpec(memory_space=pltpu.SMEM)
ANY = pl.BlockSpec(memory_space=pl.ANY)
MESH = pl.DeviceIdType.MESH
LIMIT = 56 * 1024 * 1024


def migrate_kernel(
    slabs, members, lists, counts, wanted, leave, stay,
    res_out, nb_out, asked_out,
    leaving, staying, packed, res, nb, request, asked, names, chosen,
    row_send, row_recv, ghost_send, ghost_recv, name_send, name_recv, near_send, near_recv, local_sem,
):
    slab = lax.axis_index("slab")
    grp = lax.axis_index("grp")
    ghosts = members * NEED
    barrier = pltpu.get_barrier_semaphore()

    def greet_slab(r, carry):
        pl.semaphore_signal(barrier, inc=1, device_id={"slab": (slab + r) % slabs}, device_id_type=MESH)
        return carry

    def greet_grp(r, carry):
        pl.semaphore_signal(barrier, inc=1, device_id={"grp": (grp + r) % members}, device_id_type=MESH)
        return carry

    fetch_leave = pltpu.make_async_copy(leave, leaving, local_sem.at[0])
    fetch_stay = pltpu.make_async_copy(stay, staying, local_sem.at[1])
    fetch_leave.start()
    fetch_stay.start()
    lax.fori_loop(1, members, greet_grp, 0)
    lax.fori_loop(1, slabs, greet_slab, 0)

    lane = lax.broadcasted_iota(jnp.int32, (1, BLK), 1)
    for p in range(members):
        ask = jnp.zeros((1, BLK), jnp.int32)
        for k in range(NEED):
            ask = jnp.where(lane == k, wanted[0, k, p], ask)
        request[p] = ask
    fetch_stay.wait()
    for b in range(NSTAY):
        res[b, 0:7, :] = staying[b]
        res[b, 7:8, :] = jnp.ones((1, BLK), jnp.float32)
    fetch_leave.wait()
    for t in range(slabs):
        count = counts[0, t]
        for k in range(SM):
            keep = jnp.broadcast_to(jnp.minimum(jnp.maximum(count - k, 0), 1), (1, BLK)).astype(jnp.float32)
            packed[t * SM + k, 0:7, :] = leaving[lists[0, k, t]] * keep
            packed[t * SM + k, 7:8, :] = keep
    pl.semaphore_wait(barrier, slabs - 1 + members - 1)

    def name_copy(r):
        target = (grp + r) % members
        return pltpu.make_async_remote_copy(
            src_ref=request.at[target], dst_ref=asked.at[grp], send_sem=name_send.at[r], recv_sem=name_recv.at[r],
            device_id={"grp": target}, device_id_type=MESH,
        )

    def row_copy(r):
        target = (slab + r) % slabs
        return pltpu.make_async_remote_copy(
            src_ref=packed.at[pl.ds(target * SM, SM)], dst_ref=res.at[pl.ds(NSTAY + slab * SM, SM)],
            send_sem=row_send.at[r], recv_sem=row_recv.at[r],
            device_id={"slab": target}, device_id_type=MESH,
        )

    def ghost_copy(side):
        first = NSTAY - GH if side == 0 else 0
        target = (slab + (1 if side == 0 else slabs - 1)) % slabs
        return pltpu.make_async_remote_copy(
            src_ref=res.at[pl.ds(first, GH)], dst_ref=nb.at[pl.ds(ghosts + side * GH, GH)],
            send_sem=ghost_send.at[side], recv_sem=ghost_recv.at[side],
            device_id={"slab": target}, device_id_type=MESH,
        )

    def near_copy(r):
        target = (grp + r) % members
        return pltpu.make_async_remote_copy(
            src_ref=chosen.at[target], dst_ref=nb.at[pl.ds(grp * NEED, NEED)],
            send_sem=near_send.at[r], recv_sem=near_recv.at[r],
            device_id={"grp": target}, device_id_type=MESH,
        )

    def each(first, last, step):
        def body(r, carry):
            step(r)
            return carry

        lax.fori_loop(first, last, body, 0)

    each(1, members, lambda r: name_copy(r).start())
    each(1, slabs, lambda r: row_copy(r).start())
    ghost_copy(0).start()
    ghost_copy(1).start()
    asked[grp] = request[grp]
    mine = pl.ds(NSTAY + slab * SM, SM)
    res[mine] = packed[pl.ds(slab * SM, SM)]
    each(1, members, lambda r: name_copy(r).wait_recv())
    local = pltpu.make_async_copy(asked, names, local_sem.at[2])
    local.start()
    local.wait()
    asked_out[...] = asked[...]
    each(1, slabs, lambda r: row_copy(r).wait_recv())
    for d in range(members):
        for k in range(NEED):
            chosen[d, k] = res[names[d, 0, k]]
    each(1, members, lambda r: near_copy(r).start())
    nb[pl.ds(grp * NEED, NEED)] = chosen[grp]
    store_res = pltpu.make_async_copy(res, res_out, local_sem.at[3])
    store_res.start()
    ghost_copy(0).wait_recv()
    ghost_copy(1).wait_recv()
    for side, some in ((0, slab > 0), (1, slab < slabs - 1)):
        rows = pl.ds(ghosts + side * GH, GH)
        nb[rows] = nb[rows] * some.astype(jnp.float32)
    each(1, members, lambda r: near_copy(r).wait_recv())
    store_nb = pltpu.make_async_copy(nb, nb_out, local_sem.at[4])
    store_nb.start()
    each(1, members, lambda r: name_copy(r).wait_send())
    each(1, slabs, lambda r: row_copy(r).wait_send())
    each(1, members, lambda r: near_copy(r).wait_send())
    ghost_copy(0).wait_send()
    ghost_copy(1).wait_send()
    store_res.wait()
    store_nb.wait()


def migrate_call(slabs, members, lists, counts, wanted, leave, stay):
    blocks = NSTAY + slabs * SM
    near = members * NEED + 2 * GH
    f32 = jnp.float32
    dma = pltpu.SemaphoreType.DMA
    return pl.pallas_call(
        functools.partial(migrate_kernel, slabs, members),
        out_shape=(
            jax.ShapeDtypeStruct((blocks, 8, BLK), f32),
            jax.ShapeDtypeStruct((near, 8, BLK), f32),
            jax.ShapeDtypeStruct((members, 1, BLK), jnp.int32),
        ),
        in_specs=[SMEM, SMEM, SMEM, ANY, ANY],
        out_specs=(ANY, ANY, VMEM),
        scratch_shapes=[
            pltpu.VMEM(leave.shape, f32),
            pltpu.VMEM(stay.shape, f32),
            pltpu.VMEM((slabs * SM, 8, BLK), f32),
            pltpu.VMEM((blocks, 8, BLK), f32),
            pltpu.VMEM((near, 8, BLK), f32),
            pltpu.VMEM((members, 1, BLK), jnp.int32),
            pltpu.VMEM((members, 1, BLK), jnp.int32),
            pltpu.SMEM((members, 1, BLK), jnp.int32),
            pltpu.VMEM((members, NEED, 8, BLK), f32),
            dma((slabs,)), dma((slabs,)), dma((2,)), dma((2,)),
            dma((members,)), dma((members,)), dma((members,)), dma((members,)), dma((5,)),
        ],
        compiler_params=pltpu.CompilerParams(collective_id=0, has_side_effects=True, vmem_limit_bytes=LIMIT),
    )(lists, counts, wanted, leave, stay)


def field_kernel(
    slabs, members, names, field, out, tiles, edges, far, near_send, near_recv, edge_send, edge_recv
):
    slab = lax.axis_index("slab")
    grp = lax.axis_index("grp")
    above = (slab + 1) % slabs
    below = (slab + slabs - 1) % slabs
    barrier = pltpu.get_barrier_semaphore()
    for r in range(1, members):
        pl.semaphore_signal(barrier, inc=1, device_id={"grp": (grp + r) % members}, device_id_type=MESH)
    for target in (above, below):
        pl.semaphore_signal(barrier, inc=1, device_id={"slab": target}, device_id_type=MESH)
    for d in range(members):
        for k in range(NEED):
            tiles[d, 2 * k : 2 * k + 2, :] = field[names[d, 0, k]]
    for k in range(GH):
        edges[0, 2 * k : 2 * k + 2, :] = field[NSTAY - GH + k]
        edges[1, 2 * k : 2 * k + 2, :] = field[k]
    pl.semaphore_wait(barrier, members + 1)

    def near_copy(r):
        target = (grp + r) % members
        return pltpu.make_async_remote_copy(
            src_ref=tiles.at[target], dst_ref=far.at[grp], send_sem=near_send.at[r], recv_sem=near_recv.at[r],
            device_id={"grp": target}, device_id_type=MESH,
        )

    def edge_copy(side):
        return pltpu.make_async_remote_copy(
            src_ref=edges.at[side], dst_ref=far.at[members + side],
            send_sem=edge_send.at[side], recv_sem=edge_recv.at[side],
            device_id={"slab": above if side == 0 else below}, device_id_type=MESH,
        )

    copies = [near_copy(r) for r in range(1, members)] + [edge_copy(0), edge_copy(1)]
    for copy in copies:
        copy.start()
    far[grp] = tiles[grp]
    for copy in copies:
        copy.wait_recv()
    out[0:members] = far[0:members]
    out[members] = far[members] * (slab > 0).astype(jnp.float32)
    out[members + 1] = far[members + 1] * (slab < slabs - 1).astype(jnp.float32)
    for copy in copies:
        copy.wait_send()


def field_call(slabs, members, names, field):
    f32 = jnp.float32
    dma = pltpu.SemaphoreType.DMA
    out = pl.pallas_call(
        functools.partial(field_kernel, slabs, members),
        out_shape=jax.ShapeDtypeStruct((members + 2, 8, BLK), f32),
        in_specs=[SMEM, VMEM],
        out_specs=VMEM,
        scratch_shapes=[
            pltpu.VMEM((members, 8, BLK), f32),
            pltpu.VMEM((2, 8, BLK), f32),
            pltpu.VMEM((members + 2, 8, BLK), f32),
            dma((members,)), dma((members,)), dma((2,)), dma((2,)),
        ],
        compiler_params=pltpu.CompilerParams(collective_id=1, has_side_effects=True, vmem_limit_bytes=LIMIT),
    )(names, field)
    return out.reshape(-1, BLK)


def shell_of(radius2):
    ratio = radius2 * lax.rsqrt(jnp.maximum(radius2, TINY))
    return jnp.maximum(1.0 - ratio, 0.0)


def weight_of(shell):
    square = shell * shell
    return square * square * (1.25 - shell)


def write_lists(count, pairs, res, nb, out):
    left = pairs[0:1, :]
    right = pairs[1:2, :]
    lane = lax.broadcasted_iota(jnp.int32, (1, PAIR_MAX), 1)
    res_live = res[:, 7, :]
    nb_live = nb[:, 7, :]
    res_live = jnp.concatenate([res_live, res_live], 1)
    nb_live = jnp.concatenate([nb_live, nb_live], 1)
    hit = lax.broadcasted_iota(jnp.int32, (RES, PAIR_MAX), 0) == left
    live_left = jnp.sum(jnp.where(hit, res_live, 0.0), 0, keepdims=True)
    hit = lax.broadcasted_iota(jnp.int32, (NJ, PAIR_MAX), 0) == right
    live_right = jnp.sum(jnp.where(hit, nb_live, 0.0), 0, keepdims=True)
    valid = jnp.where(lane < count, live_right, 0.0)
    heavy = valid * live_left
    light = valid * (1.0 - live_left)
    before = lax.broadcasted_iota(jnp.int32, (PAIR_MAX, PAIR_MAX), 0) < lax.broadcasted_iota(
        jnp.int32, (PAIR_MAX, PAIR_MAX), 1
    )
    blank = jnp.zeros((6, PAIR_MAX), jnp.float32)
    kinds = jnp.concatenate([heavy, light, blank], 0).astype(jnp.bfloat16)
    spots = jnp.dot(kinds, jnp.where(before, 1.0, 0.0).astype(jnp.bfloat16), preferred_element_type=jnp.float32)
    names = jnp.concatenate([left.astype(jnp.float32), right.astype(jnp.float32), blank], 0).astype(jnp.bfloat16)
    row = lax.broadcasted_iota(jnp.int32, (PAIR_MAX, PAIR_MAX), 0).astype(jnp.float32)
    sums = jnp.sum(jnp.concatenate([heavy, light, blank], 0), 1, keepdims=True)
    for kind, member in ((0, heavy), (1, light)):
        target = jnp.where(member > 0.5, spots[kind : kind + 1, :], -1.0)
        chosen = jnp.where(row == target, 1.0, 0.0).astype(jnp.bfloat16)
        packed = lax.dot_general(names, chosen, (((1,), (1,)), ((), ())), preferred_element_type=jnp.float32)
        amount = jnp.broadcast_to(sums[kind : kind + 1, :], (1, PAIR_MAX))
        filled = lane.astype(jnp.float32) < amount
        out[2 * kind : 2 * kind + 1, :] = jnp.where(filled, packed[0:1, :], float(RES)).astype(jnp.int32)
        out[2 * kind + 1 : 2 * kind + 2, :] = packed[1:2, :].astype(jnp.int32)
        out[4 + kind : 5 + kind, :] = amount.astype(jnp.int32)
    out[6:8, :] = jnp.zeros((2, PAIR_MAX), jnp.int32)


def pieces(value):
    high = value.astype(jnp.bfloat16)
    rest = value - high.astype(jnp.float32)
    mid = rest.astype(jnp.bfloat16)
    low = (rest - mid.astype(jnp.float32)).astype(jnp.bfloat16)
    return high, mid, low


def write_columns(nb, table, fields):
    count = len(fields)
    row = lax.broadcasted_iota(jnp.int32, (32, count * BLK), 0)
    spot = lax.broadcasted_iota(jnp.int32, (32, count * BLK), 1) // BLK
    spread = jnp.zeros((32, count * BLK), jnp.float32)
    for n, (field, scale) in enumerate(fields):
        mine = (row == field) | (row == 8 + field) | (row == 16 + field)
        spread = jnp.where((spot == n) & mine, scale, spread)
    spread = spread.astype(jnp.bfloat16)

    def some(step, carry):
        for u in range(COLUMN_STEP):
            j = step * COLUMN_STEP + u
            high, mid, low = (p.astype(jnp.float32) for p in pieces(nb[j]))
            stacked = jnp.concatenate([high, mid, low, jnp.zeros((8, BLK), jnp.float32)], 0)
            turned = jnp.transpose(stacked, (1, 0)).astype(jnp.bfloat16)
            wide = jnp.dot(turned, spread, preferred_element_type=jnp.float32)
            for n in range(count):
                table[j, n] = wide[:, n * BLK : (n + 1) * BLK]
        return carry

    lax.fori_loop(0, NJ // COLUMN_STEP, some, 0)


def density_kernel(count, pairs, res, nb, dens_out, field_out, list_out, shell_out, table, acc, origin, held, lists, sem, held_sem):
    write_lists(count[0], pairs, res, nb, list_out)
    copy = pltpu.make_async_copy(list_out, lists, sem)
    copy.start()
    write_columns(nb, table, ((0, HALF), (1, HALF), (2, HALF), (6, 4.0)))
    x, y, z = (nb[:, f, :] * HALF for f in range(3))
    alone = jnp.sum(weight_of(shell_of(x * x + y * y + z * z)) * (4.0 * nb[:, 6, :]), 1, keepdims=True)
    origin[...] = jnp.zeros_like(origin)
    origin[:, 0, :] = jnp.broadcast_to(alone, (NJ, BLK))
    acc[...] = jnp.zeros_like(acc)
    copy.wait()
    steps = (lists[4, 0] + STEP - 1) // STEP

    def shell_copy(step):
        rows = pl.ds(STEP * step, STEP)
        return pltpu.make_async_copy(held.at[rows], shell_out.at[rows], held_sem.at[step])

    def whole(step, carry):
        for u in range(STEP):
            i = lists[0, STEP * step + u]
            j = lists[1, STEP * step + u]
            ax, ay, az = (res[jnp.minimum(i, RES - 1), f : f + 1, :] * HALF for f in range(3))
            ax, ay, az = (jnp.broadcast_to(a, (8, BLK)) for a in (ax, ay, az))
            totals = [jnp.zeros((8, BLK), jnp.float32)] * 2
            for g in range(GROUPS):
                rows = pl.ds(8 * g, 8)
                dx = ax - table[j, 0, rows, :]
                dy = ay - table[j, 1, rows, :]
                dz = az - table[j, 2, rows, :]
                shell = shell_of(dx * dx + dy * dy + dz * dz)
                held[STEP * step + u, rows, :] = shell
                totals[g % 2] = totals[g % 2] + weight_of(shell) * table[j, 3, rows, :]
            acc[i] = acc[i] + (totals[0] + totals[1])
        shell_copy(step).start()
        return carry

    lax.fori_loop(0, steps, whole, 0)

    def blank(step, carry):
        for u in range(STEP):
            i = lists[2, STEP * step + u]
            acc[i] = acc[i] + origin[lists[3, STEP * step + u]]
        return carry

    lax.fori_loop(0, (lists[5, 0] + STEP - 1) // STEP, blank, 0)

    def settle(step, carry):
        shell_copy(step).wait()
        return carry

    lax.fori_loop(0, steps, settle, 0)
    dens = jnp.sum(acc[0:RES], 1) * KERNEL_NORM
    dens_out[...] = dens
    inverse = 1.0 / jnp.maximum(dens, DENS_FLOOR)
    cube = dens * dens * dens
    field_out[:, 0, :] = STIFF * (cube * cube * dens - 1.0) * inverse * inverse
    field_out[:, 1, :] = res[:, 6, :] * inverse


def two_pieces(value):
    high = value.astype(jnp.bfloat16)
    return high, (value - high.astype(jnp.float32)).astype(jnp.bfloat16)


def write_factors(nb, far, press, damp, centre):
    row = lax.broadcasted_iota(jnp.int32, (8, BLK), 0)
    upper = row < 3
    lower = (row >= 3) & (row < 6)

    def store(ref, j, values):
        for p, some in enumerate(zip(*[pieces(v) for v in values])):
            for h in range(0, len(values), 2):
                pair = jnp.concatenate([some[h].astype(jnp.float32), some[h + 1].astype(jnp.float32)], 0)
                pair = pair.astype(jnp.bfloat16)
                rows = pl.ds(8 * (len(values) * p + h), 16)
                ref[j, rows, 0:BLK] = pair
                ref[j, rows, BLK : 2 * BLK] = pair

    def some(step, carry):
        for u in range(FACTOR_STEP):
            j = step * FACTOR_STEP + u
            tile = nb[j]
            mass = jnp.broadcast_to(tile[6:7, :], (8, BLK))
            scaled = tile * HALF
            middle = jnp.where(upper, jnp.broadcast_to(scaled[:, 0:1], (8, BLK)), 0.0)
            centre[j] = middle
            place = scaled - middle
            mass_q = mass * jnp.broadcast_to(far[pl.ds(2 * j, 1), :], (8, BLK))
            mass_s = jnp.where(lower, mass * jnp.broadcast_to(far[pl.ds(2 * j + 1, 1), :], (8, BLK)), 0.0)
            mass = jnp.where(upper, mass, 0.0)
            mass_q = jnp.where(upper, mass_q, 0.0)
            store(press, j, (mass, mass * place, mass_q, mass_q * place))
            store(damp, j, (mass_s, mass_s * tile))
        return carry

    lax.fori_loop(0, NJ // FACTOR_STEP, some, 0)


def force_kernel(
    lists, shells, res, nb, field, far, flag, out, held, acc, origin, press, damp, centre, cubes, damps, sem
):
    steps = (lists[4, 0] + WIDE - 1) // WIDE

    def shell_copy(step):
        rows = pl.ds(WIDE * step, WIDE)
        return pltpu.make_async_copy(shells.at[rows], held.at[rows], sem.at[step])

    def fetch(step, carry):
        shell_copy(step).start()
        return carry

    lax.fori_loop(0, steps, fetch, 0)
    write_factors(nb, far, press, damp, centre)
    acc[...] = jnp.zeros_like(acc)
    row = lax.broadcasted_iota(jnp.int32, (8, BLK), 0)
    upper = row < 3
    lower = (row >= 3) & (row < 6)
    scale = jnp.where(upper, HALF, 1.0)

    x, y, z = (nb[:, f, :] * HALF for f in range(3))
    radius2 = x * x + y * y + z * z
    shell = shell_of(radius2)
    cube = shell * shell * shell * nb[:, 6, :]
    drag = cube * radius2 / (radius2 + SOFT) * far[pl.ds(1, NJ, stride=2), :]
    push = cube * far[pl.ds(0, NJ, stride=2), :]
    origin[...] = jnp.zeros_like(origin)
    for f, place in enumerate((x, y, z)):
        origin[:, f, :] = jnp.broadcast_to(jnp.sum(cube * place, 1, keepdims=True), (NJ, BLK))
        origin[:, 8 + f, :] = jnp.broadcast_to(jnp.sum(push * place, 1, keepdims=True), (NJ, BLK))
        origin[:, 3 + f, :] = jnp.broadcast_to(jnp.sum(drag * nb[:, 3 + f, :], 1, keepdims=True), (NJ, BLK))

    def coefficients(i):
        q = jnp.broadcast_to(field[i, 0:1, :], (8, BLK))
        s = jnp.broadcast_to(field[i, 1:2, :], (8, BLK))
        return jnp.where(upper, q, jnp.where(lower, s, 0.0))

    def geometry(u, n):
        for g in range(GROUPS // 2):
            rows = pl.ds(16 * g, 16)
            shell = held[n, rows, :]
            ratio = 1.0 - shell
            radius2 = ratio * ratio
            cube = shell * shell * shell
            soft = lax.rsqrt(radius2 + SOFT)
            high, low = two_pieces(cube)
            cubes[u, rows, :] = high
            cubes[u, pl.ds(BLK + 16 * g, 16), :] = low
            high, low = two_pieces(cube * (radius2 * (soft * soft)))
            damps[u, rows, :] = high
            damps[u, pl.ds(BLK + 16 * g, 16), :] = low

    def sums_of(u, j):
        first = jnp.dot(press[j], cubes[u], preferred_element_type=jnp.float32)
        second = jnp.dot(damp[j], damps[u], preferred_element_type=jnp.float32)
        return first[0:32] + (first[32:64] + first[64:96]), second[0:16] + (second[16:32] + second[32:48])

    def whole(step, before):
        @pl.when(step < steps)
        def _():
            shell_copy(step).wait()

        sums = [sums_of(u, j) for u, (i, j) in enumerate(before)]
        after = []
        for u in range(WIDE):
            n = jnp.minimum(WIDE * step + u, PAIR_MAX - 1)
            geometry(u, n)
            after.append((lists[0, n], lists[1, n]))
        for u, (i, j) in enumerate(before):
            own = jnp.minimum(i, RES - 1)
            first, second = sums[u]
            place = res[own] * scale - centre[j]
            both = place * (first[0:8] + second[0:8]) - (first[8:16] + second[8:16])
            acc[i] = acc[i] + (coefficients(own) * both + (place * first[16:24] - first[24:32]))
        return tuple(after)

    cubes[...] = jnp.zeros_like(cubes)
    damps[...] = jnp.zeros_like(damps)
    nowhere = tuple((jnp.int32(RES), jnp.int32(0)) for _ in range(WIDE))
    lax.fori_loop(0, steps + 1, whole, nowhere)

    def blank(step, carry):
        for u in range(STEP):
            i = lists[2, STEP * step + u]
            j = lists[3, STEP * step + u]
            own = jnp.minimum(i, RES - 1)
            acc[i] = acc[i] - (coefficients(own) * origin[j, 0:8, :] + origin[j, 8:16, :])
        return carry

    lax.fori_loop(0, (lists[5, 0] + STEP - 1) // STEP, blank, 0)
    gravity = jnp.where(lax.broadcasted_iota(jnp.int32, (3, BLK), 0) == 2, -GRAVITY, 0.0)
    for b in range(RES):
        total = acc[b, 0:3, :] * PRESS_SCALE + acc[b, 3:6, :] * VISC_SCALE + gravity
        if b < NSTAY:
            total = total * (1.0 - flag[b : b + 1, :].astype(jnp.float32))
        out[:, b * BLK : (b + 1) * BLK] = total


def density_call(count, pairs, resident, neighbour):
    return pl.pallas_call(
        density_kernel,
        out_shape=(
            jax.ShapeDtypeStruct((RES, BLK), jnp.float32),
            jax.ShapeDtypeStruct((RES, 2, BLK), jnp.float32),
            jax.ShapeDtypeStruct((8, PAIR_MAX), jnp.int32),
            jax.ShapeDtypeStruct((PAIR_MAX, BLK, BLK), jnp.float32),
        ),
        in_specs=[SMEM, VMEM, VMEM, VMEM],
        out_specs=(VMEM, VMEM, VMEM, ANY),
        scratch_shapes=[
            pltpu.VMEM((NJ, 4, BLK, BLK), jnp.float32),
            pltpu.VMEM((RES + 1, 8, BLK), jnp.float32),
            pltpu.VMEM((NJ, 8, BLK), jnp.float32),
            pltpu.VMEM((PAIR_MAX, BLK, BLK), jnp.float32),
            pltpu.SMEM((8, PAIR_MAX), jnp.int32),
            pltpu.SemaphoreType.DMA,
            pltpu.SemaphoreType.DMA((PAIR_MAX // STEP,)),
        ],
        compiler_params=pltpu.CompilerParams(vmem_limit_bytes=LIMIT),
    )(count, pairs, resident, neighbour)


def force_call(lists, shells, resident, neighbour, field, far, flag):
    return pl.pallas_call(
        force_kernel,
        out_shape=jax.ShapeDtypeStruct((3, RES * BLK), jnp.float32),
        in_specs=[SMEM, ANY, VMEM, VMEM, VMEM, VMEM, VMEM],
        out_specs=VMEM,
        scratch_shapes=[
            pltpu.VMEM((PAIR_MAX, BLK, BLK), jnp.float32),
            pltpu.VMEM((RES + 1, 8, BLK), jnp.float32),
            pltpu.VMEM((NJ, 16, BLK), jnp.float32),
            pltpu.VMEM((NJ, 96, 2 * BLK), jnp.bfloat16),
            pltpu.VMEM((NJ, 48, 2 * BLK), jnp.bfloat16),
            pltpu.VMEM((NJ, 8, BLK), jnp.float32),
            pltpu.VMEM((WIDE, 2 * BLK, BLK), jnp.bfloat16),
            pltpu.VMEM((WIDE, 2 * BLK, BLK), jnp.bfloat16),
            pltpu.SemaphoreType.DMA((PAIR_MAX // WIDE,)),
        ],
        compiler_params=pltpu.CompilerParams(vmem_limit_bytes=LIMIT),
    )(lists, shells, resident, neighbour, field, far, flag)


def on_device(stay, leave, stay_flag, send_list, send_count, wanted, pair_tiles, pair_count):
    slabs = send_list.shape[1]
    members = wanted.shape[1]
    leaving = leave.reshape(7, slabs * SM, BLK).transpose(1, 0, 2)
    staying = stay.reshape(7, NSTAY, BLK).transpose(1, 0, 2)
    resident, neighbour, asked = migrate_call(
        slabs, members, send_list.transpose(0, 2, 1), send_count, wanted.transpose(0, 2, 1), leaving, staying
    )
    dens, field, lists, shells = density_call(pair_count, pair_tiles[0], resident, neighbour)
    far = field_call(slabs, members, asked, field)
    accel = force_call(lists, shells, resident, neighbour, field, far, stay_flag.reshape(NSTAY, BLK))
    return (dens.reshape(-1), accel)


def solution(mesh):
    in_specs = (
        P(None, ("slab", "grp")),
        P(None, ("slab", "grp")),
        P(("slab", "grp")),
        P(("slab", "grp"), None, None),
        P(("slab", "grp"), None),
        P(("slab", "grp"), None, None),
        P(("slab", "grp"), None, None),
        P(("slab", "grp")),
    )
    out_specs = (P(("slab", "grp")), P(None, ("slab", "grp")))
    return jax.shard_map(
        on_device, mesh=mesh, in_specs=in_specs, out_specs=out_specs, check_vma=False
    )
```

```python
import functools
import math

import jax
import jax.numpy as jnp
from jax import lax
from jax.experimental import pallas as pl
from jax.experimental.pallas import tpu as pltpu
from jax.sharding import PartitionSpec as P

BLK = 128
SM = 2
GH = 4
NEED = 4
PAIR_MAX = 256
NSTAY = 16
RES = 80
NJ = 40
GROUPS = BLK // 8
COLUMN_STEP = 8
STEP = 4
WIDE = 8
FACTOR_STEP = 4

KERNEL_NORM = 21.0 / (16.0 * math.pi)
SMOOTH = 1.0
HALF = 0.5 / SMOOTH
DENS_FLOOR = 0.5
STIFF = 0.02
VISCOUS = 0.1
GRAVITY = 1.0
TINY = 1e-30
SOFT = 0.01 * HALF * HALF
PRESS_SCALE = 5.0 * KERNEL_NORM / (SMOOTH * SMOOTH) / HALF
VISC_SCALE = -VISCOUS * 5.0 * KERNEL_NORM / (SMOOTH * SMOOTH)

VMEM = pl.BlockSpec(memory_space=pltpu.VMEM)
SMEM = pl.BlockSpec(memory_space=pltpu.SMEM)
ANY = pl.BlockSpec(memory_space=pl.ANY)
MESH = pl.DeviceIdType.MESH
LIMIT = 56 * 1024 * 1024


def ring_steps(r, size):
    return min(r, size - r)


def migrate_kernel(
    slabs, members, lists_in, counts_in, wanted_in, leave, stay,
    res_out, nb_out, asked_out,
    lists, counts, wanted, leaving, staying, packed, res, nb, request, asked, names, chosen,
    row_send, row_recv, ghost_send, ghost_recv, name_send, name_recv, near_send, near_recv, local_sem,
):
    slab = lax.axis_index("slab")
    grp = lax.axis_index("grp")
    ghosts = members * NEED
    barrier = pltpu.get_barrier_semaphore()

    far_slabs = sorted(range(1, slabs), key=lambda r: -ring_steps(r // 8, 4) - ring_steps(r // 2 % 4, 4))
    far_members = sorted(range(1, members), key=lambda r: -ring_steps(r, members))
    for r in far_members:
        pl.semaphore_signal(barrier, inc=1, device_id={"grp": (grp + r) % members}, device_id_type=MESH)
    for r in far_slabs:
        pl.semaphore_signal(barrier, inc=1, device_id={"slab": (slab + r) % slabs}, device_id_type=MESH)
    fetch_leave = pltpu.make_async_copy(leave, leaving, local_sem.at[0])
    fetch_stay = pltpu.make_async_copy(stay, staying, local_sem.at[1])
    fetch_leave.start()
    fetch_stay.start()
    small = [
        pltpu.make_async_copy(source, target, local_sem.at[5 + n])
        for n, (source, target) in enumerate(((wanted_in, wanted), (lists_in, lists), (counts_in, counts)))
    ]
    for copy in small:
        copy.start()
    for copy in small:
        copy.wait()
    lane = lax.broadcasted_iota(jnp.int32, (1, BLK), 1)
    for p in range(members):
        ask = jnp.zeros((1, BLK), jnp.int32)
        for k in range(NEED):
            ask = jnp.where(lane == k, wanted[0, k, p], ask)
        request[p] = ask
    fetch_stay.wait()
    for b in range(NSTAY):
        res[b, 0:7, :] = staying[b]
        res[b, 7:8, :] = jnp.ones((1, BLK), jnp.float32)
    fetch_leave.wait()
    for t in range(slabs):
        count = counts[0, t]
        for k in range(SM):
            keep = jnp.broadcast_to(jnp.minimum(jnp.maximum(count - k, 0), 1), (1, BLK)).astype(jnp.float32)
            packed[t * SM + k, 0:7, :] = leaving[lists[0, k, t]] * keep
            packed[t * SM + k, 7:8, :] = keep
    pl.semaphore_wait(barrier, slabs - 1 + members - 1)

    def name_copy(r):
        target = (grp + r) % members
        return pltpu.make_async_remote_copy(
            src_ref=request.at[target], dst_ref=asked.at[grp], send_sem=name_send.at[r], recv_sem=name_recv.at[r],
            device_id={"grp": target}, device_id_type=MESH,
        )

    def row_copy(r):
        target = (slab + r) % slabs
        return pltpu.make_async_remote_copy(
            src_ref=packed.at[pl.ds(target * SM, SM)], dst_ref=res.at[pl.ds(NSTAY + slab * SM, SM)],
            send_sem=row_send.at[r], recv_sem=row_recv.at[r],
            device_id={"slab": target}, device_id_type=MESH,
        )

    def ghost_copy(side):
        first = NSTAY - GH if side == 0 else 0
        target = (slab + (1 if side == 0 else slabs - 1)) % slabs
        return pltpu.make_async_remote_copy(
            src_ref=res.at[pl.ds(first, GH)], dst_ref=nb.at[pl.ds(ghosts + side * GH, GH)],
            send_sem=ghost_send.at[side], recv_sem=ghost_recv.at[side],
            device_id={"slab": target}, device_id_type=MESH,
        )

    def near_copy(r):
        target = (grp + r) % members
        return pltpu.make_async_remote_copy(
            src_ref=chosen.at[target], dst_ref=nb.at[pl.ds(grp * NEED, NEED)],
            send_sem=near_send.at[r], recv_sem=near_recv.at[r],
            device_id={"grp": target}, device_id_type=MESH,
        )

    def each(order, step):
        for r in order:
            step(r)

    each(far_members, lambda r: name_copy(r).start())
    each(far_slabs, lambda r: row_copy(r).start())
    ghost_copy(0).start()
    ghost_copy(1).start()
    asked[grp] = request[grp]
    mine = pl.ds(NSTAY + slab * SM, SM)
    res[mine] = packed[pl.ds(slab * SM, SM)]
    each(far_members, lambda r: name_copy(r).wait_recv())
    local = pltpu.make_async_copy(asked, names, local_sem.at[2])
    local.start()
    local.wait()
    asked_out[...] = asked[...]
    each(far_slabs, lambda r: row_copy(r).wait_recv())
    for d in range(members):
        for k in range(NEED):
            chosen[d, k] = res[names[d, 0, k]]
    each(far_members, lambda r: near_copy(r).start())
    nb[pl.ds(grp * NEED, NEED)] = chosen[grp]
    store_res = pltpu.make_async_copy(res, res_out, local_sem.at[3])
    store_res.start()
    ghost_copy(0).wait_recv()
    ghost_copy(1).wait_recv()
    for side, some in ((0, slab > 0), (1, slab < slabs - 1)):
        rows = pl.ds(ghosts + side * GH, GH)
        nb[rows] = nb[rows] * some.astype(jnp.float32)
    each(far_members, lambda r: near_copy(r).wait_recv())
    store_nb = pltpu.make_async_copy(nb, nb_out, local_sem.at[4])
    store_nb.start()
    each(far_members, lambda r: name_copy(r).wait_send())
    each(far_slabs, lambda r: row_copy(r).wait_send())
    each(far_members, lambda r: near_copy(r).wait_send())
    ghost_copy(0).wait_send()
    ghost_copy(1).wait_send()
    store_res.wait()
    store_nb.wait()


def migrate_call(slabs, members, lists, counts, wanted, leave, stay):
    blocks = NSTAY + slabs * SM
    near = members * NEED + 2 * GH
    f32 = jnp.float32
    dma = pltpu.SemaphoreType.DMA
    return pl.pallas_call(
        functools.partial(migrate_kernel, slabs, members),
        out_shape=(
            jax.ShapeDtypeStruct((blocks, 8, BLK), f32),
            jax.ShapeDtypeStruct((near, 8, BLK), f32),
            jax.ShapeDtypeStruct((members, 1, BLK), jnp.int32),
        ),
        in_specs=[ANY, ANY, ANY, ANY, ANY],
        out_specs=(ANY, ANY, VMEM),
        scratch_shapes=[
            pltpu.SMEM(lists.shape, jnp.int32),
            pltpu.SMEM(counts.shape, jnp.int32),
            pltpu.SMEM(wanted.shape, jnp.int32),
            pltpu.VMEM(leave.shape, f32),
            pltpu.VMEM(stay.shape, f32),
            pltpu.VMEM((slabs * SM, 8, BLK), f32),
            pltpu.VMEM((blocks, 8, BLK), f32),
            pltpu.VMEM((near, 8, BLK), f32),
            pltpu.VMEM((members, 1, BLK), jnp.int32),
            pltpu.VMEM((members, 1, BLK), jnp.int32),
            pltpu.SMEM((members, 1, BLK), jnp.int32),
            pltpu.VMEM((members, NEED, 8, BLK), f32),
            dma((slabs,)), dma((slabs,)), dma((2,)), dma((2,)),
            dma((members,)), dma((members,)), dma((members,)), dma((members,)), dma((8,)),
        ],
        compiler_params=pltpu.CompilerParams(collective_id=0, has_side_effects=True, vmem_limit_bytes=LIMIT),
    )(lists, counts, wanted, leave, stay)


def field_kernel(slabs, members, messages, out, near_send, near_recv, edge_send, edge_recv, own_sem):
    slab = lax.axis_index("slab")
    grp = lax.axis_index("grp")
    above = (slab + 1) % slabs
    below = (slab + slabs - 1) % slabs
    far_members = sorted(range(1, members), key=lambda r: -ring_steps(r, members))
    barrier = pltpu.get_barrier_semaphore()
    for r in far_members:
        pl.semaphore_signal(barrier, inc=1, device_id={"grp": (grp + r) % members}, device_id_type=MESH)
    for target in (above, below):
        pl.semaphore_signal(barrier, inc=1, device_id={"slab": target}, device_id_type=MESH)
    own = pltpu.make_async_copy(messages.at[grp], out.at[grp], own_sem)
    own.start()
    pl.semaphore_wait(barrier, members + 1)

    def near_copy(r):
        target = (grp + r) % members
        return pltpu.make_async_remote_copy(
            src_ref=messages.at[target], dst_ref=out.at[grp], send_sem=near_send.at[r], recv_sem=near_recv.at[r],
            device_id={"grp": target}, device_id_type=MESH,
        )

    def edge_copy(side):
        return pltpu.make_async_remote_copy(
            src_ref=messages.at[members + side], dst_ref=out.at[members + side],
            send_sem=edge_send.at[side], recv_sem=edge_recv.at[side],
            device_id={"slab": above if side == 0 else below}, device_id_type=MESH,
        )

    copies = [near_copy(r) for r in far_members] + [edge_copy(0), edge_copy(1)]
    for copy in copies:
        copy.start()
    own.wait()
    for copy in copies:
        copy.wait_recv()
    for copy in copies:
        copy.wait_send()


def field_call(slabs, members, messages):
    dma = pltpu.SemaphoreType.DMA
    out = pl.pallas_call(
        functools.partial(field_kernel, slabs, members),
        out_shape=jax.ShapeDtypeStruct((members + 2, 8, BLK), jnp.float32),
        in_specs=[ANY],
        out_specs=ANY,
        scratch_shapes=[dma((members,)), dma((members,)), dma((2,)), dma((2,)), dma],
        compiler_params=pltpu.CompilerParams(collective_id=1, has_side_effects=True),
    )(messages)
    return out.reshape(-1, BLK)


def shell_of(radius2):
    ratio = radius2 * lax.rsqrt(jnp.maximum(radius2, TINY))
    return jnp.maximum(1.0 - ratio, 0.0)


def weight_of(shell):
    square = shell * shell
    return square * square * (1.25 - shell)


def write_lists(count, pairs, res, nb, out):
    left = pairs[0:1, :]
    right = pairs[1:2, :]
    lane = lax.broadcasted_iota(jnp.int32, (1, PAIR_MAX), 1)
    res_live = res[:, 7, :]
    nb_live = nb[:, 7, :]
    res_live = jnp.concatenate([res_live, res_live], 1)
    nb_live = jnp.concatenate([nb_live, nb_live], 1)
    hit = lax.broadcasted_iota(jnp.int32, (RES, PAIR_MAX), 0) == left
    live_left = jnp.sum(jnp.where(hit, res_live, 0.0), 0, keepdims=True)
    hit = lax.broadcasted_iota(jnp.int32, (NJ, PAIR_MAX), 0) == right
    live_right = jnp.sum(jnp.where(hit, nb_live, 0.0), 0, keepdims=True)
    valid = jnp.where(lane < count, live_right, 0.0)
    heavy = valid * live_left
    light = valid * (1.0 - live_left)
    before = lax.broadcasted_iota(jnp.int32, (PAIR_MAX, PAIR_MAX), 0) < lax.broadcasted_iota(
        jnp.int32, (PAIR_MAX, PAIR_MAX), 1
    )
    blank = jnp.zeros((6, PAIR_MAX), jnp.float32)
    kinds = jnp.concatenate([heavy, light, blank], 0).astype(jnp.bfloat16)
    spots = jnp.dot(kinds, jnp.where(before, 1.0, 0.0).astype(jnp.bfloat16), preferred_element_type=jnp.float32)
    names = jnp.concatenate([left.astype(jnp.float32), right.astype(jnp.float32), blank], 0).astype(jnp.bfloat16)
    row = lax.broadcasted_iota(jnp.int32, (PAIR_MAX, PAIR_MAX), 0).astype(jnp.float32)
    sums = jnp.sum(jnp.concatenate([heavy, light, blank], 0), 1, keepdims=True)
    for kind, member in ((0, heavy), (1, light)):
        target = jnp.where(member > 0.5, spots[kind : kind + 1, :], -1.0)
        chosen = jnp.where(row == target, 1.0, 0.0).astype(jnp.bfloat16)
        packed = lax.dot_general(names, chosen, (((1,), (1,)), ((), ())), preferred_element_type=jnp.float32)
        amount = jnp.broadcast_to(sums[kind : kind + 1, :], (1, PAIR_MAX))
        filled = lane.astype(jnp.float32) < amount
        out[2 * kind : 2 * kind + 1, :] = jnp.where(filled, packed[0:1, :], float(RES)).astype(jnp.int32)
        out[2 * kind + 1 : 2 * kind + 2, :] = packed[1:2, :].astype(jnp.int32)
        out[4 + kind : 5 + kind, :] = amount.astype(jnp.int32)
    out[6:8, :] = jnp.zeros((2, PAIR_MAX), jnp.int32)


def pieces(value):
    high = value.astype(jnp.bfloat16)
    rest = value - high.astype(jnp.float32)
    mid = rest.astype(jnp.bfloat16)
    low = (rest - mid.astype(jnp.float32)).astype(jnp.bfloat16)
    return high, mid, low


def write_columns(nb, table, fields):
    count = len(fields)
    row = lax.broadcasted_iota(jnp.int32, (32, count * BLK), 0)
    spot = lax.broadcasted_iota(jnp.int32, (32, count * BLK), 1) // BLK
    spread = jnp.zeros((32, count * BLK), jnp.float32)
    for n, (field, scale) in enumerate(fields):
        mine = (row == field) | (row == 8 + field) | (row == 16 + field)
        spread = jnp.where((spot == n) & mine, scale, spread)
    spread = spread.astype(jnp.bfloat16)

    def some(step, carry):
        for u in range(COLUMN_STEP):
            j = step * COLUMN_STEP + u
            high, mid, low = (p.astype(jnp.float32) for p in pieces(nb[j]))
            stacked = jnp.concatenate([high, mid, low, jnp.zeros((8, BLK), jnp.float32)], 0)
            turned = jnp.transpose(stacked, (1, 0)).astype(jnp.bfloat16)
            wide = jnp.dot(turned, spread, preferred_element_type=jnp.float32)
            for n in range(count):
                table[j, n] = wide[:, n * BLK : (n + 1) * BLK]
        return carry

    lax.fori_loop(0, NJ // COLUMN_STEP, some, 0)


def density_kernel(
    count_in, pairs_in, names_in, res_in, nb_in, dens_out, field_out, list_out, message_out, shell_out,
    count, pairs, names, res, nb, table, acc, origin, held, lists, sem, held_sem,
):
    members = names.shape[0]
    fetches = [
        pltpu.make_async_copy(source, target, sem.at[n])
        for n, (source, target) in enumerate(
            ((nb_in, nb), (res_in, res), (pairs_in, pairs), (count_in, count), (names_in, names))
        )
    ]
    for fetch in fetches:
        fetch.start()
    for fetch in fetches:
        fetch.wait()
    write_lists(count[0], pairs, res, nb, list_out)
    copy = pltpu.make_async_copy(list_out, lists, sem.at[5])
    copy.start()
    write_columns(nb, table, ((0, HALF), (1, HALF), (2, HALF), (6, 4.0)))
    x, y, z = (nb[:, f, :] * HALF for f in range(3))
    alone = jnp.sum(weight_of(shell_of(x * x + y * y + z * z)) * (4.0 * nb[:, 6, :]), 1, keepdims=True)
    origin[...] = jnp.zeros_like(origin)
    origin[:, 0, :] = jnp.broadcast_to(alone, (NJ, BLK))
    acc[...] = jnp.zeros_like(acc)
    copy.wait()
    steps = (lists[4, 0] + STEP - 1) // STEP

    def shell_copy(step):
        rows = pl.ds(STEP * step, STEP)
        return pltpu.make_async_copy(held.at[rows], shell_out.at[rows], held_sem.at[step])

    def whole(step, carry):
        for u in range(STEP):
            i = lists[0, STEP * step + u]
            j = lists[1, STEP * step + u]
            ax, ay, az = (res[jnp.minimum(i, RES - 1), f : f + 1, :] * HALF for f in range(3))
            ax, ay, az = (jnp.broadcast_to(a, (8, BLK)) for a in (ax, ay, az))
            totals = [jnp.zeros((8, BLK), jnp.float32)] * 2
            for g in range(GROUPS):
                rows = pl.ds(8 * g, 8)
                dx = ax - table[j, 0, rows, :]
                dy = ay - table[j, 1, rows, :]
                dz = az - table[j, 2, rows, :]
                shell = shell_of(dx * dx + dy * dy + dz * dz)
                held[STEP * step + u, rows, :] = shell
                totals[g % 2] = totals[g % 2] + weight_of(shell) * table[j, 3, rows, :]
            acc[i] = acc[i] + (totals[0] + totals[1])
        shell_copy(step).start()
        return carry

    lax.fori_loop(0, steps, whole, 0)

    def blank(step, carry):
        for u in range(STEP):
            i = lists[2, STEP * step + u]
            acc[i] = acc[i] + origin[lists[3, STEP * step + u]]
        return carry

    lax.fori_loop(0, (lists[5, 0] + STEP - 1) // STEP, blank, 0)
    dens = jnp.sum(acc[0:RES], 1) * KERNEL_NORM
    dens_out[...] = dens
    inverse = 1.0 / jnp.maximum(dens, DENS_FLOOR)
    cube = dens * dens * dens
    field_out[:, 0, :] = STIFF * (cube * cube * dens - 1.0) * inverse * inverse
    field_out[:, 1, :] = res[:, 6, :] * inverse
    for d in range(members):
        for k in range(NEED):
            message_out[d, 2 * k : 2 * k + 2, :] = field_out[names[d, 0, k]]
    for k in range(GH):
        message_out[members, 2 * k : 2 * k + 2, :] = field_out[NSTAY - GH + k]
        message_out[members + 1, 2 * k : 2 * k + 2, :] = field_out[k]

    def settle(step, carry):
        shell_copy(step).wait()
        return carry

    lax.fori_loop(0, steps, settle, 0)


def two_pieces(value):
    high = value.astype(jnp.bfloat16)
    return high, (value - high.astype(jnp.float32)).astype(jnp.bfloat16)


def write_factors(nb, far, press, damp, centre):
    row = lax.broadcasted_iota(jnp.int32, (8, BLK), 0)
    upper = row < 3
    lower = (row >= 3) & (row < 6)

    def store(ref, j, values):
        for p, some in enumerate(zip(*[pieces(v) for v in values])):
            for h in range(0, len(values), 2):
                pair = jnp.concatenate([some[h].astype(jnp.float32), some[h + 1].astype(jnp.float32)], 0)
                pair = pair.astype(jnp.bfloat16)
                rows = pl.ds(8 * (len(values) * p + h), 16)
                ref[j, rows, 0:BLK] = pair
                ref[j, rows, BLK : 2 * BLK] = pair

    def some(step, carry):
        for u in range(FACTOR_STEP):
            j = step * FACTOR_STEP + u
            tile = nb[j]
            mass = jnp.broadcast_to(tile[6:7, :], (8, BLK))
            scaled = tile * HALF
            middle = jnp.where(upper, jnp.broadcast_to(scaled[:, 0:1], (8, BLK)), 0.0)
            centre[j] = middle
            place = scaled - middle
            mass_q = mass * jnp.broadcast_to(far[pl.ds(2 * j, 1), :], (8, BLK))
            mass_s = jnp.where(lower, mass * jnp.broadcast_to(far[pl.ds(2 * j + 1, 1), :], (8, BLK)), 0.0)
            mass = jnp.where(upper, mass, 0.0)
            mass_q = jnp.where(upper, mass_q, 0.0)
            store(press, j, (mass, mass * place, mass_q, mass_q * place))
            store(damp, j, (mass_s, mass_s * tile))
        return carry

    lax.fori_loop(0, NJ // FACTOR_STEP, some, 0)


def force_kernel(
    lists_in, shells, res_in, nb_in, field_in, far_in, flag_in, out,
    lists, res, nb, field, far, flag, held, acc, origin, press, damp, centre, cubes, damps, sem, fetch_sem,
):
    fetches = [
        pltpu.make_async_copy(source, target, fetch_sem.at[n])
        for n, (source, target) in enumerate(
            ((lists_in, lists), (nb_in, nb), (far_in, far), (res_in, res), (field_in, field), (flag_in, flag))
        )
    ]
    for fetch in fetches:
        fetch.start()
    fetches[0].wait()
    steps = (lists[4, 0] + WIDE - 1) // WIDE

    def shell_copy(step):
        rows = pl.ds(WIDE * step, WIDE)
        return pltpu.make_async_copy(shells.at[rows], held.at[rows], sem.at[step])

    def fetch(step, carry):
        shell_copy(step).start()
        return carry

    lax.fori_loop(0, steps, fetch, 0)
    fetches[1].wait()
    fetches[2].wait()
    write_factors(nb, far, press, damp, centre)
    acc[...] = jnp.zeros_like(acc)
    row = lax.broadcasted_iota(jnp.int32, (8, BLK), 0)
    upper = row < 3
    lower = (row >= 3) & (row < 6)
    scale = jnp.where(upper, HALF, 1.0)

    x, y, z = (nb[:, f, :] * HALF for f in range(3))
    radius2 = x * x + y * y + z * z
    shell = shell_of(radius2)
    cube = shell * shell * shell * nb[:, 6, :]
    drag = cube * radius2 / (radius2 + SOFT) * far[pl.ds(1, NJ, stride=2), :]
    push = cube * far[pl.ds(0, NJ, stride=2), :]
    origin[...] = jnp.zeros_like(origin)
    for f, place in enumerate((x, y, z)):
        origin[:, f, :] = jnp.broadcast_to(jnp.sum(cube * place, 1, keepdims=True), (NJ, BLK))
        origin[:, 8 + f, :] = jnp.broadcast_to(jnp.sum(push * place, 1, keepdims=True), (NJ, BLK))
        origin[:, 3 + f, :] = jnp.broadcast_to(jnp.sum(drag * nb[:, 3 + f, :], 1, keepdims=True), (NJ, BLK))

    def coefficients(i):
        q = jnp.broadcast_to(field[i, 0:1, :], (8, BLK))
        s = jnp.broadcast_to(field[i, 1:2, :], (8, BLK))
        return jnp.where(upper, q, jnp.where(lower, s, 0.0))

    def geometry(u, n):
        for g in range(GROUPS // 2):
            rows = pl.ds(16 * g, 16)
            shell = held[n, rows, :]
            ratio = 1.0 - shell
            radius2 = ratio * ratio
            cube = shell * shell * shell
            soft = lax.rsqrt(radius2 + SOFT)
            high, low = two_pieces(cube)
            cubes[u, rows, :] = high
            cubes[u, pl.ds(BLK + 16 * g, 16), :] = low
            high, low = two_pieces(cube * (radius2 * (soft * soft)))
            damps[u, rows, :] = high
            damps[u, pl.ds(BLK + 16 * g, 16), :] = low

    def sums_of(u, j):
        first = jnp.dot(press[j], cubes[u], preferred_element_type=jnp.float32)
        second = jnp.dot(damp[j], damps[u], preferred_element_type=jnp.float32)
        return first[0:32] + (first[32:64] + first[64:96]), second[0:16] + (second[16:32] + second[32:48])

    def whole(step, before):
        @pl.when(step < steps)
        def _():
            shell_copy(step).wait()

        sums = [sums_of(u, j) for u, (i, j) in enumerate(before)]
        after = []
        for u in range(WIDE):
            n = jnp.minimum(WIDE * step + u, PAIR_MAX - 1)
            geometry(u, n)
            after.append((lists[0, n], lists[1, n]))
        for u, (i, j) in enumerate(before):
            own = jnp.minimum(i, RES - 1)
            first, second = sums[u]
            place = res[own] * scale - centre[j]
            both = place * (first[0:8] + second[0:8]) - (first[8:16] + second[8:16])
            acc[i] = acc[i] + (coefficients(own) * both + (place * first[16:24] - first[24:32]))
        return tuple(after)

    for copy in fetches[3:]:
        copy.wait()
    cubes[...] = jnp.zeros_like(cubes)
    damps[...] = jnp.zeros_like(damps)
    nowhere = tuple((jnp.int32(RES), jnp.int32(0)) for _ in range(WIDE))
    lax.fori_loop(0, steps + 1, whole, nowhere)

    def blank(step, carry):
        for u in range(STEP):
            i = lists[2, STEP * step + u]
            j = lists[3, STEP * step + u]
            own = jnp.minimum(i, RES - 1)
            acc[i] = acc[i] - (coefficients(own) * origin[j, 0:8, :] + origin[j, 8:16, :])
        return carry

    lax.fori_loop(0, (lists[5, 0] + STEP - 1) // STEP, blank, 0)
    gravity = jnp.where(lax.broadcasted_iota(jnp.int32, (3, BLK), 0) == 2, -GRAVITY, 0.0)
    for b in range(RES):
        total = acc[b, 0:3, :] * PRESS_SCALE + acc[b, 3:6, :] * VISC_SCALE + gravity
        if b < NSTAY:
            total = total * (1.0 - flag[b : b + 1, :].astype(jnp.float32))
        out[:, b * BLK : (b + 1) * BLK] = total


def density_call(count, pairs, names, resident, neighbour):
    members = names.shape[0]
    return pl.pallas_call(
        density_kernel,
        out_shape=(
            jax.ShapeDtypeStruct((RES, BLK), jnp.float32),
            jax.ShapeDtypeStruct((RES, 2, BLK), jnp.float32),
            jax.ShapeDtypeStruct((8, PAIR_MAX), jnp.int32),
            jax.ShapeDtypeStruct((members + 2, 8, BLK), jnp.float32),
            jax.ShapeDtypeStruct((PAIR_MAX, BLK, BLK), jnp.float32),
        ),
        in_specs=[ANY] * 5,
        out_specs=(VMEM, VMEM, VMEM, VMEM, ANY),
        scratch_shapes=[
            pltpu.SMEM(count.shape, jnp.int32),
            pltpu.VMEM(pairs.shape, jnp.int32),
            pltpu.SMEM(names.shape, jnp.int32),
            pltpu.VMEM(resident.shape, jnp.float32),
            pltpu.VMEM(neighbour.shape, jnp.float32),
            pltpu.VMEM((NJ, 4, BLK, BLK), jnp.float32),
            pltpu.VMEM((RES + 1, 8, BLK), jnp.float32),
            pltpu.VMEM((NJ, 8, BLK), jnp.float32),
            pltpu.VMEM((PAIR_MAX, BLK, BLK), jnp.float32),
            pltpu.SMEM((8, PAIR_MAX), jnp.int32),
            pltpu.SemaphoreType.DMA((6,)),
            pltpu.SemaphoreType.DMA((PAIR_MAX // STEP,)),
        ],
        compiler_params=pltpu.CompilerParams(vmem_limit_bytes=LIMIT),
    )(count, pairs, names, resident, neighbour)


def force_call(lists, shells, resident, neighbour, field, far, flag):
    return pl.pallas_call(
        force_kernel,
        out_shape=jax.ShapeDtypeStruct((3, RES * BLK), jnp.float32),
        in_specs=[ANY] * 7,
        out_specs=VMEM,
        scratch_shapes=[
            pltpu.SMEM(lists.shape, jnp.int32),
            pltpu.VMEM(resident.shape, jnp.float32),
            pltpu.VMEM(neighbour.shape, jnp.float32),
            pltpu.VMEM(field.shape, jnp.float32),
            pltpu.VMEM(far.shape, jnp.float32),
            pltpu.VMEM(flag.shape, jnp.int32),
            pltpu.VMEM((PAIR_MAX, BLK, BLK), jnp.float32),
            pltpu.VMEM((RES + 1, 8, BLK), jnp.float32),
            pltpu.VMEM((NJ, 16, BLK), jnp.float32),
            pltpu.VMEM((NJ, 96, 2 * BLK), jnp.bfloat16),
            pltpu.VMEM((NJ, 48, 2 * BLK), jnp.bfloat16),
            pltpu.VMEM((NJ, 8, BLK), jnp.float32),
            pltpu.VMEM((WIDE, 2 * BLK, BLK), jnp.bfloat16),
            pltpu.VMEM((WIDE, 2 * BLK, BLK), jnp.bfloat16),
            pltpu.SemaphoreType.DMA((PAIR_MAX // WIDE,)),
            pltpu.SemaphoreType.DMA((6,)),
        ],
        compiler_params=pltpu.CompilerParams(vmem_limit_bytes=LIMIT),
    )(lists, shells, resident, neighbour, field, far, flag)


def on_device(stay, leave, stay_flag, send_list, send_count, wanted, pair_tiles, pair_count):
    slabs = send_list.shape[1]
    members = wanted.shape[1]
    leaving = leave.reshape(7, slabs * SM, BLK).transpose(1, 0, 2)
    staying = stay.reshape(7, NSTAY, BLK).transpose(1, 0, 2)
    resident, neighbour, asked = migrate_call(
        slabs, members, send_list.transpose(0, 2, 1), send_count, wanted.transpose(0, 2, 1), leaving, staying
    )
    dens, field, lists, messages, shells = density_call(pair_count, pair_tiles[0], asked, resident, neighbour)
    far = field_call(slabs, members, messages)
    accel = force_call(lists, shells, resident, neighbour, field, far, stay_flag.reshape(NSTAY, BLK))
    return (dens.reshape(-1), accel)


def solution(mesh):
    in_specs = (
        P(None, ("slab", "grp")),
        P(None, ("slab", "grp")),
        P(("slab", "grp")),
        P(("slab", "grp"), None, None),
        P(("slab", "grp"), None),
        P(("slab", "grp"), None, None),
        P(("slab", "grp"), None, None),
        P(("slab", "grp")),
    )
    out_specs = (P(("slab", "grp")), P(None, ("slab", "grp")))
    return jax.shard_map(
        on_device, mesh=mesh, in_specs=in_specs, out_specs=out_specs, check_vma=False
    )
```

```python
import functools
import math

import jax
import jax.numpy as jnp
from jax import lax
from jax.experimental import pallas as pl
from jax.experimental.pallas import tpu as pltpu
from jax.sharding import PartitionSpec as P

BLK = 128
SM = 2
GH = 4
NEED = 4
PAIR_MAX = 256
NSTAY = 16
RES = 80
NJ = 40
GROUPS = BLK // 8
COLUMN_STEP = 8
STEP = 4
WIDE = 8
NARROW = 6.0
SQUARE_ROWS = 48
FACTOR_STEP = 4

KERNEL_NORM = 21.0 / (16.0 * math.pi)
SMOOTH = 1.0
HALF = 0.5 / SMOOTH
DENS_FLOOR = 0.5
STIFF = 0.02
VISCOUS = 0.1
GRAVITY = 1.0
TINY = 1e-30
FAR = 3e38
SOFT = 0.01 * HALF * HALF
PRESS_SCALE = 5.0 * KERNEL_NORM / (SMOOTH * SMOOTH) / HALF
VISC_SCALE = -VISCOUS * 5.0 * KERNEL_NORM / (SMOOTH * SMOOTH)

VMEM = pl.BlockSpec(memory_space=pltpu.VMEM)
SMEM = pl.BlockSpec(memory_space=pltpu.SMEM)
ANY = pl.BlockSpec(memory_space=pl.ANY)
MESH = pl.DeviceIdType.MESH
LIMIT = 56 * 1024 * 1024


def ring_steps(r, size):
    return min(r, size - r)


def migrate_kernel(
    slabs, members, lists_in, counts_in, wanted_in, leave, stay,
    res_out, nb_out, asked_out,
    lists, counts, wanted, leaving, staying, packed, res, nb, request, asked, names, chosen,
    row_send, row_recv, ghost_send, ghost_recv, name_send, name_recv, near_send, near_recv, local_sem,
):
    slab = lax.axis_index("slab")
    grp = lax.axis_index("grp")
    ghosts = members * NEED
    barrier = pltpu.get_barrier_semaphore()

    far_slabs = sorted(range(1, slabs), key=lambda r: -ring_steps(r // 8, 4) - ring_steps(r // 2 % 4, 4))
    far_members = sorted(range(1, members), key=lambda r: -ring_steps(r, members))
    for r in far_members:
        pl.semaphore_signal(barrier, inc=1, device_id={"grp": (grp + r) % members}, device_id_type=MESH)
    for r in far_slabs:
        pl.semaphore_signal(barrier, inc=1, device_id={"slab": (slab + r) % slabs}, device_id_type=MESH)
    fetch_leave = pltpu.make_async_copy(leave, leaving, local_sem.at[0])
    fetch_stay = pltpu.make_async_copy(stay, staying, local_sem.at[1])
    fetch_leave.start()
    fetch_stay.start()
    small = [
        pltpu.make_async_copy(source, target, local_sem.at[5 + n])
        for n, (source, target) in enumerate(((wanted_in, wanted), (lists_in, lists), (counts_in, counts)))
    ]
    for copy in small:
        copy.start()
    for copy in small:
        copy.wait()
    lane = lax.broadcasted_iota(jnp.int32, (1, BLK), 1)
    for p in range(members):
        ask = jnp.zeros((1, BLK), jnp.int32)
        for k in range(NEED):
            ask = jnp.where(lane == k, wanted[0, k, p], ask)
        request[p] = ask
    fetch_stay.wait()
    for b in range(NSTAY):
        res[b, 0:7, :] = staying[b]
        res[b, 7:8, :] = jnp.ones((1, BLK), jnp.float32)
    fetch_leave.wait()
    for t in range(slabs):
        count = counts[0, t]
        for k in range(SM):
            keep = jnp.broadcast_to(jnp.minimum(jnp.maximum(count - k, 0), 1), (1, BLK)).astype(jnp.float32)
            packed[t * SM + k, 0:7, :] = leaving[lists[0, k, t]] * keep
            packed[t * SM + k, 7:8, :] = keep
    pl.semaphore_wait(barrier, slabs - 1 + members - 1)

    def name_copy(r):
        target = (grp + r) % members
        return pltpu.make_async_remote_copy(
            src_ref=request.at[target], dst_ref=asked.at[grp], send_sem=name_send.at[r], recv_sem=name_recv.at[r],
            device_id={"grp": target}, device_id_type=MESH,
        )

    def row_copy(r):
        target = (slab + r) % slabs
        return pltpu.make_async_remote_copy(
            src_ref=packed.at[pl.ds(target * SM, SM)], dst_ref=res.at[pl.ds(NSTAY + slab * SM, SM)],
            send_sem=row_send.at[r], recv_sem=row_recv.at[r],
            device_id={"slab": target}, device_id_type=MESH,
        )

    def ghost_copy(side):
        first = NSTAY - GH if side == 0 else 0
        target = (slab + (1 if side == 0 else slabs - 1)) % slabs
        return pltpu.make_async_remote_copy(
            src_ref=res.at[pl.ds(first, GH)], dst_ref=nb.at[pl.ds(ghosts + side * GH, GH)],
            send_sem=ghost_send.at[side], recv_sem=ghost_recv.at[side],
            device_id={"slab": target}, device_id_type=MESH,
        )

    def near_copy(r):
        target = (grp + r) % members
        return pltpu.make_async_remote_copy(
            src_ref=chosen.at[target], dst_ref=nb.at[pl.ds(grp * NEED, NEED)],
            send_sem=near_send.at[r], recv_sem=near_recv.at[r],
            device_id={"grp": target}, device_id_type=MESH,
        )

    def each(order, step):
        for r in order:
            step(r)

    each(far_members, lambda r: name_copy(r).start())
    each(far_slabs, lambda r: row_copy(r).start())
    ghost_copy(0).start()
    ghost_copy(1).start()
    asked[grp] = request[grp]
    mine = pl.ds(NSTAY + slab * SM, SM)
    res[mine] = packed[pl.ds(slab * SM, SM)]
    each(far_members, lambda r: name_copy(r).wait_recv())
    local = pltpu.make_async_copy(asked, names, local_sem.at[2])
    local.start()
    local.wait()
    asked_out[...] = asked[...]
    each(far_slabs, lambda r: row_copy(r).wait_recv())
    for d in range(members):
        for k in range(NEED):
            chosen[d, k] = res[names[d, 0, k]]
    each(far_members, lambda r: near_copy(r).start())
    nb[pl.ds(grp * NEED, NEED)] = chosen[grp]
    store_res = pltpu.make_async_copy(res, res_out, local_sem.at[3])
    store_res.start()
    ghost_copy(0).wait_recv()
    ghost_copy(1).wait_recv()
    for side, some in ((0, slab > 0), (1, slab < slabs - 1)):
        rows = pl.ds(ghosts + side * GH, GH)
        nb[rows] = nb[rows] * some.astype(jnp.float32)
    each(far_members, lambda r: near_copy(r).wait_recv())
    store_nb = pltpu.make_async_copy(nb, nb_out, local_sem.at[4])
    store_nb.start()
    each(far_members, lambda r: name_copy(r).wait_send())
    each(far_slabs, lambda r: row_copy(r).wait_send())
    each(far_members, lambda r: near_copy(r).wait_send())
    ghost_copy(0).wait_send()
    ghost_copy(1).wait_send()
    store_res.wait()
    store_nb.wait()


def migrate_call(slabs, members, lists, counts, wanted, leave, stay):
    blocks = NSTAY + slabs * SM
    near = members * NEED + 2 * GH
    f32 = jnp.float32
    dma = pltpu.SemaphoreType.DMA
    return pl.pallas_call(
        functools.partial(migrate_kernel, slabs, members),
        out_shape=(
            jax.ShapeDtypeStruct((blocks, 8, BLK), f32),
            jax.ShapeDtypeStruct((near, 8, BLK), f32),
            jax.ShapeDtypeStruct((members, 1, BLK), jnp.int32),
        ),
        in_specs=[ANY, ANY, ANY, ANY, ANY],
        out_specs=(ANY, ANY, VMEM),
        scratch_shapes=[
            pltpu.SMEM(lists.shape, jnp.int32),
            pltpu.SMEM(counts.shape, jnp.int32),
            pltpu.SMEM(wanted.shape, jnp.int32),
            pltpu.VMEM(leave.shape, f32),
            pltpu.VMEM(stay.shape, f32),
            pltpu.VMEM((slabs * SM, 8, BLK), f32),
            pltpu.VMEM((blocks, 8, BLK), f32),
            pltpu.VMEM((near, 8, BLK), f32),
            pltpu.VMEM((members, 1, BLK), jnp.int32),
            pltpu.VMEM((members, 1, BLK), jnp.int32),
            pltpu.SMEM((members, 1, BLK), jnp.int32),
            pltpu.VMEM((members, NEED, 8, BLK), f32),
            dma((slabs,)), dma((slabs,)), dma((2,)), dma((2,)),
            dma((members,)), dma((members,)), dma((members,)), dma((members,)), dma((8,)),
        ],
        compiler_params=pltpu.CompilerParams(collective_id=0, has_side_effects=True, vmem_limit_bytes=LIMIT),
    )(lists, counts, wanted, leave, stay)


def field_kernel(slabs, members, messages, out, near_send, near_recv, edge_send, edge_recv, own_sem):
    slab = lax.axis_index("slab")
    grp = lax.axis_index("grp")
    above = (slab + 1) % slabs
    below = (slab + slabs - 1) % slabs
    far_members = sorted(range(1, members), key=lambda r: -ring_steps(r, members))
    barrier = pltpu.get_barrier_semaphore()
    for r in far_members:
        pl.semaphore_signal(barrier, inc=1, device_id={"grp": (grp + r) % members}, device_id_type=MESH)
    for target in (above, below):
        pl.semaphore_signal(barrier, inc=1, device_id={"slab": target}, device_id_type=MESH)
    own = pltpu.make_async_copy(messages.at[grp], out.at[grp], own_sem)
    own.start()
    pl.semaphore_wait(barrier, members + 1)

    def near_copy(r):
        target = (grp + r) % members
        return pltpu.make_async_remote_copy(
            src_ref=messages.at[target], dst_ref=out.at[grp], send_sem=near_send.at[r], recv_sem=near_recv.at[r],
            device_id={"grp": target}, device_id_type=MESH,
        )

    def edge_copy(side):
        return pltpu.make_async_remote_copy(
            src_ref=messages.at[members + side], dst_ref=out.at[members + side],
            send_sem=edge_send.at[side], recv_sem=edge_recv.at[side],
            device_id={"slab": above if side == 0 else below}, device_id_type=MESH,
        )

    copies = [near_copy(r) for r in far_members] + [edge_copy(0), edge_copy(1)]
    for copy in copies:
        copy.start()
    own.wait()
    for copy in copies:
        copy.wait_recv()
    for copy in copies:
        copy.wait_send()


def field_call(slabs, members, messages):
    dma = pltpu.SemaphoreType.DMA
    out = pl.pallas_call(
        functools.partial(field_kernel, slabs, members),
        out_shape=jax.ShapeDtypeStruct((members + 2, 8, BLK), jnp.float32),
        in_specs=[ANY],
        out_specs=ANY,
        scratch_shapes=[dma((members,)), dma((members,)), dma((2,)), dma((2,)), dma],
        compiler_params=pltpu.CompilerParams(collective_id=1, has_side_effects=True),
    )(messages)
    return out.reshape(-1, BLK)


def shell_of(radius2):
    square = jnp.maximum(radius2, TINY)
    return jnp.maximum(1.0 - square * lax.rsqrt(square), 0.0)


def weight_of(shell):
    square = shell * shell
    return square * square * (1.25 - shell)


def write_lists(count, pairs, res, nb, out):
    left = pairs[0:1, :]
    right = pairs[1:2, :]
    lane = lax.broadcasted_iota(jnp.int32, (1, PAIR_MAX), 1)
    res_live = res[:, 7, :]
    nb_live = nb[:, 7, :]
    res_live = jnp.concatenate([res_live, res_live], 1)
    nb_live = jnp.concatenate([nb_live, nb_live], 1)
    hit = lax.broadcasted_iota(jnp.int32, (RES, PAIR_MAX), 0) == left
    live_left = jnp.sum(jnp.where(hit, res_live, 0.0), 0, keepdims=True)
    hit = lax.broadcasted_iota(jnp.int32, (NJ, PAIR_MAX), 0) == right
    live_right = jnp.sum(jnp.where(hit, nb_live, 0.0), 0, keepdims=True)
    valid = jnp.where(lane < count, live_right, 0.0)
    heavy = valid * live_left
    light = valid * (1.0 - live_left)
    before = lax.broadcasted_iota(jnp.int32, (PAIR_MAX, PAIR_MAX), 0) < lax.broadcasted_iota(
        jnp.int32, (PAIR_MAX, PAIR_MAX), 1
    )
    blank = jnp.zeros((6, PAIR_MAX), jnp.float32)
    kinds = jnp.concatenate([heavy, light, blank], 0).astype(jnp.bfloat16)
    spots = jnp.dot(kinds, jnp.where(before, 1.0, 0.0).astype(jnp.bfloat16), preferred_element_type=jnp.float32)
    names = jnp.concatenate([left.astype(jnp.float32), right.astype(jnp.float32), blank], 0).astype(jnp.bfloat16)
    row = lax.broadcasted_iota(jnp.int32, (PAIR_MAX, PAIR_MAX), 0).astype(jnp.float32)
    sums = jnp.sum(jnp.concatenate([heavy, light, blank], 0), 1, keepdims=True)
    for kind, member in ((0, heavy), (1, light)):
        target = jnp.where(member > 0.5, spots[kind : kind + 1, :], -1.0)
        chosen = jnp.where(row == target, 1.0, 0.0).astype(jnp.bfloat16)
        packed = lax.dot_general(names, chosen, (((1,), (1,)), ((), ())), preferred_element_type=jnp.float32)
        amount = jnp.broadcast_to(sums[kind : kind + 1, :], (1, PAIR_MAX))
        filled = lane.astype(jnp.float32) < amount
        out[2 * kind : 2 * kind + 1, :] = jnp.where(filled, packed[0:1, :], float(RES)).astype(jnp.int32)
        out[2 * kind + 1 : 2 * kind + 2, :] = packed[1:2, :].astype(jnp.int32)
        out[4 + kind : 5 + kind, :] = amount.astype(jnp.int32)
    out[6:8, :] = jnp.zeros((2, PAIR_MAX), jnp.int32)


def box_of(tiles):
    live = jnp.broadcast_to(tiles[:, 7:8, :], tiles.shape) > 0.5
    least = jnp.min(jnp.where(live, tiles * HALF, FAR), 0)
    most = jnp.max(jnp.where(live, tiles * HALF, -FAR), 0)
    return jnp.min(least, 1, keepdims=True), jnp.max(most, 1, keepdims=True)


def square_rows(tile, centre, own, other):
    row = lax.broadcasted_iota(jnp.int32, (8, BLK), 0)
    place = jnp.where(row < 3, tile * HALF - centre, 0.0)
    square = jnp.broadcast_to(jnp.sum(place * place, 0, keepdims=True), (8, BLK))
    high, mid, low = (p.astype(jnp.float32) for p in pieces(jnp.where(row == own, square, place)))
    return row < 3, jnp.where(row == other, 1.0, 0.0), high, mid, low


def write_squares(res, nb, centre, left, right, table):
    left[...] = jnp.zeros_like(left)
    row = lax.broadcasted_iota(jnp.int32, (SQUARE_ROWS, BLK), 0)
    spread = jnp.where((row == 5) | (row == 13) | (row == 21), 4.0, 0.0).astype(jnp.bfloat16)
    eight = lax.broadcasted_iota(jnp.int32, (8, BLK), 0)

    def columns(step, carry):
        for u in range(COLUMN_STEP):
            j = step * COLUMN_STEP + u
            tile = nb[j]
            place, one, high, mid, low = square_rows(tile, centre, 3, 4)
            mass = jnp.where(eight == 5, jnp.broadcast_to(tile[6:7, :], (8, BLK)), 0.0)
            masses = [m.astype(jnp.float32) for m in pieces(mass)]
            stacked = jnp.concatenate(
                [
                    high + one + masses[0],
                    jnp.where(place, high, mid) + one + masses[1],
                    jnp.where(place, mid, low) + one + masses[2],
                    jnp.where(place, mid, 0.0),
                    jnp.where(place, high, 0.0),
                    jnp.where(place, low, 0.0),
                ],
                0,
            )
            turned = jnp.transpose(stacked, (1, 0)).astype(jnp.bfloat16)
            left[j, :, 0:SQUARE_ROWS] = turned
            table[j, 3] = jnp.dot(turned, spread, preferred_element_type=jnp.float32)
        return carry

    lax.fori_loop(0, NJ // COLUMN_STEP, columns, 0)

    def rows(step, carry):
        for u in range(COLUMN_STEP):
            i = step * COLUMN_STEP + u
            place, one, high, mid, low = square_rows(res[i], centre, 4, 3)
            twice = jnp.where(place, -2.0, 1.0)
            high, mid, low = high * twice, mid * twice, low * twice
            stacked = jnp.concatenate(
                [
                    high + one,
                    mid + one,
                    jnp.where(place, high, low) + one,
                    jnp.where(place, mid, 0.0),
                    jnp.where(place, low, 0.0),
                    jnp.where(place, high, 0.0),
                ],
                0,
            )
            right[i] = stacked.astype(jnp.bfloat16)
        return carry

    lax.fori_loop(0, RES // COLUMN_STEP, rows, 0)


def pieces(value):
    high = value.astype(jnp.bfloat16)
    rest = value - high.astype(jnp.float32)
    mid = rest.astype(jnp.bfloat16)
    low = (rest - mid.astype(jnp.float32)).astype(jnp.bfloat16)
    return high, mid, low


def write_columns(nb, table, fields):
    count = len(fields)
    row = lax.broadcasted_iota(jnp.int32, (32, count * BLK), 0)
    spot = lax.broadcasted_iota(jnp.int32, (32, count * BLK), 1) // BLK
    spread = jnp.zeros((32, count * BLK), jnp.float32)
    for n, (field, scale) in enumerate(fields):
        mine = (row == field) | (row == 8 + field) | (row == 16 + field)
        spread = jnp.where((spot == n) & mine, scale, spread)
    spread = spread.astype(jnp.bfloat16)

    def some(step, carry):
        for u in range(COLUMN_STEP):
            j = step * COLUMN_STEP + u
            high, mid, low = (p.astype(jnp.float32) for p in pieces(nb[j]))
            stacked = jnp.concatenate([high, mid, low, jnp.zeros((8, BLK), jnp.float32)], 0)
            turned = jnp.transpose(stacked, (1, 0)).astype(jnp.bfloat16)
            wide = jnp.dot(turned, spread, preferred_element_type=jnp.float32)
            for n in range(count):
                table[j, n] = wide[:, n * BLK : (n + 1) * BLK]
        return carry

    lax.fori_loop(0, NJ // COLUMN_STEP, some, 0)


def pieces(value):
    high = value.astype(jnp.bfloat16)
    rest = value - high.astype(jnp.float32)
    mid = rest.astype(jnp.bfloat16)
    low = (rest - mid.astype(jnp.float32)).astype(jnp.bfloat16)
    return high, mid, low


def write_columns(nb, table, fields):
    count = len(fields)
    row = lax.broadcasted_iota(jnp.int32, (32, count * BLK), 0)
    spot = lax.broadcasted_iota(jnp.int32, (32, count * BLK), 1) // BLK
    spread = jnp.zeros((32, count * BLK), jnp.float32)
    for n, (field, scale) in enumerate(fields):
        mine = (row == field) | (row == 8 + field) | (row == 16 + field)
        spread = jnp.where((spot == n) & mine, scale, spread)
    spread = spread.astype(jnp.bfloat16)

    def some(step, carry):
        for u in range(COLUMN_STEP):
            j = step * COLUMN_STEP + u
            high, mid, low = (p.astype(jnp.float32) for p in pieces(nb[j]))
            stacked = jnp.concatenate([high, mid, low, jnp.zeros((8, BLK), jnp.float32)], 0)
            turned = jnp.transpose(stacked, (1, 0)).astype(jnp.bfloat16)
            wide = jnp.dot(turned, spread, preferred_element_type=jnp.float32)
            for n in range(count):
                table[j, n] = wide[:, n * BLK : (n + 1) * BLK]
        return carry

    lax.fori_loop(0, NJ // COLUMN_STEP, some, 0)


def density_kernel(
    count_in, pairs_in, names_in, res_in, nb_in, dens_out, field_out, list_out, message_out, shell_out,
    count, pairs, names, res, nb, table, acc, origin, held, left, right, first, second, lists, sem, held_sem,
):
    members = names.shape[0]
    fetches = [
        pltpu.make_async_copy(source, target, sem.at[n])
        for n, (source, target) in enumerate(
            ((nb_in, nb), (res_in, res), (pairs_in, pairs), (count_in, count), (names_in, names))
        )
    ]
    for fetch in fetches:
        fetch.start()
    for fetch in fetches:
        fetch.wait()
    write_lists(count[0], pairs, res, nb, list_out)
    least, most = box_of(nb[...])
    least_res, most_res = box_of(res[...])
    least, most = jnp.minimum(least, least_res), jnp.maximum(most, most_res)
    centre = jnp.broadcast_to(0.5 * least + 0.5 * most, (8, BLK))
    spread = jnp.max((most - least)[0:3], 0, keepdims=True)
    list_out[6:7, :] = jnp.broadcast_to(jnp.where(spread <= NARROW, 1, 0), (1, PAIR_MAX))
    copy = pltpu.make_async_copy(list_out, lists, sem.at[5])
    copy.start()
    x, y, z = (nb[:, f, :] * HALF for f in range(3))
    alone = jnp.sum(weight_of(shell_of(x * x + y * y + z * z)) * (4.0 * nb[:, 6, :]), 1, keepdims=True)
    origin[...] = jnp.zeros_like(origin)
    origin[:, 0, :] = jnp.broadcast_to(alone, (NJ, BLK))
    acc[...] = jnp.zeros_like(acc)
    copy.wait()
    steps = (lists[4, 0] + 2 * WIDE - 1) // (2 * WIDE)

    def shell_copy(step):
        rows = pl.ds(2 * WIDE * step, 2 * WIDE)
        return pltpu.make_async_copy(held.at[rows], shell_out.at[rows], held_sem.at[step])

    def whole(n, radius2_of):
        i = lists[0, n]
        j = lists[1, n]
        totals = [jnp.zeros((8, BLK), jnp.float32)] * 2
        for g in range(GROUPS):
            rows = pl.ds(8 * g, 8)
            shell = shell_of(radius2_of(i, j, rows))
            held[n, rows, :] = shell
            totals[g % 2] = totals[g % 2] + weight_of(shell) * table[j, 3, rows, :]
        acc[i] = acc[i] + (totals[0] + totals[1])

    @pl.when(lists[6, 0] == 1)
    def _():
        write_squares(res, nb, centre, left, right, table)

        def squares(n, into):
            for u in range(WIDE):
                m = jnp.minimum(n + u, PAIR_MAX - 1)
                own = jnp.minimum(lists[0, m], RES - 1)
                columns = left[lists[1, m], :, 0:SQUARE_ROWS]
                into[u] = jnp.dot(columns, right[own], preferred_element_type=jnp.float32)

        def step_of(step, carry):
            n = 2 * WIDE * step
            squares(n + WIDE, second)
            for u in range(WIDE):
                whole(n + u, lambda i, j, rows: first[u, rows, :])
            squares(n + 2 * WIDE, first)
            for u in range(WIDE):
                whole(n + WIDE + u, lambda i, j, rows: second[u, rows, :])
            shell_copy(step).start()
            return carry

        squares(0, first)
        lax.fori_loop(0, steps, step_of, 0)

    @pl.when(lists[6, 0] == 0)
    def _():
        write_columns(nb, table, ((0, HALF), (1, HALF), (2, HALF), (6, 4.0)))

        def direct(i, j, rows):
            own = jnp.minimum(i, RES - 1)
            dx, dy, dz = (res[own, f : f + 1, :] * HALF - table[j, f, rows, :] for f in range(3))
            return dx * dx + dy * dy + dz * dz

        def step_of(step, carry):
            def part(quarter, carry):
                for u in range(STEP):
                    whole(2 * WIDE * step + STEP * quarter + u, direct)
                return carry

            lax.fori_loop(0, 2 * WIDE // STEP, part, 0)
            shell_copy(step).start()
            return carry

        lax.fori_loop(0, steps, step_of, 0)

    def blank(step, carry):
        for u in range(STEP):
            i = lists[2, STEP * step + u]
            acc[i] = acc[i] + origin[lists[3, STEP * step + u]]
        return carry

    lax.fori_loop(0, (lists[5, 0] + STEP - 1) // STEP, blank, 0)
    dens = jnp.sum(acc[0:RES], 1) * KERNEL_NORM
    dens_out[...] = dens
    inverse = 1.0 / jnp.maximum(dens, DENS_FLOOR)
    cube = dens * dens * dens
    field_out[:, 0, :] = STIFF * (cube * cube * dens - 1.0) * inverse * inverse
    field_out[:, 1, :] = res[:, 6, :] * inverse
    for d in range(members):
        for k in range(NEED):
            message_out[d, 2 * k : 2 * k + 2, :] = field_out[names[d, 0, k]]
    for k in range(GH):
        message_out[members, 2 * k : 2 * k + 2, :] = field_out[NSTAY - GH + k]
        message_out[members + 1, 2 * k : 2 * k + 2, :] = field_out[k]

    def settle(step, carry):
        shell_copy(step).wait()
        return carry

    lax.fori_loop(0, steps, settle, 0)


def two_pieces(value):
    high = value.astype(jnp.bfloat16)
    return high, (value - high.astype(jnp.float32)).astype(jnp.bfloat16)


def write_factors(nb, far, press, damp, centre):
    row = lax.broadcasted_iota(jnp.int32, (8, BLK), 0)
    upper = row < 3
    lower = (row >= 3) & (row < 6)

    def store(ref, j, tiles):
        for h in range(0, len(tiles), 2):
            pair = jnp.concatenate([tiles[h].astype(jnp.float32), tiles[h + 1].astype(jnp.float32)], 0)
            pair = pair.astype(jnp.bfloat16)
            rows = pl.ds(8 * h, 16)
            ref[j, rows, 0:BLK] = pair
            ref[j, rows, BLK : 2 * BLK] = pair

    def some(step, carry):
        for u in range(FACTOR_STEP):
            j = step * FACTOR_STEP + u
            tile = nb[j]
            mass = jnp.broadcast_to(tile[6:7, :], (8, BLK))
            scaled = tile * HALF
            middle = jnp.where(upper, jnp.broadcast_to(scaled[:, 0:1], (8, BLK)), 0.0)
            centre[j] = middle
            place = scaled - middle
            mass_q = mass * jnp.broadcast_to(far[pl.ds(2 * j, 1), :], (8, BLK))
            mass_s = mass * jnp.broadcast_to(far[pl.ds(2 * j + 1, 1), :], (8, BLK))
            first = jnp.where(upper, mass * place, jnp.where(row == 6, mass, jnp.where(row == 7, mass_q, 0.0)))
            second = jnp.where(upper, mass_q * place, 0.0)
            third = jnp.where(lower, mass_s * tile, jnp.where(row == 6, mass_s, 0.0))
            store(press, j, [p for both in zip(pieces(first), pieces(second)) for p in both])
            store(damp, j, [*pieces(third), jnp.zeros((8, BLK), jnp.bfloat16)])
        return carry

    lax.fori_loop(0, NJ // FACTOR_STEP, some, 0)


def force_kernel(
    lists_in, shells, res_in, nb_in, field_in, far_in, flag_in, out,
    lists, res, nb, field, far, flag, held, acc, origin, press, damp, centre, cubes, damps, sem, fetch_sem,
):
    fetches = [
        pltpu.make_async_copy(source, target, fetch_sem.at[n])
        for n, (source, target) in enumerate(
            ((lists_in, lists), (nb_in, nb), (far_in, far), (res_in, res), (field_in, field), (flag_in, flag))
        )
    ]
    for fetch in fetches:
        fetch.start()
    fetches[0].wait()
    steps = (lists[4, 0] + WIDE - 1) // WIDE

    def shell_copy(step):
        rows = pl.ds(WIDE * step, WIDE)
        return pltpu.make_async_copy(shells.at[rows], held.at[rows], sem.at[step])

    def fetch(step, carry):
        shell_copy(step).start()
        return carry

    lax.fori_loop(0, steps, fetch, 0)
    fetches[1].wait()
    fetches[2].wait()
    write_factors(nb, far, press, damp, centre)
    acc[...] = jnp.zeros_like(acc)
    row = lax.broadcasted_iota(jnp.int32, (8, BLK), 0)
    upper = row < 3
    lower = (row >= 3) & (row < 6)
    scale = jnp.where(upper, HALF, 1.0)

    x, y, z = (nb[:, f, :] * HALF for f in range(3))
    radius2 = x * x + y * y + z * z
    shell = shell_of(radius2)
    cube = shell * shell * shell * nb[:, 6, :]
    drag = cube * radius2 / (radius2 + SOFT) * far[pl.ds(1, NJ, stride=2), :]
    push = cube * far[pl.ds(0, NJ, stride=2), :]
    origin[...] = jnp.zeros_like(origin)
    for f, place in enumerate((x, y, z)):
        origin[:, f, :] = jnp.broadcast_to(jnp.sum(cube * place, 1, keepdims=True), (NJ, BLK))
        origin[:, 8 + f, :] = jnp.broadcast_to(jnp.sum(push * place, 1, keepdims=True), (NJ, BLK))
        origin[:, 3 + f, :] = jnp.broadcast_to(jnp.sum(drag * nb[:, 3 + f, :], 1, keepdims=True), (NJ, BLK))

    def coefficients(i):
        q = jnp.broadcast_to(field[i, 0:1, :], (8, BLK))
        s = jnp.broadcast_to(field[i, 1:2, :], (8, BLK))
        return jnp.where(upper, q, jnp.where(lower, s, 0.0))

    def geometry(u, n):
        for g in range(GROUPS // 2):
            rows = pl.ds(16 * g, 16)
            shell = held[n, rows, :]
            ratio = 1.0 - shell
            radius2 = ratio * ratio
            cube = shell * shell * shell
            soft = lax.rsqrt(radius2 + SOFT)
            high, low = two_pieces(cube)
            cubes[u, rows, :] = high
            cubes[u, pl.ds(BLK + 16 * g, 16), :] = low
            high, low = two_pieces(cube * (radius2 * (soft * soft)))
            damps[u, rows, :] = high
            damps[u, pl.ds(BLK + 16 * g, 16), :] = low

    def sums_of(u, j):
        first = jnp.dot(press[j], cubes[u], preferred_element_type=jnp.float32)
        second = jnp.dot(damp[j], damps[u], preferred_element_type=jnp.float32)
        return first[0:16] + (first[16:32] + first[32:48]), second[0:8] + (second[8:16] + second[16:24])

    def whole(step, before):
        @pl.when(step < steps)
        def _():
            shell_copy(step).wait()

        sums = [sums_of(u, j) for u, (i, j) in enumerate(before)]
        after = []
        for u in range(WIDE):
            n = jnp.minimum(WIDE * step + u, PAIR_MAX - 1)
            geometry(u, n)
            after.append((lists[0, n], lists[1, n]))
        for u, (i, j) in enumerate(before):
            own = jnp.minimum(i, RES - 1)
            first, second = sums[u]
            place = res[own] * scale - centre[j]
            one, two = first[0:8], first[8:16]
            both = jnp.where(upper, jnp.broadcast_to(one[6:7], (8, BLK)), jnp.broadcast_to(second[6:7], (8, BLK)))
            only = jnp.where(upper, jnp.broadcast_to(one[7:8], (8, BLK)), 0.0)
            part = coefficients(own) * (place * both - (one + second)) + (place * only - two)
            acc[i] = acc[i] + part
        return tuple(after)

    for copy in fetches[3:]:
        copy.wait()
    nowhere = tuple((jnp.int32(RES), jnp.int32(0)) for _ in range(WIDE))
    lax.fori_loop(0, steps + 1, whole, nowhere)

    def blank(step, carry):
        for u in range(STEP):
            i = lists[2, STEP * step + u]
            j = lists[3, STEP * step + u]
            own = jnp.minimum(i, RES - 1)
            acc[i] = acc[i] - (coefficients(own) * origin[j, 0:8, :] + origin[j, 8:16, :])
        return carry

    lax.fori_loop(0, (lists[5, 0] + STEP - 1) // STEP, blank, 0)
    gravity = jnp.where(lax.broadcasted_iota(jnp.int32, (3, BLK), 0) == 2, -GRAVITY, 0.0)
    for b in range(RES):
        total = acc[b, 0:3, :] * PRESS_SCALE + acc[b, 3:6, :] * VISC_SCALE + gravity
        if b < NSTAY:
            total = total * (1.0 - flag[b : b + 1, :].astype(jnp.float32))
        out[:, b * BLK : (b + 1) * BLK] = total


def density_call(count, pairs, names, resident, neighbour):
    members = names.shape[0]
    return pl.pallas_call(
        density_kernel,
        out_shape=(
            jax.ShapeDtypeStruct((RES, BLK), jnp.float32),
            jax.ShapeDtypeStruct((RES, 2, BLK), jnp.float32),
            jax.ShapeDtypeStruct((8, PAIR_MAX), jnp.int32),
            jax.ShapeDtypeStruct((members + 2, 8, BLK), jnp.float32),
            jax.ShapeDtypeStruct((PAIR_MAX, BLK, BLK), jnp.float32),
        ),
        in_specs=[ANY] * 5,
        out_specs=(VMEM, VMEM, VMEM, VMEM, ANY),
        scratch_shapes=[
            pltpu.SMEM(count.shape, jnp.int32),
            pltpu.VMEM(pairs.shape, jnp.int32),
            pltpu.SMEM(names.shape, jnp.int32),
            pltpu.VMEM(resident.shape, jnp.float32),
            pltpu.VMEM(neighbour.shape, jnp.float32),
            pltpu.VMEM((NJ, 4, BLK, BLK), jnp.float32),
            pltpu.VMEM((RES + 1, 8, BLK), jnp.float32),
            pltpu.VMEM((NJ, 8, BLK), jnp.float32),
            pltpu.VMEM((PAIR_MAX, BLK, BLK), jnp.float32),
            pltpu.VMEM((NJ, BLK, BLK), jnp.bfloat16),
            pltpu.VMEM((RES, SQUARE_ROWS, BLK), jnp.bfloat16),
            pltpu.VMEM((WIDE, BLK, BLK), jnp.float32),
            pltpu.VMEM((WIDE, BLK, BLK), jnp.float32),
            pltpu.SMEM((8, PAIR_MAX), jnp.int32),
            pltpu.SemaphoreType.DMA((6,)),
            pltpu.SemaphoreType.DMA((PAIR_MAX // (2 * WIDE),)),
        ],
        compiler_params=pltpu.CompilerParams(vmem_limit_bytes=LIMIT),
    )(count, pairs, names, resident, neighbour)


def force_call(lists, shells, resident, neighbour, field, far, flag):
    return pl.pallas_call(
        force_kernel,
        out_shape=jax.ShapeDtypeStruct((3, RES * BLK), jnp.float32),
        in_specs=[ANY] * 7,
        out_specs=VMEM,
        scratch_shapes=[
            pltpu.SMEM(lists.shape, jnp.int32),
            pltpu.VMEM(resident.shape, jnp.float32),
            pltpu.VMEM(neighbour.shape, jnp.float32),
            pltpu.VMEM(field.shape, jnp.float32),
            pltpu.VMEM(far.shape, jnp.float32),
            pltpu.VMEM(flag.shape, jnp.int32),
            pltpu.VMEM((PAIR_MAX, BLK, BLK), jnp.float32),
            pltpu.VMEM((RES + 1, 8, BLK), jnp.float32),
            pltpu.VMEM((NJ, 16, BLK), jnp.float32),
            pltpu.VMEM((NJ, 48, 2 * BLK), jnp.bfloat16),
            pltpu.VMEM((NJ, 32, 2 * BLK), jnp.bfloat16),
            pltpu.VMEM((NJ, 8, BLK), jnp.float32),
            pltpu.VMEM((WIDE, 2 * BLK, BLK), jnp.bfloat16),
            pltpu.VMEM((WIDE, 2 * BLK, BLK), jnp.bfloat16),
            pltpu.SemaphoreType.DMA((PAIR_MAX // WIDE,)),
            pltpu.SemaphoreType.DMA((6,)),
        ],
        compiler_params=pltpu.CompilerParams(vmem_limit_bytes=LIMIT),
    )(lists, shells, resident, neighbour, field, far, flag)


def on_device(stay, leave, stay_flag, send_list, send_count, wanted, pair_tiles, pair_count):
    slabs = send_list.shape[1]
    members = wanted.shape[1]
    leaving = leave.reshape(7, slabs * SM, BLK).transpose(1, 0, 2)
    staying = stay.reshape(7, NSTAY, BLK).transpose(1, 0, 2)
    resident, neighbour, asked = migrate_call(
        slabs, members, send_list.transpose(0, 2, 1), send_count, wanted.transpose(0, 2, 1), leaving, staying
    )
    dens, field, lists, messages, shells = density_call(pair_count, pair_tiles[0], asked, resident, neighbour)
    far = field_call(slabs, members, messages)
    accel = force_call(lists, shells, resident, neighbour, field, far, stay_flag.reshape(NSTAY, BLK))
    return (dens.reshape(-1), accel)


def solution(mesh):
    in_specs = (
        P(None, ("slab", "grp")),
        P(None, ("slab", "grp")),
        P(("slab", "grp")),
        P(("slab", "grp"), None, None),
        P(("slab", "grp"), None),
        P(("slab", "grp"), None, None),
        P(("slab", "grp"), None, None),
        P(("slab", "grp")),
    )
    out_specs = (P(("slab", "grp")), P(None, ("slab", "grp")))
    return jax.shard_map(
        on_device, mesh=mesh, in_specs=in_specs, out_specs=out_specs, check_vma=False
    )
```

```python
import functools
import math

import jax
import jax.numpy as jnp
from jax import lax
from jax.experimental import pallas as pl
from jax.experimental.pallas import tpu as pltpu
from jax.sharding import PartitionSpec as P

BLK = 128
SM = 2
GH = 4
NEED = 4
PAIR_MAX = 256
NSTAY = 16
RES = 80
NJ = 40
GROUPS = BLK // 8
COLUMN_STEP = 8
SQUARE_STEP = 40
STEP = 4
WIDE = 8
NARROW = 6.0
SQUARE_ROWS = 48
FACTOR_STEP = 20

KERNEL_NORM = 21.0 / (16.0 * math.pi)
SMOOTH = 1.0
HALF = 0.5 / SMOOTH
DENS_FLOOR = 0.5
STIFF = 0.02
VISCOUS = 0.1
GRAVITY = 1.0
TINY = 1e-30
FAR = 3e38
SOFT = 0.01 * HALF * HALF
PRESS_SCALE = 5.0 * KERNEL_NORM / (SMOOTH * SMOOTH) / HALF
VISC_SCALE = -VISCOUS * 5.0 * KERNEL_NORM / (SMOOTH * SMOOTH)

VMEM = pl.BlockSpec(memory_space=pltpu.VMEM)
SMEM = pl.BlockSpec(memory_space=pltpu.SMEM)
ANY = pl.BlockSpec(memory_space=pl.ANY)
MESH = pl.DeviceIdType.MESH
LIMIT = 56 * 1024 * 1024


def ring_steps(r, size):
    return min(r, size - r)


def migrate_kernel(
    slabs, members, lists_in, counts_in, wanted_in, leave, stay,
    res_out, nb_out, asked_out,
    lists, counts, wanted, leaving, staying, packed, res, nb, request, asked, names, chosen,
    row_send, row_recv, ghost_send, ghost_recv, name_send, name_recv, near_send, near_recv, local_sem,
):
    slab = lax.axis_index("slab")
    grp = lax.axis_index("grp")
    ghosts = members * NEED
    barrier = pltpu.get_barrier_semaphore()

    far_slabs = sorted(range(1, slabs), key=lambda r: -ring_steps(r // 8, 4) - ring_steps(r // 2 % 4, 4))
    far_members = sorted(range(1, members), key=lambda r: -ring_steps(r, members))
    for r in far_members:
        pl.semaphore_signal(barrier, inc=1, device_id={"grp": (grp + r) % members}, device_id_type=MESH)
    for r in far_slabs:
        pl.semaphore_signal(barrier, inc=1, device_id={"slab": (slab + r) % slabs}, device_id_type=MESH)
    fetch_leave = pltpu.make_async_copy(leave, leaving, local_sem.at[0])
    fetch_stay = pltpu.make_async_copy(stay, staying, local_sem.at[1])
    fetch_leave.start()
    fetch_stay.start()
    small = [
        pltpu.make_async_copy(source, target, local_sem.at[5 + n])
        for n, (source, target) in enumerate(((wanted_in, wanted), (lists_in, lists), (counts_in, counts)))
    ]
    for copy in small:
        copy.start()
    for copy in small:
        copy.wait()
    lane = lax.broadcasted_iota(jnp.int32, (1, BLK), 1)
    for p in range(members):
        ask = jnp.zeros((1, BLK), jnp.int32)
        for k in range(NEED):
            ask = jnp.where(lane == k, wanted[0, k, p], ask)
        request[p] = ask
    fetch_stay.wait()
    for b in range(NSTAY):
        res[b, 0:7, :] = staying[b]
        res[b, 7:8, :] = jnp.ones((1, BLK), jnp.float32)
    fetch_leave.wait()
    for t in range(slabs):
        count = counts[0, t]
        for k in range(SM):
            keep = jnp.broadcast_to(jnp.minimum(jnp.maximum(count - k, 0), 1), (1, BLK)).astype(jnp.float32)
            packed[t * SM + k, 0:7, :] = leaving[lists[0, k, t]] * keep
            packed[t * SM + k, 7:8, :] = keep
    pl.semaphore_wait(barrier, slabs - 1 + members - 1)

    def name_copy(r):
        target = (grp + r) % members
        return pltpu.make_async_remote_copy(
            src_ref=request.at[target], dst_ref=asked.at[grp], send_sem=name_send.at[r], recv_sem=name_recv.at[r],
            device_id={"grp": target}, device_id_type=MESH,
        )

    def row_copy(r):
        target = (slab + r) % slabs
        return pltpu.make_async_remote_copy(
            src_ref=packed.at[pl.ds(target * SM, SM)], dst_ref=res.at[pl.ds(NSTAY + slab * SM, SM)],
            send_sem=row_send.at[r], recv_sem=row_recv.at[r],
            device_id={"slab": target}, device_id_type=MESH,
        )

    def ghost_copy(side):
        first = NSTAY - GH if side == 0 else 0
        target = (slab + (1 if side == 0 else slabs - 1)) % slabs
        return pltpu.make_async_remote_copy(
            src_ref=res.at[pl.ds(first, GH)], dst_ref=nb.at[pl.ds(ghosts + side * GH, GH)],
            send_sem=ghost_send.at[side], recv_sem=ghost_recv.at[side],
            device_id={"slab": target}, device_id_type=MESH,
        )

    def near_copy(r):
        target = (grp + r) % members
        return pltpu.make_async_remote_copy(
            src_ref=chosen.at[target], dst_ref=nb.at[pl.ds(grp * NEED, NEED)],
            send_sem=near_send.at[r], recv_sem=near_recv.at[r],
            device_id={"grp": target}, device_id_type=MESH,
        )

    def each(order, step):
        for r in order:
            step(r)

    each(far_members, lambda r: name_copy(r).start())
    each(far_slabs, lambda r: row_copy(r).start())
    ghost_copy(0).start()
    ghost_copy(1).start()
    asked[grp] = request[grp]
    mine = pl.ds(NSTAY + slab * SM, SM)
    res[mine] = packed[pl.ds(slab * SM, SM)]
    each(far_members, lambda r: name_copy(r).wait_recv())
    local = pltpu.make_async_copy(asked, names, local_sem.at[2])
    local.start()
    local.wait()
    asked_out[...] = asked[...]
    each(far_slabs, lambda r: row_copy(r).wait_recv())
    for d in range(members):
        for k in range(NEED):
            chosen[d, k] = res[names[d, 0, k]]
    each(far_members, lambda r: near_copy(r).start())
    nb[pl.ds(grp * NEED, NEED)] = chosen[grp]
    store_res = pltpu.make_async_copy(res, res_out, local_sem.at[3])
    store_res.start()
    ghost_copy(0).wait_recv()
    ghost_copy(1).wait_recv()
    for side, some in ((0, slab > 0), (1, slab < slabs - 1)):
        rows = pl.ds(ghosts + side * GH, GH)
        nb[rows] = nb[rows] * some.astype(jnp.float32)
    each(far_members, lambda r: near_copy(r).wait_recv())
    store_nb = pltpu.make_async_copy(nb, nb_out, local_sem.at[4])
    store_nb.start()
    each(far_members, lambda r: name_copy(r).wait_send())
    each(far_slabs, lambda r: row_copy(r).wait_send())
    each(far_members, lambda r: near_copy(r).wait_send())
    ghost_copy(0).wait_send()
    ghost_copy(1).wait_send()
    store_res.wait()
    store_nb.wait()


def migrate_call(slabs, members, lists, counts, wanted, leave, stay):
    blocks = NSTAY + slabs * SM
    near = members * NEED + 2 * GH
    f32 = jnp.float32
    dma = pltpu.SemaphoreType.DMA
    return pl.pallas_call(
        functools.partial(migrate_kernel, slabs, members),
        out_shape=(
            jax.ShapeDtypeStruct((blocks, 8, BLK), f32),
            jax.ShapeDtypeStruct((near, 8, BLK), f32),
            jax.ShapeDtypeStruct((members, 1, BLK), jnp.int32),
        ),
        in_specs=[ANY, ANY, ANY, ANY, ANY],
        out_specs=(ANY, ANY, VMEM),
        scratch_shapes=[
            pltpu.SMEM(lists.shape, jnp.int32),
            pltpu.SMEM(counts.shape, jnp.int32),
            pltpu.SMEM(wanted.shape, jnp.int32),
            pltpu.VMEM(leave.shape, f32),
            pltpu.VMEM(stay.shape, f32),
            pltpu.VMEM((slabs * SM, 8, BLK), f32),
            pltpu.VMEM((blocks, 8, BLK), f32),
            pltpu.VMEM((near, 8, BLK), f32),
            pltpu.VMEM((members, 1, BLK), jnp.int32),
            pltpu.VMEM((members, 1, BLK), jnp.int32),
            pltpu.SMEM((members, 1, BLK), jnp.int32),
            pltpu.VMEM((members, NEED, 8, BLK), f32),
            dma((slabs,)), dma((slabs,)), dma((2,)), dma((2,)),
            dma((members,)), dma((members,)), dma((members,)), dma((members,)), dma((8,)),
        ],
        compiler_params=pltpu.CompilerParams(collective_id=0, has_side_effects=True, vmem_limit_bytes=LIMIT),
    )(lists, counts, wanted, leave, stay)


def field_kernel(slabs, members, messages, out, near_send, near_recv, edge_send, edge_recv, own_sem):
    slab = lax.axis_index("slab")
    grp = lax.axis_index("grp")
    above = (slab + 1) % slabs
    below = (slab + slabs - 1) % slabs
    far_members = sorted(range(1, members), key=lambda r: -ring_steps(r, members))
    barrier = pltpu.get_barrier_semaphore()
    for r in far_members:
        pl.semaphore_signal(barrier, inc=1, device_id={"grp": (grp + r) % members}, device_id_type=MESH)
    for target in (above, below):
        pl.semaphore_signal(barrier, inc=1, device_id={"slab": target}, device_id_type=MESH)
    own = pltpu.make_async_copy(messages.at[grp], out.at[grp], own_sem)
    own.start()
    pl.semaphore_wait(barrier, members + 1)

    def near_copy(r):
        target = (grp + r) % members
        return pltpu.make_async_remote_copy(
            src_ref=messages.at[target], dst_ref=out.at[grp], send_sem=near_send.at[r], recv_sem=near_recv.at[r],
            device_id={"grp": target}, device_id_type=MESH,
        )

    def edge_copy(side):
        return pltpu.make_async_remote_copy(
            src_ref=messages.at[members + side], dst_ref=out.at[members + side],
            send_sem=edge_send.at[side], recv_sem=edge_recv.at[side],
            device_id={"slab": above if side == 0 else below}, device_id_type=MESH,
        )

    copies = [near_copy(r) for r in far_members] + [edge_copy(0), edge_copy(1)]
    for copy in copies:
        copy.start()
    own.wait()
    for copy in copies:
        copy.wait_recv()
    for copy in copies:
        copy.wait_send()


def field_call(slabs, members, messages):
    dma = pltpu.SemaphoreType.DMA
    out = pl.pallas_call(
        functools.partial(field_kernel, slabs, members),
        out_shape=jax.ShapeDtypeStruct((members + 2, 8, BLK), jnp.float32),
        in_specs=[ANY],
        out_specs=ANY,
        scratch_shapes=[dma((members,)), dma((members,)), dma((2,)), dma((2,)), dma],
        compiler_params=pltpu.CompilerParams(collective_id=1, has_side_effects=True),
    )(messages)
    return out.reshape(-1, BLK)


def shell_of(radius2):
    square = jnp.maximum(radius2, TINY)
    return jnp.maximum(1.0 - square * lax.rsqrt(square), 0.0)


def weight_of(shell):
    square = shell * shell
    return square * square * (1.25 - shell)


def write_lists(count, pairs, res, nb, out):
    left = pairs[0:1, :]
    right = pairs[1:2, :]
    lane = lax.broadcasted_iota(jnp.int32, (1, PAIR_MAX), 1)
    res_live = res[:, 7, :]
    nb_live = nb[:, 7, :]
    res_live = jnp.concatenate([res_live, res_live], 1)
    nb_live = jnp.concatenate([nb_live, nb_live], 1)
    hit = lax.broadcasted_iota(jnp.int32, (RES, PAIR_MAX), 0) == left
    live_left = jnp.sum(jnp.where(hit, res_live, 0.0), 0, keepdims=True)
    hit = lax.broadcasted_iota(jnp.int32, (NJ, PAIR_MAX), 0) == right
    live_right = jnp.sum(jnp.where(hit, nb_live, 0.0), 0, keepdims=True)
    valid = jnp.where(lane < count, live_right, 0.0)
    heavy = valid * live_left
    light = valid * (1.0 - live_left)
    before = lax.broadcasted_iota(jnp.int32, (PAIR_MAX, PAIR_MAX), 0) < lax.broadcasted_iota(
        jnp.int32, (PAIR_MAX, PAIR_MAX), 1
    )
    blank = jnp.zeros((6, PAIR_MAX), jnp.float32)
    kinds = jnp.concatenate([heavy, light, blank], 0).astype(jnp.bfloat16)
    spots = jnp.dot(kinds, jnp.where(before, 1.0, 0.0).astype(jnp.bfloat16), preferred_element_type=jnp.float32)
    names = jnp.concatenate([left.astype(jnp.float32), right.astype(jnp.float32), blank], 0).astype(jnp.bfloat16)
    row = lax.broadcasted_iota(jnp.int32, (PAIR_MAX, PAIR_MAX), 0).astype(jnp.float32)
    sums = jnp.sum(jnp.concatenate([heavy, light, blank], 0), 1, keepdims=True)
    for kind, member in ((0, heavy), (1, light)):
        target = jnp.where(member > 0.5, spots[kind : kind + 1, :], -1.0)
        chosen = jnp.where(row == target, 1.0, 0.0).astype(jnp.bfloat16)
        packed = lax.dot_general(names, chosen, (((1,), (1,)), ((), ())), preferred_element_type=jnp.float32)
        amount = jnp.broadcast_to(sums[kind : kind + 1, :], (1, PAIR_MAX))
        filled = lane.astype(jnp.float32) < amount
        out[2 * kind : 2 * kind + 1, :] = jnp.where(filled, packed[0:1, :], float(RES)).astype(jnp.int32)
        out[2 * kind + 1 : 2 * kind + 2, :] = packed[1:2, :].astype(jnp.int32)
        out[4 + kind : 5 + kind, :] = amount.astype(jnp.int32)
    out[6:8, :] = jnp.zeros((2, PAIR_MAX), jnp.int32)


def box_of(tiles):
    live = jnp.broadcast_to(tiles[:, 7:8, :], tiles.shape) > 0.5
    least = jnp.min(jnp.where(live, tiles * HALF, FAR), 0)
    most = jnp.max(jnp.where(live, tiles * HALF, -FAR), 0)
    return jnp.min(least, 1, keepdims=True), jnp.max(most, 1, keepdims=True)


def square_rows(tile, centre, own, other):
    row = lax.broadcasted_iota(jnp.int32, (8, BLK), 0)
    place = jnp.where(row < 3, tile * HALF - centre, 0.0)
    square = jnp.broadcast_to(jnp.sum(place * place, 0, keepdims=True), (8, BLK))
    high, mid, low = (p.astype(jnp.float32) for p in pieces(jnp.where(row == own, square, place)))
    return row < 3, jnp.where(row == other, 1.0, 0.0), high, mid, low


def write_squares(res, nb, centre, left, right, table):
    left[...] = jnp.zeros_like(left)
    row = lax.broadcasted_iota(jnp.int32, (SQUARE_ROWS, BLK), 0)
    spread = jnp.where((row == 5) | (row == 13) | (row == 21), 4.0, 0.0).astype(jnp.bfloat16)
    eight = lax.broadcasted_iota(jnp.int32, (8, BLK), 0)

    def columns(step, carry):
        for u in range(SQUARE_STEP):
            j = step * SQUARE_STEP + u
            tile = nb[j]
            place, one, high, mid, low = square_rows(tile, centre, 3, 4)
            mass = jnp.where(eight == 5, jnp.broadcast_to(tile[6:7, :], (8, BLK)), 0.0)
            masses = [m.astype(jnp.float32) for m in pieces(mass)]
            stacked = jnp.concatenate(
                [
                    high + one + masses[0],
                    jnp.where(place, high, mid) + one + masses[1],
                    jnp.where(place, mid, low) + one + masses[2],
                    jnp.where(place, mid, 0.0),
                    jnp.where(place, high, 0.0),
                    jnp.where(place, low, 0.0),
                ],
                0,
            )
            turned = jnp.transpose(stacked, (1, 0)).astype(jnp.bfloat16)
            left[j, :, 0:SQUARE_ROWS] = turned
            table[j, 3] = jnp.dot(turned, spread, preferred_element_type=jnp.float32)
        return carry

    lax.fori_loop(0, NJ // SQUARE_STEP, columns, 0)

    def rows(step, carry):
        for u in range(SQUARE_STEP):
            i = step * SQUARE_STEP + u
            place, one, high, mid, low = square_rows(res[i], centre, 4, 3)
            twice = jnp.where(place, -2.0, 1.0)
            high, mid, low = high * twice, mid * twice, low * twice
            stacked = jnp.concatenate(
                [
                    high + one,
                    mid + one,
                    jnp.where(place, high, low) + one,
                    jnp.where(place, mid, 0.0),
                    jnp.where(place, low, 0.0),
                    jnp.where(place, high, 0.0),
                ],
                0,
            )
            right[i] = stacked.astype(jnp.bfloat16)
        return carry

    lax.fori_loop(0, RES // SQUARE_STEP, rows, 0)


def pieces(value):
    high = value.astype(jnp.bfloat16)
    rest = value - high.astype(jnp.float32)
    mid = rest.astype(jnp.bfloat16)
    low = (rest - mid.astype(jnp.float32)).astype(jnp.bfloat16)
    return high, mid, low


def write_columns(nb, table, fields):
    count = len(fields)
    row = lax.broadcasted_iota(jnp.int32, (32, count * BLK), 0)
    spot = lax.broadcasted_iota(jnp.int32, (32, count * BLK), 1) // BLK
    spread = jnp.zeros((32, count * BLK), jnp.float32)
    for n, (field, scale) in enumerate(fields):
        mine = (row == field) | (row == 8 + field) | (row == 16 + field)
        spread = jnp.where((spot == n) & mine, scale, spread)
    spread = spread.astype(jnp.bfloat16)

    def some(step, carry):
        for u in range(COLUMN_STEP):
            j = step * COLUMN_STEP + u
            high, mid, low = (p.astype(jnp.float32) for p in pieces(nb[j]))
            stacked = jnp.concatenate([high, mid, low, jnp.zeros((8, BLK), jnp.float32)], 0)
            turned = jnp.transpose(stacked, (1, 0)).astype(jnp.bfloat16)
            wide = jnp.dot(turned, spread, preferred_element_type=jnp.float32)
            for n in range(count):
                table[j, n] = wide[:, n * BLK : (n + 1) * BLK]
        return carry

    lax.fori_loop(0, NJ // COLUMN_STEP, some, 0)


def pieces(value):
    high = value.astype(jnp.bfloat16)
    rest = value - high.astype(jnp.float32)
    mid = rest.astype(jnp.bfloat16)
    low = (rest - mid.astype(jnp.float32)).astype(jnp.bfloat16)
    return high, mid, low


def write_columns(nb, table, fields):
    count = len(fields)
    row = lax.broadcasted_iota(jnp.int32, (32, count * BLK), 0)
    spot = lax.broadcasted_iota(jnp.int32, (32, count * BLK), 1) // BLK
    spread = jnp.zeros((32, count * BLK), jnp.float32)
    for n, (field, scale) in enumerate(fields):
        mine = (row == field) | (row == 8 + field) | (row == 16 + field)
        spread = jnp.where((spot == n) & mine, scale, spread)
    spread = spread.astype(jnp.bfloat16)

    def some(step, carry):
        for u in range(COLUMN_STEP):
            j = step * COLUMN_STEP + u
            high, mid, low = (p.astype(jnp.float32) for p in pieces(nb[j]))
            stacked = jnp.concatenate([high, mid, low, jnp.zeros((8, BLK), jnp.float32)], 0)
            turned = jnp.transpose(stacked, (1, 0)).astype(jnp.bfloat16)
            wide = jnp.dot(turned, spread, preferred_element_type=jnp.float32)
            for n in range(count):
                table[j, n] = wide[:, n * BLK : (n + 1) * BLK]
        return carry

    lax.fori_loop(0, NJ // COLUMN_STEP, some, 0)


def density_kernel(
    count_in, pairs_in, names_in, res_in, nb_in, dens_out, field_out, list_out, message_out, shell_out,
    count, pairs, names, res, nb, table, acc, origin, held, left, right, first, second, lists, sem, held_sem,
):
    members = names.shape[0]
    fetches = [
        pltpu.make_async_copy(source, target, sem.at[n])
        for n, (source, target) in enumerate(
            ((nb_in, nb), (res_in, res), (pairs_in, pairs), (count_in, count), (names_in, names))
        )
    ]
    for fetch in fetches:
        fetch.start()
    for fetch in fetches:
        fetch.wait()
    write_lists(count[0], pairs, res, nb, list_out)
    least, most = box_of(nb[...])
    least_res, most_res = box_of(res[...])
    least, most = jnp.minimum(least, least_res), jnp.maximum(most, most_res)
    centre = jnp.broadcast_to(0.5 * least + 0.5 * most, (8, BLK))
    spread = jnp.max((most - least)[0:3], 0, keepdims=True)
    list_out[6:7, :] = jnp.broadcast_to(jnp.where(spread <= NARROW, 1, 0), (1, PAIR_MAX))
    copy = pltpu.make_async_copy(list_out, lists, sem.at[5])
    copy.start()
    write_squares(res, nb, centre, left, right, table)
    x, y, z = (nb[:, f, :] * HALF for f in range(3))
    alone = jnp.sum(weight_of(shell_of(x * x + y * y + z * z)) * (4.0 * nb[:, 6, :]), 1, keepdims=True)
    origin[...] = jnp.zeros_like(origin)
    origin[:, 0, :] = jnp.broadcast_to(alone, (NJ, BLK))
    acc[...] = jnp.zeros_like(acc)
    copy.wait()
    steps = (lists[4, 0] + 2 * WIDE - 1) // (2 * WIDE)

    def shell_copy(step):
        rows = pl.ds(2 * WIDE * step, 2 * WIDE)
        return pltpu.make_async_copy(held.at[rows], shell_out.at[rows], held_sem.at[step])

    def whole(n, radius2_of):
        i = lists[0, n]
        j = lists[1, n]
        totals = [jnp.zeros((8, BLK), jnp.float32)] * 2
        for g in range(GROUPS):
            rows = pl.ds(8 * g, 8)
            shell = shell_of(radius2_of(i, j, rows))
            held[n, rows, :] = shell
            totals[g % 2] = totals[g % 2] + weight_of(shell) * table[j, 3, rows, :]
        acc[i] = acc[i] + (totals[0] + totals[1])

    @pl.when(lists[6, 0] == 1)
    def _():
        def squares(n, into):
            for u in range(WIDE):
                m = jnp.minimum(n + u, PAIR_MAX - 1)
                own = jnp.minimum(lists[0, m], RES - 1)
                columns = left[lists[1, m], :, 0:SQUARE_ROWS]
                into[u] = jnp.dot(columns, right[own], preferred_element_type=jnp.float32)

        def step_of(step, carry):
            n = 2 * WIDE * step
            squares(n + WIDE, second)
            for u in range(WIDE):
                whole(n + u, lambda i, j, rows: first[u, rows, :])
            squares(n + 2 * WIDE, first)
            for u in range(WIDE):
                whole(n + WIDE + u, lambda i, j, rows: second[u, rows, :])
            shell_copy(step).start()
            return carry

        squares(0, first)
        lax.fori_loop(0, steps, step_of, 0)

    @pl.when(lists[6, 0] == 0)
    def _():
        write_columns(nb, table, ((0, HALF), (1, HALF), (2, HALF), (6, 4.0)))

        def direct(i, j, rows):
            own = jnp.minimum(i, RES - 1)
            dx, dy, dz = (res[own, f : f + 1, :] * HALF - table[j, f, rows, :] for f in range(3))
            return dx * dx + dy * dy + dz * dz

        def step_of(step, carry):
            def part(quarter, carry):
                for u in range(STEP):
                    whole(2 * WIDE * step + STEP * quarter + u, direct)
                return carry

            lax.fori_loop(0, 2 * WIDE // STEP, part, 0)
            shell_copy(step).start()
            return carry

        lax.fori_loop(0, steps, step_of, 0)

    def blank(step, carry):
        for u in range(STEP):
            i = lists[2, STEP * step + u]
            acc[i] = acc[i] + origin[lists[3, STEP * step + u]]
        return carry

    lax.fori_loop(0, (lists[5, 0] + STEP - 1) // STEP, blank, 0)
    dens = jnp.sum(acc[0:RES], 1) * KERNEL_NORM
    dens_out[...] = dens
    inverse = 1.0 / jnp.maximum(dens, DENS_FLOOR)
    cube = dens * dens * dens
    field_out[:, 0, :] = STIFF * (cube * cube * dens - 1.0) * inverse * inverse
    field_out[:, 1, :] = res[:, 6, :] * inverse
    for d in range(members):
        for k in range(NEED):
            message_out[d, 2 * k : 2 * k + 2, :] = field_out[names[d, 0, k]]
    for k in range(GH):
        message_out[members, 2 * k : 2 * k + 2, :] = field_out[NSTAY - GH + k]
        message_out[members + 1, 2 * k : 2 * k + 2, :] = field_out[k]

    def settle(step, carry):
        shell_copy(step).wait()
        return carry

    lax.fori_loop(0, steps, settle, 0)


def two_pieces(value):
    high = value.astype(jnp.bfloat16)
    return high, (value - high.astype(jnp.float32)).astype(jnp.bfloat16)


def write_factors(nb, far, press, damp, centre):
    row = lax.broadcasted_iota(jnp.int32, (8, BLK), 0)
    upper = row < 3
    lower = (row >= 3) & (row < 6)

    def store(ref, j, tiles):
        for h in range(0, len(tiles), 2):
            pair = jnp.concatenate([tiles[h].astype(jnp.float32), tiles[h + 1].astype(jnp.float32)], 0)
            pair = pair.astype(jnp.bfloat16)
            rows = pl.ds(8 * h, 16)
            ref[j, rows, 0:BLK] = pair
            ref[j, rows, BLK : 2 * BLK] = pair

    def some(step, carry):
        for u in range(FACTOR_STEP):
            j = step * FACTOR_STEP + u
            tile = nb[j]
            mass = jnp.broadcast_to(tile[6:7, :], (8, BLK))
            scaled = tile * HALF
            middle = jnp.where(upper, jnp.broadcast_to(scaled[:, 0:1], (8, BLK)), 0.0)
            centre[j] = middle
            place = scaled - middle
            mass_q = mass * jnp.broadcast_to(far[pl.ds(2 * j, 1), :], (8, BLK))
            mass_s = mass * jnp.broadcast_to(far[pl.ds(2 * j + 1, 1), :], (8, BLK))
            first = jnp.where(upper, mass * place, jnp.where(row == 6, mass, jnp.where(row == 7, mass_q, 0.0)))
            second = jnp.where(upper, mass_q * place, 0.0)
            third = jnp.where(lower, mass_s * tile, jnp.where(row == 6, mass_s, 0.0))
            store(press, j, [p for both in zip(pieces(first), pieces(second)) for p in both])
            store(damp, j, [*pieces(third), jnp.zeros((8, BLK), jnp.bfloat16)])
        return carry

    lax.fori_loop(0, NJ // FACTOR_STEP, some, 0)


def force_kernel(
    lists_in, shells, res_in, nb_in, field_in, far_in, flag_in, out,
    lists, res, nb, field, far, flag, held, acc, origin, press, damp, centre, cubes, damps, sem, fetch_sem,
):
    fetches = [
        pltpu.make_async_copy(source, target, fetch_sem.at[n])
        for n, (source, target) in enumerate(
            ((lists_in, lists), (nb_in, nb), (far_in, far), (res_in, res), (field_in, field), (flag_in, flag))
        )
    ]
    for fetch in fetches:
        fetch.start()
    fetches[0].wait()
    steps = (lists[4, 0] + WIDE - 1) // WIDE

    def shell_copy(step):
        rows = pl.ds(WIDE * step, WIDE)
        return pltpu.make_async_copy(shells.at[rows], held.at[rows], sem.at[step])

    def fetch(step, carry):
        shell_copy(step).start()
        return carry

    lax.fori_loop(0, steps, fetch, 0)
    fetches[1].wait()
    fetches[2].wait()
    write_factors(nb, far, press, damp, centre)
    acc[...] = jnp.zeros_like(acc)
    row = lax.broadcasted_iota(jnp.int32, (8, BLK), 0)
    upper = row < 3
    lower = (row >= 3) & (row < 6)
    scale = jnp.where(upper, HALF, 1.0)

    x, y, z = (nb[:, f, :] * HALF for f in range(3))
    radius2 = x * x + y * y + z * z
    shell = shell_of(radius2)
    cube = shell * shell * shell * nb[:, 6, :]
    drag = cube * radius2 / (radius2 + SOFT) * far[pl.ds(1, NJ, stride=2), :]
    push = cube * far[pl.ds(0, NJ, stride=2), :]
    origin[...] = jnp.zeros_like(origin)
    for f, place in enumerate((x, y, z)):
        origin[:, f, :] = jnp.broadcast_to(jnp.sum(cube * place, 1, keepdims=True), (NJ, BLK))
        origin[:, 8 + f, :] = jnp.broadcast_to(jnp.sum(push * place, 1, keepdims=True), (NJ, BLK))
        origin[:, 3 + f, :] = jnp.broadcast_to(jnp.sum(drag * nb[:, 3 + f, :], 1, keepdims=True), (NJ, BLK))

    def coefficients(i):
        q = jnp.broadcast_to(field[i, 0:1, :], (8, BLK))
        s = jnp.broadcast_to(field[i, 1:2, :], (8, BLK))
        return jnp.where(upper, q, jnp.where(lower, s, 0.0))

    def geometry(u, n):
        for g in range(GROUPS // 2):
            rows = pl.ds(16 * g, 16)
            shell = held[n, rows, :]
            ratio = 1.0 - shell
            radius2 = ratio * ratio
            cube = shell * shell * shell
            soft = lax.rsqrt(radius2 + SOFT)
            high, low = two_pieces(cube)
            cubes[u, rows, :] = high
            cubes[u, pl.ds(BLK + 16 * g, 16), :] = low
            high, low = two_pieces(cube * (radius2 * (soft * soft)))
            damps[u, rows, :] = high
            damps[u, pl.ds(BLK + 16 * g, 16), :] = low

    def sums_of(u, j):
        first = jnp.dot(press[j], cubes[u], preferred_element_type=jnp.float32)
        second = jnp.dot(damp[j], damps[u], preferred_element_type=jnp.float32)
        return first[0:16] + (first[16:32] + first[32:48]), second[0:8] + (second[8:16] + second[16:24])

    def whole(step, before):
        @pl.when(step < steps)
        def _():
            shell_copy(step).wait()

        sums = [sums_of(u, j) for u, (i, j) in enumerate(before)]
        after = []
        for u in range(WIDE):
            n = jnp.minimum(WIDE * step + u, PAIR_MAX - 1)
            geometry(u, n)
            after.append((lists[0, n], lists[1, n]))
        for u, (i, j) in enumerate(before):
            own = jnp.minimum(i, RES - 1)
            first, second = sums[u]
            place = res[own] * scale - centre[j]
            one, two = first[0:8], first[8:16]
            both = jnp.where(upper, jnp.broadcast_to(one[6:7], (8, BLK)), jnp.broadcast_to(second[6:7], (8, BLK)))
            only = jnp.where(upper, jnp.broadcast_to(one[7:8], (8, BLK)), 0.0)
            part = coefficients(own) * (place * both - (one + second)) + (place * only - two)
            acc[i] = acc[i] + part
        return tuple(after)

    for copy in fetches[3:]:
        copy.wait()
    nowhere = tuple((jnp.int32(RES), jnp.int32(0)) for _ in range(WIDE))
    lax.fori_loop(0, steps + 1, whole, nowhere)

    def blank(step, carry):
        for u in range(STEP):
            i = lists[2, STEP * step + u]
            j = lists[3, STEP * step + u]
            own = jnp.minimum(i, RES - 1)
            acc[i] = acc[i] - (coefficients(own) * origin[j, 0:8, :] + origin[j, 8:16, :])
        return carry

    lax.fori_loop(0, (lists[5, 0] + STEP - 1) // STEP, blank, 0)
    gravity = jnp.where(lax.broadcasted_iota(jnp.int32, (3, BLK), 0) == 2, -GRAVITY, 0.0)
    for b in range(RES):
        total = acc[b, 0:3, :] * PRESS_SCALE + acc[b, 3:6, :] * VISC_SCALE + gravity
        if b < NSTAY:
            total = total * (1.0 - flag[b : b + 1, :].astype(jnp.float32))
        out[:, b * BLK : (b + 1) * BLK] = total


def density_call(count, pairs, names, resident, neighbour):
    members = names.shape[0]
    return pl.pallas_call(
        density_kernel,
        out_shape=(
            jax.ShapeDtypeStruct((RES, BLK), jnp.float32),
            jax.ShapeDtypeStruct((RES, 2, BLK), jnp.float32),
            jax.ShapeDtypeStruct((8, PAIR_MAX), jnp.int32),
            jax.ShapeDtypeStruct((members + 2, 8, BLK), jnp.float32),
            jax.ShapeDtypeStruct((PAIR_MAX, BLK, BLK), jnp.float32),
        ),
        in_specs=[ANY] * 5,
        out_specs=(VMEM, VMEM, VMEM, VMEM, ANY),
        scratch_shapes=[
            pltpu.SMEM(count.shape, jnp.int32),
            pltpu.VMEM(pairs.shape, jnp.int32),
            pltpu.SMEM(names.shape, jnp.int32),
            pltpu.VMEM(resident.shape, jnp.float32),
            pltpu.VMEM(neighbour.shape, jnp.float32),
            pltpu.VMEM((NJ, 4, BLK, BLK), jnp.float32),
            pltpu.VMEM((RES + 1, 8, BLK), jnp.float32),
            pltpu.VMEM((NJ, 8, BLK), jnp.float32),
            pltpu.VMEM((PAIR_MAX, BLK, BLK), jnp.float32),
            pltpu.VMEM((NJ, BLK, BLK), jnp.bfloat16),
            pltpu.VMEM((RES, SQUARE_ROWS, BLK), jnp.bfloat16),
            pltpu.VMEM((WIDE, BLK, BLK), jnp.float32),
            pltpu.VMEM((WIDE, BLK, BLK), jnp.float32),
            pltpu.SMEM((8, PAIR_MAX), jnp.int32),
            pltpu.SemaphoreType.DMA((6,)),
            pltpu.SemaphoreType.DMA((PAIR_MAX // (2 * WIDE),)),
        ],
        compiler_params=pltpu.CompilerParams(vmem_limit_bytes=LIMIT),
    )(count, pairs, names, resident, neighbour)


def force_call(lists, shells, resident, neighbour, field, far, flag):
    return pl.pallas_call(
        force_kernel,
        out_shape=jax.ShapeDtypeStruct((3, RES * BLK), jnp.float32),
        in_specs=[ANY] * 7,
        out_specs=VMEM,
        scratch_shapes=[
            pltpu.SMEM(lists.shape, jnp.int32),
            pltpu.VMEM(resident.shape, jnp.float32),
            pltpu.VMEM(neighbour.shape, jnp.float32),
            pltpu.VMEM(field.shape, jnp.float32),
            pltpu.VMEM(far.shape, jnp.float32),
            pltpu.VMEM(flag.shape, jnp.int32),
            pltpu.VMEM((PAIR_MAX, BLK, BLK), jnp.float32),
            pltpu.VMEM((RES + 1, 8, BLK), jnp.float32),
            pltpu.VMEM((NJ, 16, BLK), jnp.float32),
            pltpu.VMEM((NJ, 48, 2 * BLK), jnp.bfloat16),
            pltpu.VMEM((NJ, 32, 2 * BLK), jnp.bfloat16),
            pltpu.VMEM((NJ, 8, BLK), jnp.float32),
            pltpu.VMEM((WIDE, 2 * BLK, BLK), jnp.bfloat16),
            pltpu.VMEM((WIDE, 2 * BLK, BLK), jnp.bfloat16),
            pltpu.SemaphoreType.DMA((PAIR_MAX // WIDE,)),
            pltpu.SemaphoreType.DMA((6,)),
        ],
        compiler_params=pltpu.CompilerParams(vmem_limit_bytes=LIMIT),
    )(lists, shells, resident, neighbour, field, far, flag)


def on_device(stay, leave, stay_flag, send_list, send_count, wanted, pair_tiles, pair_count):
    slabs = send_list.shape[1]
    members = wanted.shape[1]
    leaving = leave.reshape(7, slabs * SM, BLK).transpose(1, 0, 2)
    staying = stay.reshape(7, NSTAY, BLK).transpose(1, 0, 2)
    resident, neighbour, asked = migrate_call(
        slabs, members, send_list.transpose(0, 2, 1), send_count, wanted.transpose(0, 2, 1), leaving, staying
    )
    dens, field, lists, messages, shells = density_call(pair_count, pair_tiles[0], asked, resident, neighbour)
    far = field_call(slabs, members, messages)
    accel = force_call(lists, shells, resident, neighbour, field, far, stay_flag.reshape(NSTAY, BLK))
    return (dens.reshape(-1), accel)


def solution(mesh):
    in_specs = (
        P(None, ("slab", "grp")),
        P(None, ("slab", "grp")),
        P(("slab", "grp")),
        P(("slab", "grp"), None, None),
        P(("slab", "grp"), None),
        P(("slab", "grp"), None, None),
        P(("slab", "grp"), None, None),
        P(("slab", "grp")),
    )
    out_specs = (P(("slab", "grp")), P(None, ("slab", "grp")))
    return jax.shard_map(
        on_device, mesh=mesh, in_specs=in_specs, out_specs=out_specs, check_vma=False
    )
```

```python
import functools
import math

import jax
import jax.numpy as jnp
from jax import lax
from jax.experimental import pallas as pl
from jax.experimental.pallas import tpu as pltpu
from jax.sharding import PartitionSpec as P

BLK = 128
SM = 2
GH = 4
NEED = 4
PAIR_MAX = 256
NSTAY = 16
RES = 80
NJ = 40
GROUPS = BLK // 8
COLUMN_STEP = 8
SQUARE_STEP = 40
STEP = 4
WIDE = 8
NARROW = 6.0
SQUARE_ROWS = 48
FACTOR_STEP = 20

KERNEL_NORM = 21.0 / (16.0 * math.pi)
SMOOTH = 1.0
HALF = 0.5 / SMOOTH
DENS_FLOOR = 0.5
STIFF = 0.02
VISCOUS = 0.1
GRAVITY = 1.0
TINY = 1e-30
FAR = 3e38
SOFT = 0.01 * HALF * HALF
PRESS_SCALE = 5.0 * KERNEL_NORM / (SMOOTH * SMOOTH) / HALF
VISC_SCALE = -VISCOUS * 5.0 * KERNEL_NORM / (SMOOTH * SMOOTH)

VMEM = pl.BlockSpec(memory_space=pltpu.VMEM)
SMEM = pl.BlockSpec(memory_space=pltpu.SMEM)
ANY = pl.BlockSpec(memory_space=pl.ANY)
MESH = pl.DeviceIdType.MESH
LIMIT = 56 * 1024 * 1024


def ring_steps(r, size):
    return min(r, size - r)


def migrate_kernel(
    slabs, members, lists_in, counts_in, wanted_in, leave, stay,
    res_out, nb_out, asked_out,
    lists, counts, wanted, leaving, staying, packed, res, edges, request, asked, names, chosen,
    row_send, row_recv, ghost_send, ghost_recv, name_send, name_recv, near_send, near_recv, local_sem,
):
    slab = lax.axis_index("slab")
    grp = lax.axis_index("grp")
    ghosts = members * NEED
    barrier = pltpu.get_barrier_semaphore()

    far_slabs = sorted(range(1, slabs), key=lambda r: -ring_steps(r // 8, 4) - ring_steps(r // 2 % 4, 4))
    far_members = sorted(range(1, members), key=lambda r: -ring_steps(r, members))
    for r in far_members:
        pl.semaphore_signal(barrier, inc=1, device_id={"grp": (grp + r) % members}, device_id_type=MESH)
    for r in far_slabs:
        pl.semaphore_signal(barrier, inc=1, device_id={"slab": (slab + r) % slabs}, device_id_type=MESH)
    fetch_leave = pltpu.make_async_copy(leave, leaving, local_sem.at[0])
    fetch_stay = pltpu.make_async_copy(stay, staying, local_sem.at[1])
    fetch_leave.start()
    fetch_stay.start()
    small = [
        pltpu.make_async_copy(source, target, local_sem.at[5 + n])
        for n, (source, target) in enumerate(((wanted_in, wanted), (lists_in, lists), (counts_in, counts)))
    ]
    for copy in small:
        copy.start()
    for copy in small:
        copy.wait()
    lane = lax.broadcasted_iota(jnp.int32, (1, BLK), 1)
    for p in range(members):
        ask = jnp.zeros((1, BLK), jnp.int32)
        for k in range(NEED):
            ask = jnp.where(lane == k, wanted[0, k, p], ask)
        request[p] = ask
    fetch_stay.wait()
    for b in range(NSTAY):
        res[b, 0:7, :] = staying[b]
        res[b, 7:8, :] = jnp.ones((1, BLK), jnp.float32)
    fetch_leave.wait()
    for t in range(slabs):
        count = counts[0, t]
        for k in range(SM):
            keep = jnp.broadcast_to(jnp.minimum(jnp.maximum(count - k, 0), 1), (1, BLK)).astype(jnp.float32)
            packed[t * SM + k, 0:7, :] = leaving[lists[0, k, t]] * keep
            packed[t * SM + k, 7:8, :] = keep
    pl.semaphore_wait(barrier, slabs - 1 + members - 1)

    def name_copy(r):
        target = (grp + r) % members
        return pltpu.make_async_remote_copy(
            src_ref=request.at[target], dst_ref=asked.at[grp], send_sem=name_send.at[r], recv_sem=name_recv.at[r],
            device_id={"grp": target}, device_id_type=MESH,
        )

    def row_copy(r):
        target = (slab + r) % slabs
        return pltpu.make_async_remote_copy(
            src_ref=packed.at[pl.ds(target * SM, SM)], dst_ref=res.at[pl.ds(NSTAY + slab * SM, SM)],
            send_sem=row_send.at[r], recv_sem=row_recv.at[r],
            device_id={"slab": target}, device_id_type=MESH,
        )

    def ghost_copy(side):
        first = NSTAY - GH if side == 0 else 0
        target = (slab + (1 if side == 0 else slabs - 1)) % slabs
        return pltpu.make_async_remote_copy(
            src_ref=res.at[pl.ds(first, GH)], dst_ref=edges.at[pl.ds(side * GH, GH)],
            send_sem=ghost_send.at[side], recv_sem=ghost_recv.at[side],
            device_id={"slab": target}, device_id_type=MESH,
        )

    def near_copy(r):
        target = (grp + r) % members
        return pltpu.make_async_remote_copy(
            src_ref=chosen.at[target], dst_ref=nb_out.at[pl.ds(grp * NEED, NEED)],
            send_sem=near_send.at[r], recv_sem=near_recv.at[r],
            device_id={"grp": target}, device_id_type=MESH,
        )

    def each(order, step):
        for r in order:
            step(r)

    each(far_members, lambda r: name_copy(r).start())
    each(far_slabs, lambda r: row_copy(r).start())
    ghost_copy(0).start()
    ghost_copy(1).start()
    asked[grp] = request[grp]
    mine = pl.ds(NSTAY + slab * SM, SM)
    res[mine] = packed[pl.ds(slab * SM, SM)]
    each(far_members, lambda r: name_copy(r).wait_recv())
    local = pltpu.make_async_copy(asked, names, local_sem.at[2])
    local.start()
    local.wait()
    store_asked = pltpu.make_async_copy(asked, asked_out, local_sem.at[8])
    store_asked.start()
    each(far_slabs, lambda r: row_copy(r).wait_recv())
    for d in range(members):
        for k in range(NEED):
            chosen[d, k] = res[names[d, 0, k]]
    each(far_members, lambda r: near_copy(r).start())
    store_own = pltpu.make_async_copy(chosen.at[grp], nb_out.at[pl.ds(grp * NEED, NEED)], local_sem.at[4])
    store_own.start()
    store_res = pltpu.make_async_copy(res, res_out, local_sem.at[3])
    store_res.start()
    ghost_copy(0).wait_recv()
    ghost_copy(1).wait_recv()
    for side, some in ((0, slab > 0), (1, slab < slabs - 1)):
        rows = pl.ds(side * GH, GH)
        edges[rows] = edges[rows] * some.astype(jnp.float32)
    store_edges = pltpu.make_async_copy(edges, nb_out.at[pl.ds(ghosts, 2 * GH)], local_sem.at[9])
    store_edges.start()
    each(far_members, lambda r: near_copy(r).wait_recv())
    each(far_members, lambda r: name_copy(r).wait_send())
    each(far_slabs, lambda r: row_copy(r).wait_send())
    each(far_members, lambda r: near_copy(r).wait_send())
    ghost_copy(0).wait_send()
    ghost_copy(1).wait_send()
    for store in (store_asked, store_own, store_res, store_edges):
        store.wait()


def migrate_call(slabs, members, lists, counts, wanted, leave, stay):
    blocks = NSTAY + slabs * SM
    near = members * NEED + 2 * GH
    f32 = jnp.float32
    dma = pltpu.SemaphoreType.DMA
    return pl.pallas_call(
        functools.partial(migrate_kernel, slabs, members),
        out_shape=(
            jax.ShapeDtypeStruct((blocks, 8, BLK), f32),
            jax.ShapeDtypeStruct((near, 8, BLK), f32),
            jax.ShapeDtypeStruct((members, 1, BLK), jnp.int32),
        ),
        in_specs=[ANY, ANY, ANY, ANY, ANY],
        out_specs=(ANY, ANY, ANY),
        scratch_shapes=[
            pltpu.SMEM(lists.shape, jnp.int32),
            pltpu.SMEM(counts.shape, jnp.int32),
            pltpu.SMEM(wanted.shape, jnp.int32),
            pltpu.VMEM(leave.shape, f32),
            pltpu.VMEM(stay.shape, f32),
            pltpu.VMEM((slabs * SM, 8, BLK), f32),
            pltpu.VMEM((blocks, 8, BLK), f32),
            pltpu.VMEM((2 * GH, 8, BLK), f32),
            pltpu.VMEM((members, 1, BLK), jnp.int32),
            pltpu.VMEM((members, 1, BLK), jnp.int32),
            pltpu.SMEM((members, 1, BLK), jnp.int32),
            pltpu.VMEM((members, NEED, 8, BLK), f32),
            dma((slabs,)), dma((slabs,)), dma((2,)), dma((2,)),
            dma((members,)), dma((members,)), dma((members,)), dma((members,)), dma((10,)),
        ],
        compiler_params=pltpu.CompilerParams(collective_id=0, has_side_effects=True, vmem_limit_bytes=LIMIT),
    )(lists, counts, wanted, leave, stay)


def field_kernel(slabs, members, messages, out, near_send, near_recv, edge_send, edge_recv, own_sem):
    slab = lax.axis_index("slab")
    grp = lax.axis_index("grp")
    above = (slab + 1) % slabs
    below = (slab + slabs - 1) % slabs
    far_members = sorted(range(1, members), key=lambda r: -ring_steps(r, members))
    barrier = pltpu.get_barrier_semaphore()
    for r in far_members:
        pl.semaphore_signal(barrier, inc=1, device_id={"grp": (grp + r) % members}, device_id_type=MESH)
    for target in (above, below):
        pl.semaphore_signal(barrier, inc=1, device_id={"slab": target}, device_id_type=MESH)
    own = pltpu.make_async_copy(messages.at[grp], out.at[grp], own_sem)
    own.start()
    pl.semaphore_wait(barrier, members + 1)

    def near_copy(r):
        target = (grp + r) % members
        return pltpu.make_async_remote_copy(
            src_ref=messages.at[target], dst_ref=out.at[grp], send_sem=near_send.at[r], recv_sem=near_recv.at[r],
            device_id={"grp": target}, device_id_type=MESH,
        )

    def edge_copy(side):
        return pltpu.make_async_remote_copy(
            src_ref=messages.at[members + side], dst_ref=out.at[members + side],
            send_sem=edge_send.at[side], recv_sem=edge_recv.at[side],
            device_id={"slab": above if side == 0 else below}, device_id_type=MESH,
        )

    copies = [near_copy(r) for r in far_members] + [edge_copy(0), edge_copy(1)]
    for copy in copies:
        copy.start()
    own.wait()
    for copy in copies:
        copy.wait_recv()
    for copy in copies:
        copy.wait_send()


def field_call(slabs, members, messages):
    dma = pltpu.SemaphoreType.DMA
    out = pl.pallas_call(
        functools.partial(field_kernel, slabs, members),
        out_shape=jax.ShapeDtypeStruct((members + 2, 8, BLK), jnp.float32),
        in_specs=[ANY],
        out_specs=ANY,
        scratch_shapes=[dma((members,)), dma((members,)), dma((2,)), dma((2,)), dma],
        compiler_params=pltpu.CompilerParams(collective_id=1, has_side_effects=True),
    )(messages)
    return out.reshape(-1, BLK)


def shell_of(radius2):
    square = jnp.maximum(radius2, TINY)
    return jnp.maximum(1.0 - square * lax.rsqrt(square), 0.0)


def weight_of(shell):
    square = shell * shell
    return square * square * (1.25 - shell)


def write_lists(count, pairs, res, nb, out):
    left = pairs[0:1, :]
    right = pairs[1:2, :]
    lane = lax.broadcasted_iota(jnp.int32, (1, PAIR_MAX), 1)
    res_live = res[:, 7, :]
    nb_live = nb[:, 7, :]
    res_live = jnp.concatenate([res_live, res_live], 1)
    nb_live = jnp.concatenate([nb_live, nb_live], 1)
    hit = lax.broadcasted_iota(jnp.int32, (RES, PAIR_MAX), 0) == left
    live_left = jnp.sum(jnp.where(hit, res_live, 0.0), 0, keepdims=True)
    hit = lax.broadcasted_iota(jnp.int32, (NJ, PAIR_MAX), 0) == right
    live_right = jnp.sum(jnp.where(hit, nb_live, 0.0), 0, keepdims=True)
    valid = jnp.where(lane < count, live_right, 0.0)
    heavy = valid * live_left
    light = valid * (1.0 - live_left)
    before = lax.broadcasted_iota(jnp.int32, (PAIR_MAX, PAIR_MAX), 0) < lax.broadcasted_iota(
        jnp.int32, (PAIR_MAX, PAIR_MAX), 1
    )
    blank = jnp.zeros((6, PAIR_MAX), jnp.float32)
    kinds = jnp.concatenate([heavy, light, blank], 0).astype(jnp.bfloat16)
    spots = jnp.dot(kinds, jnp.where(before, 1.0, 0.0).astype(jnp.bfloat16), preferred_element_type=jnp.float32)
    names = jnp.concatenate([left.astype(jnp.float32), right.astype(jnp.float32), blank], 0).astype(jnp.bfloat16)
    row = lax.broadcasted_iota(jnp.int32, (PAIR_MAX, PAIR_MAX), 0).astype(jnp.float32)
    sums = jnp.sum(jnp.concatenate([heavy, light, blank], 0), 1, keepdims=True)
    for kind, member in ((0, heavy), (1, light)):
        target = jnp.where(member > 0.5, spots[kind : kind + 1, :], -1.0)
        chosen = jnp.where(row == target, 1.0, 0.0).astype(jnp.bfloat16)
        packed = lax.dot_general(names, chosen, (((1,), (1,)), ((), ())), preferred_element_type=jnp.float32)
        amount = jnp.broadcast_to(sums[kind : kind + 1, :], (1, PAIR_MAX))
        filled = lane.astype(jnp.float32) < amount
        out[2 * kind : 2 * kind + 1, :] = jnp.where(filled, packed[0:1, :], float(RES)).astype(jnp.int32)
        out[2 * kind + 1 : 2 * kind + 2, :] = packed[1:2, :].astype(jnp.int32)
        out[4 + kind : 5 + kind, :] = amount.astype(jnp.int32)
    out[6:8, :] = jnp.zeros((2, PAIR_MAX), jnp.int32)


def box_of(tiles):
    live = jnp.broadcast_to(tiles[:, 7:8, :], tiles.shape) > 0.5
    least = jnp.min(jnp.where(live, tiles * HALF, FAR), 0)
    most = jnp.max(jnp.where(live, tiles * HALF, -FAR), 0)
    return jnp.min(least, 1, keepdims=True), jnp.max(most, 1, keepdims=True)


def square_rows(tile, centre, own, other):
    row = lax.broadcasted_iota(jnp.int32, (8, BLK), 0)
    place = jnp.where(row < 3, tile * HALF - centre, 0.0)
    square = jnp.broadcast_to(jnp.sum(place * place, 0, keepdims=True), (8, BLK))
    high, mid, low = (p.astype(jnp.float32) for p in pieces(jnp.where(row == own, square, place)))
    return row < 3, jnp.where(row == other, 1.0, 0.0), high, mid, low


def write_squares(res, nb, centre, left, right, table):
    left[...] = jnp.zeros_like(left)
    row = lax.broadcasted_iota(jnp.int32, (SQUARE_ROWS, BLK), 0)
    spread = jnp.where((row == 5) | (row == 13) | (row == 21), 4.0, 0.0).astype(jnp.bfloat16)
    eight = lax.broadcasted_iota(jnp.int32, (8, BLK), 0)

    def columns(step, carry):
        for u in range(SQUARE_STEP):
            j = step * SQUARE_STEP + u
            tile = nb[j]
            place, one, high, mid, low = square_rows(tile, centre, 3, 4)
            mass = jnp.where(eight == 5, jnp.broadcast_to(tile[6:7, :], (8, BLK)), 0.0)
            masses = [m.astype(jnp.float32) for m in pieces(mass)]
            stacked = jnp.concatenate(
                [
                    high + one + masses[0],
                    jnp.where(place, high, mid) + one + masses[1],
                    jnp.where(place, mid, low) + one + masses[2],
                    jnp.where(place, mid, 0.0),
                    jnp.where(place, high, 0.0),
                    jnp.where(place, low, 0.0),
                ],
                0,
            )
            turned = jnp.transpose(stacked, (1, 0)).astype(jnp.bfloat16)
            left[j, :, 0:SQUARE_ROWS] = turned
            table[j, 3] = jnp.dot(turned, spread, preferred_element_type=jnp.float32)
        return carry

    lax.fori_loop(0, NJ // SQUARE_STEP, columns, 0)

    def rows(step, carry):
        for u in range(SQUARE_STEP):
            i = step * SQUARE_STEP + u
            place, one, high, mid, low = square_rows(res[i], centre, 4, 3)
            twice = jnp.where(place, -2.0, 1.0)
            high, mid, low = high * twice, mid * twice, low * twice
            stacked = jnp.concatenate(
                [
                    high + one,
                    mid + one,
                    jnp.where(place, high, low) + one,
                    jnp.where(place, mid, 0.0),
                    jnp.where(place, low, 0.0),
                    jnp.where(place, high, 0.0),
                ],
                0,
            )
            right[i] = stacked.astype(jnp.bfloat16)
        return carry

    lax.fori_loop(0, RES // SQUARE_STEP, rows, 0)


def pieces(value):
    high = value.astype(jnp.bfloat16)
    rest = value - high.astype(jnp.float32)
    mid = rest.astype(jnp.bfloat16)
    low = (rest - mid.astype(jnp.float32)).astype(jnp.bfloat16)
    return high, mid, low


def write_columns(nb, table, fields):
    count = len(fields)
    row = lax.broadcasted_iota(jnp.int32, (32, count * BLK), 0)
    spot = lax.broadcasted_iota(jnp.int32, (32, count * BLK), 1) // BLK
    spread = jnp.zeros((32, count * BLK), jnp.float32)
    for n, (field, scale) in enumerate(fields):
        mine = (row == field) | (row == 8 + field) | (row == 16 + field)
        spread = jnp.where((spot == n) & mine, scale, spread)
    spread = spread.astype(jnp.bfloat16)

    def some(step, carry):
        for u in range(COLUMN_STEP):
            j = step * COLUMN_STEP + u
            high, mid, low = (p.astype(jnp.float32) for p in pieces(nb[j]))
            stacked = jnp.concatenate([high, mid, low, jnp.zeros((8, BLK), jnp.float32)], 0)
            turned = jnp.transpose(stacked, (1, 0)).astype(jnp.bfloat16)
            wide = jnp.dot(turned, spread, preferred_element_type=jnp.float32)
            for n in range(count):
                table[j, n] = wide[:, n * BLK : (n + 1) * BLK]
        return carry

    lax.fori_loop(0, NJ // COLUMN_STEP, some, 0)


def pieces(value):
    high = value.astype(jnp.bfloat16)
    rest = value - high.astype(jnp.float32)
    mid = rest.astype(jnp.bfloat16)
    low = (rest - mid.astype(jnp.float32)).astype(jnp.bfloat16)
    return high, mid, low


def write_columns(nb, table, fields):
    count = len(fields)
    row = lax.broadcasted_iota(jnp.int32, (32, count * BLK), 0)
    spot = lax.broadcasted_iota(jnp.int32, (32, count * BLK), 1) // BLK
    spread = jnp.zeros((32, count * BLK), jnp.float32)
    for n, (field, scale) in enumerate(fields):
        mine = (row == field) | (row == 8 + field) | (row == 16 + field)
        spread = jnp.where((spot == n) & mine, scale, spread)
    spread = spread.astype(jnp.bfloat16)

    def some(step, carry):
        for u in range(COLUMN_STEP):
            j = step * COLUMN_STEP + u
            high, mid, low = (p.astype(jnp.float32) for p in pieces(nb[j]))
            stacked = jnp.concatenate([high, mid, low, jnp.zeros((8, BLK), jnp.float32)], 0)
            turned = jnp.transpose(stacked, (1, 0)).astype(jnp.bfloat16)
            wide = jnp.dot(turned, spread, preferred_element_type=jnp.float32)
            for n in range(count):
                table[j, n] = wide[:, n * BLK : (n + 1) * BLK]
        return carry

    lax.fori_loop(0, NJ // COLUMN_STEP, some, 0)


def density_kernel(
    count_in, pairs_in, names_in, res_in, nb_in, dens_out, field_out, list_out, message_out, shell_out,
    count, pairs, names, res, nb, table, acc, origin, held, left, right, first, second, lists, sem, held_sem,
):
    members = names.shape[0]
    fetches = [
        pltpu.make_async_copy(source, target, sem.at[n])
        for n, (source, target) in enumerate(
            ((nb_in, nb), (res_in, res), (pairs_in, pairs), (count_in, count), (names_in, names))
        )
    ]
    for fetch in fetches:
        fetch.start()
    for fetch in fetches:
        fetch.wait()
    write_lists(count[0], pairs, res, nb, list_out)
    least, most = box_of(nb[...])
    least_res, most_res = box_of(res[...])
    least, most = jnp.minimum(least, least_res), jnp.maximum(most, most_res)
    centre = jnp.broadcast_to(0.5 * least + 0.5 * most, (8, BLK))
    spread = jnp.max((most - least)[0:3], 0, keepdims=True)
    list_out[6:7, :] = jnp.broadcast_to(jnp.where(spread <= NARROW, 1, 0), (1, PAIR_MAX))
    copy = pltpu.make_async_copy(list_out, lists, sem.at[5])
    copy.start()
    write_squares(res, nb, centre, left, right, table)
    x, y, z = (nb[:, f, :] * HALF for f in range(3))
    alone = jnp.sum(weight_of(shell_of(x * x + y * y + z * z)) * (4.0 * nb[:, 6, :]), 1, keepdims=True)
    origin[...] = jnp.zeros_like(origin)
    origin[:, 0, :] = jnp.broadcast_to(alone, (NJ, BLK))
    acc[...] = jnp.zeros_like(acc)
    copy.wait()
    steps = (lists[4, 0] + 2 * WIDE - 1) // (2 * WIDE)

    def shell_copy(step):
        rows = pl.ds(2 * WIDE * step, 2 * WIDE)
        return pltpu.make_async_copy(held.at[rows], shell_out.at[rows], held_sem.at[step])

    def whole(n, radius2_of):
        i = lists[0, n]
        j = lists[1, n]
        totals = [jnp.zeros((8, BLK), jnp.float32)] * 2
        for g in range(GROUPS):
            rows = pl.ds(8 * g, 8)
            shell = shell_of(radius2_of(i, j, rows))
            held[n, rows, :] = shell
            totals[g % 2] = totals[g % 2] + weight_of(shell) * table[j, 3, rows, :]
        acc[i] = acc[i] + (totals[0] + totals[1])

    @pl.when(lists[6, 0] == 1)
    def _():
        def squares(n, into):
            for u in range(WIDE):
                m = jnp.minimum(n + u, PAIR_MAX - 1)
                own = jnp.minimum(lists[0, m], RES - 1)
                columns = left[lists[1, m], :, 0:SQUARE_ROWS]
                into[u] = jnp.dot(columns, right[own], preferred_element_type=jnp.float32)

        def step_of(step, carry):
            n = 2 * WIDE * step
            squares(n + WIDE, second)
            for u in range(WIDE):
                whole(n + u, lambda i, j, rows: first[u, rows, :])
            squares(n + 2 * WIDE, first)
            for u in range(WIDE):
                whole(n + WIDE + u, lambda i, j, rows: second[u, rows, :])
            shell_copy(step).start()
            return carry

        squares(0, first)
        lax.fori_loop(0, steps, step_of, 0)

    @pl.when(lists[6, 0] == 0)
    def _():
        write_columns(nb, table, ((0, HALF), (1, HALF), (2, HALF), (6, 4.0)))

        def direct(i, j, rows):
            own = jnp.minimum(i, RES - 1)
            dx, dy, dz = (res[own, f : f + 1, :] * HALF - table[j, f, rows, :] for f in range(3))
            return dx * dx + dy * dy + dz * dz

        def step_of(step, carry):
            def part(quarter, carry):
                for u in range(STEP):
                    whole(2 * WIDE * step + STEP * quarter + u, direct)
                return carry

            lax.fori_loop(0, 2 * WIDE // STEP, part, 0)
            shell_copy(step).start()
            return carry

        lax.fori_loop(0, steps, step_of, 0)

    def blank(step, carry):
        for u in range(STEP):
            i = lists[2, STEP * step + u]
            acc[i] = acc[i] + origin[lists[3, STEP * step + u]]
        return carry

    lax.fori_loop(0, (lists[5, 0] + STEP - 1) // STEP, blank, 0)
    dens = jnp.sum(acc[0:RES], 1) * KERNEL_NORM
    dens_out[...] = dens
    inverse = 1.0 / jnp.maximum(dens, DENS_FLOOR)
    cube = dens * dens * dens
    field_out[:, 0, :] = STIFF * (cube * cube * dens - 1.0) * inverse * inverse
    field_out[:, 1, :] = res[:, 6, :] * inverse
    for d in range(members):
        for k in range(NEED):
            message_out[d, 2 * k : 2 * k + 2, :] = field_out[names[d, 0, k]]
    for k in range(GH):
        message_out[members, 2 * k : 2 * k + 2, :] = field_out[NSTAY - GH + k]
        message_out[members + 1, 2 * k : 2 * k + 2, :] = field_out[k]

    def settle(step, carry):
        shell_copy(step).wait()
        return carry

    lax.fori_loop(0, steps, settle, 0)


def two_pieces(value):
    high = value.astype(jnp.bfloat16)
    return high, (value - high.astype(jnp.float32)).astype(jnp.bfloat16)


def write_factors(nb, far, press, damp, centre):
    row = lax.broadcasted_iota(jnp.int32, (8, BLK), 0)
    upper = row < 3
    lower = (row >= 3) & (row < 6)

    def store(ref, j, tiles):
        for h in range(0, len(tiles), 2):
            pair = jnp.concatenate([tiles[h].astype(jnp.float32), tiles[h + 1].astype(jnp.float32)], 0)
            pair = pair.astype(jnp.bfloat16)
            rows = pl.ds(8 * h, 16)
            ref[j, rows, 0:BLK] = pair
            ref[j, rows, BLK : 2 * BLK] = pair

    def some(step, carry):
        for u in range(FACTOR_STEP):
            j = step * FACTOR_STEP + u
            tile = nb[j]
            mass = jnp.broadcast_to(tile[6:7, :], (8, BLK))
            scaled = tile * HALF
            middle = jnp.where(upper, jnp.broadcast_to(scaled[:, 0:1], (8, BLK)), 0.0)
            centre[j] = middle
            place = scaled - middle
            mass_q = mass * jnp.broadcast_to(far[pl.ds(2 * j, 1), :], (8, BLK))
            mass_s = mass * jnp.broadcast_to(far[pl.ds(2 * j + 1, 1), :], (8, BLK))
            first = jnp.where(upper, mass * place, jnp.where(row == 6, mass, jnp.where(row == 7, mass_q, 0.0)))
            second = jnp.where(upper, mass_q * place, 0.0)
            third = jnp.where(lower, mass_s * tile, jnp.where(row == 6, mass_s, 0.0))
            store(press, j, [p for both in zip(pieces(first), pieces(second)) for p in both])
            store(damp, j, [*pieces(third), jnp.zeros((8, BLK), jnp.bfloat16)])
        return carry

    lax.fori_loop(0, NJ // FACTOR_STEP, some, 0)


def force_kernel(
    lists_in, shells, res_in, nb_in, field_in, far_in, flag_in, out,
    lists, res, nb, field, far, flag, held, acc, origin, press, damp, centre, cubes, damps, sem, fetch_sem,
):
    fetches = [
        pltpu.make_async_copy(source, target, fetch_sem.at[n])
        for n, (source, target) in enumerate(
            ((lists_in, lists), (nb_in, nb), (far_in, far), (res_in, res), (field_in, field), (flag_in, flag))
        )
    ]
    for fetch in fetches:
        fetch.start()
    fetches[0].wait()
    steps = (lists[4, 0] + WIDE - 1) // WIDE

    def shell_copy(step):
        rows = pl.ds(WIDE * step, WIDE)
        return pltpu.make_async_copy(shells.at[rows], held.at[rows], sem.at[step])

    def fetch(step, carry):
        shell_copy(step).start()
        return carry

    lax.fori_loop(0, steps, fetch, 0)
    fetches[1].wait()
    fetches[2].wait()
    write_factors(nb, far, press, damp, centre)
    acc[...] = jnp.zeros_like(acc)
    row = lax.broadcasted_iota(jnp.int32, (8, BLK), 0)
    upper = row < 3
    lower = (row >= 3) & (row < 6)
    scale = jnp.where(upper, HALF, 1.0)

    x, y, z = (nb[:, f, :] * HALF for f in range(3))
    radius2 = x * x + y * y + z * z
    shell = shell_of(radius2)
    cube = shell * shell * shell * nb[:, 6, :]
    drag = cube * radius2 / (radius2 + SOFT) * far[pl.ds(1, NJ, stride=2), :]
    push = cube * far[pl.ds(0, NJ, stride=2), :]
    origin[...] = jnp.zeros_like(origin)
    for f, place in enumerate((x, y, z)):
        origin[:, f, :] = jnp.broadcast_to(jnp.sum(cube * place, 1, keepdims=True), (NJ, BLK))
        origin[:, 8 + f, :] = jnp.broadcast_to(jnp.sum(push * place, 1, keepdims=True), (NJ, BLK))
        origin[:, 3 + f, :] = jnp.broadcast_to(jnp.sum(drag * nb[:, 3 + f, :], 1, keepdims=True), (NJ, BLK))

    def coefficients(i):
        q = jnp.broadcast_to(field[i, 0:1, :], (8, BLK))
        s = jnp.broadcast_to(field[i, 1:2, :], (8, BLK))
        return jnp.where(upper, q, jnp.where(lower, s, 0.0))

    def geometry(u, n):
        for g in range(GROUPS // 2):
            rows = pl.ds(16 * g, 16)
            shell = held[n, rows, :]
            ratio = 1.0 - shell
            radius2 = ratio * ratio
            cube = shell * shell * shell
            soft = lax.rsqrt(radius2 + SOFT)
            high, low = two_pieces(cube)
            cubes[u, rows, :] = high
            cubes[u, pl.ds(BLK + 16 * g, 16), :] = low
            high, low = two_pieces(cube * (radius2 * (soft * soft)))
            damps[u, rows, :] = high
            damps[u, pl.ds(BLK + 16 * g, 16), :] = low

    def sums_of(u, j):
        first = jnp.dot(press[j], cubes[u], preferred_element_type=jnp.float32)
        second = jnp.dot(damp[j], damps[u], preferred_element_type=jnp.float32)
        return first[0:16] + (first[16:32] + first[32:48]), second[0:8] + (second[8:16] + second[16:24])

    def whole(step, before):
        @pl.when(step < steps)
        def _():
            shell_copy(step).wait()

        sums = [sums_of(u, j) for u, (i, j) in enumerate(before)]
        after = []
        for u in range(WIDE):
            n = jnp.minimum(WIDE * step + u, PAIR_MAX - 1)
            geometry(u, n)
            after.append((lists[0, n], lists[1, n]))
        for u, (i, j) in enumerate(before):
            own = jnp.minimum(i, RES - 1)
            first, second = sums[u]
            place = res[own] * scale - centre[j]
            one, two = first[0:8], first[8:16]
            both = jnp.where(upper, jnp.broadcast_to(one[6:7], (8, BLK)), jnp.broadcast_to(second[6:7], (8, BLK)))
            only = jnp.where(upper, jnp.broadcast_to(one[7:8], (8, BLK)), 0.0)
            part = coefficients(own) * (place * both - (one + second)) + (place * only - two)
            acc[i] = acc[i] + part
        return tuple(after)

    for copy in fetches[3:]:
        copy.wait()
    nowhere = tuple((jnp.int32(RES), jnp.int32(0)) for _ in range(WIDE))
    lax.fori_loop(0, steps + 1, whole, nowhere)

    def blank(step, carry):
        for u in range(STEP):
            i = lists[2, STEP * step + u]
            j = lists[3, STEP * step + u]
            own = jnp.minimum(i, RES - 1)
            acc[i] = acc[i] - (coefficients(own) * origin[j, 0:8, :] + origin[j, 8:16, :])
        return carry

    lax.fori_loop(0, (lists[5, 0] + STEP - 1) // STEP, blank, 0)
    gravity = jnp.where(lax.broadcasted_iota(jnp.int32, (3, BLK), 0) == 2, -GRAVITY, 0.0)
    for b in range(RES):
        total = acc[b, 0:3, :] * PRESS_SCALE + acc[b, 3:6, :] * VISC_SCALE + gravity
        if b < NSTAY:
            total = total * (1.0 - flag[b : b + 1, :].astype(jnp.float32))
        out[:, b * BLK : (b + 1) * BLK] = total


def density_call(count, pairs, names, resident, neighbour):
    members = names.shape[0]
    return pl.pallas_call(
        density_kernel,
        out_shape=(
            jax.ShapeDtypeStruct((RES, BLK), jnp.float32),
            jax.ShapeDtypeStruct((RES, 2, BLK), jnp.float32),
            jax.ShapeDtypeStruct((8, PAIR_MAX), jnp.int32),
            jax.ShapeDtypeStruct((members + 2, 8, BLK), jnp.float32),
            jax.ShapeDtypeStruct((PAIR_MAX, BLK, BLK), jnp.float32),
        ),
        in_specs=[ANY] * 5,
        out_specs=(VMEM, VMEM, VMEM, VMEM, ANY),
        scratch_shapes=[
            pltpu.SMEM(count.shape, jnp.int32),
            pltpu.VMEM(pairs.shape, jnp.int32),
            pltpu.SMEM(names.shape, jnp.int32),
            pltpu.VMEM(resident.shape, jnp.float32),
            pltpu.VMEM(neighbour.shape, jnp.float32),
            pltpu.VMEM((NJ, 4, BLK, BLK), jnp.float32),
            pltpu.VMEM((RES + 1, 8, BLK), jnp.float32),
            pltpu.VMEM((NJ, 8, BLK), jnp.float32),
            pltpu.VMEM((PAIR_MAX, BLK, BLK), jnp.float32),
            pltpu.VMEM((NJ, BLK, BLK), jnp.bfloat16),
            pltpu.VMEM((RES, SQUARE_ROWS, BLK), jnp.bfloat16),
            pltpu.VMEM((WIDE, BLK, BLK), jnp.float32),
            pltpu.VMEM((WIDE, BLK, BLK), jnp.float32),
            pltpu.SMEM((8, PAIR_MAX), jnp.int32),
            pltpu.SemaphoreType.DMA((6,)),
            pltpu.SemaphoreType.DMA((PAIR_MAX // (2 * WIDE),)),
        ],
        compiler_params=pltpu.CompilerParams(vmem_limit_bytes=LIMIT),
    )(count, pairs, names, resident, neighbour)


def force_call(lists, shells, resident, neighbour, field, far, flag):
    return pl.pallas_call(
        force_kernel,
        out_shape=jax.ShapeDtypeStruct((3, RES * BLK), jnp.float32),
        in_specs=[ANY] * 7,
        out_specs=VMEM,
        scratch_shapes=[
            pltpu.SMEM(lists.shape, jnp.int32),
            pltpu.VMEM(resident.shape, jnp.float32),
            pltpu.VMEM(neighbour.shape, jnp.float32),
            pltpu.VMEM(field.shape, jnp.float32),
            pltpu.VMEM(far.shape, jnp.float32),
            pltpu.VMEM(flag.shape, jnp.int32),
            pltpu.VMEM((PAIR_MAX, BLK, BLK), jnp.float32),
            pltpu.VMEM((RES + 1, 8, BLK), jnp.float32),
            pltpu.VMEM((NJ, 16, BLK), jnp.float32),
            pltpu.VMEM((NJ, 48, 2 * BLK), jnp.bfloat16),
            pltpu.VMEM((NJ, 32, 2 * BLK), jnp.bfloat16),
            pltpu.VMEM((NJ, 8, BLK), jnp.float32),
            pltpu.VMEM((WIDE, 2 * BLK, BLK), jnp.bfloat16),
            pltpu.VMEM((WIDE, 2 * BLK, BLK), jnp.bfloat16),
            pltpu.SemaphoreType.DMA((PAIR_MAX // WIDE,)),
            pltpu.SemaphoreType.DMA((6,)),
        ],
        compiler_params=pltpu.CompilerParams(vmem_limit_bytes=LIMIT),
    )(lists, shells, resident, neighbour, field, far, flag)


def on_device(stay, leave, stay_flag, send_list, send_count, wanted, pair_tiles, pair_count):
    slabs = send_list.shape[1]
    members = wanted.shape[1]
    leaving = leave.reshape(7, slabs * SM, BLK).transpose(1, 0, 2)
    staying = stay.reshape(7, NSTAY, BLK).transpose(1, 0, 2)
    resident, neighbour, asked = migrate_call(
        slabs, members, send_list.transpose(0, 2, 1), send_count, wanted.transpose(0, 2, 1), leaving, staying
    )
    dens, field, lists, messages, shells = density_call(pair_count, pair_tiles[0], asked, resident, neighbour)
    far = field_call(slabs, members, messages)
    accel = force_call(lists, shells, resident, neighbour, field, far, stay_flag.reshape(NSTAY, BLK))
    return (dens.reshape(-1), accel)


def solution(mesh):
    in_specs = (
        P(None, ("slab", "grp")),
        P(None, ("slab", "grp")),
        P(("slab", "grp")),
        P(("slab", "grp"), None, None),
        P(("slab", "grp"), None),
        P(("slab", "grp"), None, None),
        P(("slab", "grp"), None, None),
        P(("slab", "grp")),
    )
    out_specs = (P(("slab", "grp")), P(None, ("slab", "grp")))
    return jax.shard_map(
        on_device, mesh=mesh, in_specs=in_specs, out_specs=out_specs, check_vma=False
    )
```

```python
import functools
import math

import jax
import jax.numpy as jnp
from jax import lax
from jax.experimental import pallas as pl
from jax.experimental.pallas import tpu as pltpu
from jax.sharding import PartitionSpec as P

BLK = 128
SM = 2
GH = 4
NEED = 4
PAIR_MAX = 256
NSTAY = 16
RES = 80
NJ = 40
GROUPS = BLK // 8
COLUMN_STEP = 8
SQUARE_STEP = 40
STEP = 4
WIDE = 8
AHEAD = 2
NARROW = 6.0
SQUARE_ROWS = 48
FACTOR_STEP = 20

KERNEL_NORM = 21.0 / (16.0 * math.pi)
SMOOTH = 1.0
HALF = 0.5 / SMOOTH
DENS_FLOOR = 0.5
STIFF = 0.02
VISCOUS = 0.1
GRAVITY = 1.0
TINY = 1e-30
FAR = 3e38
SOFT = 0.01 * HALF * HALF
PRESS_SCALE = 5.0 * KERNEL_NORM / (SMOOTH * SMOOTH) / HALF
VISC_SCALE = -VISCOUS * 5.0 * KERNEL_NORM / (SMOOTH * SMOOTH)

VMEM = pl.BlockSpec(memory_space=pltpu.VMEM)
SMEM = pl.BlockSpec(memory_space=pltpu.SMEM)
ANY = pl.BlockSpec(memory_space=pl.ANY)
MESH = pl.DeviceIdType.MESH
LIMIT = 56 * 1024 * 1024


def ring_steps(r, size):
    return min(r, size - r)


def migrate_kernel(
    slabs, members, lists_in, counts_in, wanted_in, leave, stay,
    res_out, nb_out, asked_out,
    lists, counts, wanted, leaving, staying, packed, res, edges, request, asked, names, chosen,
    row_send, row_recv, ghost_send, ghost_recv, name_send, name_recv, near_send, near_recv, local_sem,
):
    slab = lax.axis_index("slab")
    grp = lax.axis_index("grp")
    ghosts = members * NEED
    barrier = pltpu.get_barrier_semaphore()

    far_slabs = sorted(range(1, slabs), key=lambda r: -ring_steps(r // 8, 4) - ring_steps(r // 2 % 4, 4))
    far_members = sorted(range(1, members), key=lambda r: -ring_steps(r, members))
    for r in far_members:
        pl.semaphore_signal(barrier, inc=1, device_id={"grp": (grp + r) % members}, device_id_type=MESH)
    for r in far_slabs:
        pl.semaphore_signal(barrier, inc=1, device_id={"slab": (slab + r) % slabs}, device_id_type=MESH)
    fetch_leave = pltpu.make_async_copy(leave, leaving, local_sem.at[0])
    fetch_stay = pltpu.make_async_copy(stay, staying, local_sem.at[1])
    fetch_leave.start()
    fetch_stay.start()
    small = [
        pltpu.make_async_copy(source, target, local_sem.at[5 + n])
        for n, (source, target) in enumerate(((wanted_in, wanted), (lists_in, lists), (counts_in, counts)))
    ]
    for copy in small:
        copy.start()
    for copy in small:
        copy.wait()
    lane = lax.broadcasted_iota(jnp.int32, (1, BLK), 1)
    for p in range(members):
        ask = jnp.zeros((1, BLK), jnp.int32)
        for k in range(NEED):
            ask = jnp.where(lane == k, wanted[0, k, p], ask)
        request[p] = ask
    fetch_stay.wait()
    for b in range(NSTAY):
        res[b, 0:7, :] = staying[b]
        res[b, 7:8, :] = jnp.ones((1, BLK), jnp.float32)
    fetch_leave.wait()
    for t in range(slabs):
        count = counts[0, t]
        for k in range(SM):
            keep = jnp.broadcast_to(jnp.minimum(jnp.maximum(count - k, 0), 1), (1, BLK)).astype(jnp.float32)
            packed[t * SM + k, 0:7, :] = leaving[lists[0, k, t]] * keep
            packed[t * SM + k, 7:8, :] = keep
    pl.semaphore_wait(barrier, slabs - 1 + members - 1)

    def name_copy(r):
        target = (grp + r) % members
        return pltpu.make_async_remote_copy(
            src_ref=request.at[target], dst_ref=asked.at[grp], send_sem=name_send.at[r], recv_sem=name_recv.at[r],
            device_id={"grp": target}, device_id_type=MESH,
        )

    def row_copy(r):
        target = (slab + r) % slabs
        return pltpu.make_async_remote_copy(
            src_ref=packed.at[pl.ds(target * SM, SM)], dst_ref=res.at[pl.ds(NSTAY + slab * SM, SM)],
            send_sem=row_send.at[r], recv_sem=row_recv.at[r],
            device_id={"slab": target}, device_id_type=MESH,
        )

    def ghost_copy(side):
        first = NSTAY - GH if side == 0 else 0
        target = (slab + (1 if side == 0 else slabs - 1)) % slabs
        return pltpu.make_async_remote_copy(
            src_ref=res.at[pl.ds(first, GH)], dst_ref=edges.at[pl.ds(side * GH, GH)],
            send_sem=ghost_send.at[side], recv_sem=ghost_recv.at[side],
            device_id={"slab": target}, device_id_type=MESH,
        )

    def near_copy(r):
        target = (grp + r) % members
        return pltpu.make_async_remote_copy(
            src_ref=chosen.at[target], dst_ref=nb_out.at[pl.ds(grp * NEED, NEED)],
            send_sem=near_send.at[r], recv_sem=near_recv.at[r],
            device_id={"grp": target}, device_id_type=MESH,
        )

    def each(order, step):
        for r in order:
            step(r)

    each(far_members, lambda r: name_copy(r).start())
    each(far_slabs, lambda r: row_copy(r).start())
    ghost_copy(0).start()
    ghost_copy(1).start()
    asked[grp] = request[grp]
    mine = pl.ds(NSTAY + slab * SM, SM)
    res[mine] = packed[pl.ds(slab * SM, SM)]
    each(far_members, lambda r: name_copy(r).wait_recv())
    local = pltpu.make_async_copy(asked, names, local_sem.at[2])
    local.start()
    local.wait()
    store_asked = pltpu.make_async_copy(asked, asked_out, local_sem.at[8])
    store_asked.start()
    each(far_slabs, lambda r: row_copy(r).wait_recv())
    for d in range(members):
        for k in range(NEED):
            chosen[d, k] = res[names[d, 0, k]]
    each(far_members, lambda r: near_copy(r).start())
    store_own = pltpu.make_async_copy(chosen.at[grp], nb_out.at[pl.ds(grp * NEED, NEED)], local_sem.at[4])
    store_own.start()
    store_res = pltpu.make_async_copy(res, res_out, local_sem.at[3])
    store_res.start()
    ghost_copy(0).wait_recv()
    ghost_copy(1).wait_recv()
    for side, some in ((0, slab > 0), (1, slab < slabs - 1)):
        rows = pl.ds(side * GH, GH)
        edges[rows] = edges[rows] * some.astype(jnp.float32)
    store_edges = pltpu.make_async_copy(edges, nb_out.at[pl.ds(ghosts, 2 * GH)], local_sem.at[9])
    store_edges.start()
    each(far_members, lambda r: near_copy(r).wait_recv())
    each(far_members, lambda r: name_copy(r).wait_send())
    each(far_slabs, lambda r: row_copy(r).wait_send())
    each(far_members, lambda r: near_copy(r).wait_send())
    ghost_copy(0).wait_send()
    ghost_copy(1).wait_send()
    for store in (store_asked, store_own, store_res, store_edges):
        store.wait()


def migrate_call(slabs, members, lists, counts, wanted, leave, stay):
    blocks = NSTAY + slabs * SM
    near = members * NEED + 2 * GH
    f32 = jnp.float32
    dma = pltpu.SemaphoreType.DMA
    return pl.pallas_call(
        functools.partial(migrate_kernel, slabs, members),
        out_shape=(
            jax.ShapeDtypeStruct((blocks, 8, BLK), f32),
            jax.ShapeDtypeStruct((near, 8, BLK), f32),
            jax.ShapeDtypeStruct((members, 1, BLK), jnp.int32),
        ),
        in_specs=[ANY, ANY, ANY, ANY, ANY],
        out_specs=(ANY, ANY, ANY),
        scratch_shapes=[
            pltpu.SMEM(lists.shape, jnp.int32),
            pltpu.SMEM(counts.shape, jnp.int32),
            pltpu.SMEM(wanted.shape, jnp.int32),
            pltpu.VMEM(leave.shape, f32),
            pltpu.VMEM(stay.shape, f32),
            pltpu.VMEM((slabs * SM, 8, BLK), f32),
            pltpu.VMEM((blocks, 8, BLK), f32),
            pltpu.VMEM((2 * GH, 8, BLK), f32),
            pltpu.VMEM((members, 1, BLK), jnp.int32),
            pltpu.VMEM((members, 1, BLK), jnp.int32),
            pltpu.SMEM((members, 1, BLK), jnp.int32),
            pltpu.VMEM((members, NEED, 8, BLK), f32),
            dma((slabs,)), dma((slabs,)), dma((2,)), dma((2,)),
            dma((members,)), dma((members,)), dma((members,)), dma((members,)), dma((10,)),
        ],
        compiler_params=pltpu.CompilerParams(collective_id=0, has_side_effects=True, vmem_limit_bytes=LIMIT),
    )(lists, counts, wanted, leave, stay)


def field_kernel(slabs, members, messages, out, near_send, near_recv, edge_send, edge_recv, own_sem):
    slab = lax.axis_index("slab")
    grp = lax.axis_index("grp")
    above = (slab + 1) % slabs
    below = (slab + slabs - 1) % slabs
    far_members = sorted(range(1, members), key=lambda r: -ring_steps(r, members))
    barrier = pltpu.get_barrier_semaphore()
    for r in far_members:
        pl.semaphore_signal(barrier, inc=1, device_id={"grp": (grp + r) % members}, device_id_type=MESH)
    for target in (above, below):
        pl.semaphore_signal(barrier, inc=1, device_id={"slab": target}, device_id_type=MESH)
    own = pltpu.make_async_copy(messages.at[grp], out.at[grp], own_sem)
    own.start()
    pl.semaphore_wait(barrier, members + 1)

    def near_copy(r):
        target = (grp + r) % members
        return pltpu.make_async_remote_copy(
            src_ref=messages.at[target], dst_ref=out.at[grp], send_sem=near_send.at[r], recv_sem=near_recv.at[r],
            device_id={"grp": target}, device_id_type=MESH,
        )

    def edge_copy(side):
        return pltpu.make_async_remote_copy(
            src_ref=messages.at[members + side], dst_ref=out.at[members + side],
            send_sem=edge_send.at[side], recv_sem=edge_recv.at[side],
            device_id={"slab": above if side == 0 else below}, device_id_type=MESH,
        )

    copies = [near_copy(r) for r in far_members] + [edge_copy(0), edge_copy(1)]
    for copy in copies:
        copy.start()
    own.wait()
    for copy in copies:
        copy.wait_recv()
    for copy in copies:
        copy.wait_send()


def field_call(slabs, members, messages):
    dma = pltpu.SemaphoreType.DMA
    out = pl.pallas_call(
        functools.partial(field_kernel, slabs, members),
        out_shape=jax.ShapeDtypeStruct((members + 2, 8, BLK), jnp.float32),
        in_specs=[ANY],
        out_specs=ANY,
        scratch_shapes=[dma((members,)), dma((members,)), dma((2,)), dma((2,)), dma],
        compiler_params=pltpu.CompilerParams(collective_id=1, has_side_effects=True),
    )(messages)
    return out.reshape(-1, BLK)


def shell_of(radius2):
    square = jnp.maximum(radius2, TINY)
    return jnp.maximum(1.0 - square * lax.rsqrt(square), 0.0)


def weight_of(shell):
    square = shell * shell
    return square * square * (1.25 - shell)


def write_lists(count, pairs, res, nb, out):
    left = pairs[0:1, :]
    right = pairs[1:2, :]
    lane = lax.broadcasted_iota(jnp.int32, (1, PAIR_MAX), 1)
    res_live = res[:, 7, :]
    nb_live = nb[:, 7, :]
    res_live = jnp.concatenate([res_live, res_live], 1)
    nb_live = jnp.concatenate([nb_live, nb_live], 1)
    hit = lax.broadcasted_iota(jnp.int32, (RES, PAIR_MAX), 0) == left
    live_left = jnp.sum(jnp.where(hit, res_live, 0.0), 0, keepdims=True)
    hit = lax.broadcasted_iota(jnp.int32, (NJ, PAIR_MAX), 0) == right
    live_right = jnp.sum(jnp.where(hit, nb_live, 0.0), 0, keepdims=True)
    valid = jnp.where(lane < count, live_right, 0.0)
    heavy = valid * live_left
    light = valid * (1.0 - live_left)
    before = lax.broadcasted_iota(jnp.int32, (PAIR_MAX, PAIR_MAX), 0) < lax.broadcasted_iota(
        jnp.int32, (PAIR_MAX, PAIR_MAX), 1
    )
    blank = jnp.zeros((6, PAIR_MAX), jnp.float32)
    kinds = jnp.concatenate([heavy, light, blank], 0).astype(jnp.bfloat16)
    spots = jnp.dot(kinds, jnp.where(before, 1.0, 0.0).astype(jnp.bfloat16), preferred_element_type=jnp.float32)
    names = jnp.concatenate([left.astype(jnp.float32), right.astype(jnp.float32), blank], 0).astype(jnp.bfloat16)
    row = lax.broadcasted_iota(jnp.int32, (PAIR_MAX, PAIR_MAX), 0).astype(jnp.float32)
    sums = jnp.sum(jnp.concatenate([heavy, light, blank], 0), 1, keepdims=True)
    for kind, member in ((0, heavy), (1, light)):
        target = jnp.where(member > 0.5, spots[kind : kind + 1, :], -1.0)
        chosen = jnp.where(row == target, 1.0, 0.0).astype(jnp.bfloat16)
        packed = lax.dot_general(names, chosen, (((1,), (1,)), ((), ())), preferred_element_type=jnp.float32)
        amount = jnp.broadcast_to(sums[kind : kind + 1, :], (1, PAIR_MAX))
        filled = lane.astype(jnp.float32) < amount
        out[2 * kind : 2 * kind + 1, :] = jnp.where(filled, packed[0:1, :], float(RES)).astype(jnp.int32)
        out[2 * kind + 1 : 2 * kind + 2, :] = packed[1:2, :].astype(jnp.int32)
        out[4 + kind : 5 + kind, :] = amount.astype(jnp.int32)
    out[6:8, :] = jnp.zeros((2, PAIR_MAX), jnp.int32)


def box_of(tiles):
    live = jnp.broadcast_to(tiles[:, 7:8, :], tiles.shape) > 0.5
    least = jnp.min(jnp.where(live, tiles * HALF, FAR), 0)
    most = jnp.max(jnp.where(live, tiles * HALF, -FAR), 0)
    return jnp.min(least, 1, keepdims=True), jnp.max(most, 1, keepdims=True)


def square_rows(tile, centre, own, other):
    row = lax.broadcasted_iota(jnp.int32, (8, BLK), 0)
    place = jnp.where(row < 3, tile * HALF - centre, 0.0)
    square = jnp.broadcast_to(jnp.sum(place * place, 0, keepdims=True), (8, BLK))
    high, mid, low = (p.astype(jnp.float32) for p in pieces(jnp.where(row == own, square, place)))
    return row < 3, jnp.where(row == other, 1.0, 0.0), high, mid, low


def write_squares(res, nb, centre, left, right, table):
    left[...] = jnp.zeros_like(left)
    row = lax.broadcasted_iota(jnp.int32, (SQUARE_ROWS, BLK), 0)
    spread = jnp.where((row == 5) | (row == 13) | (row == 21), 4.0, 0.0).astype(jnp.bfloat16)
    eight = lax.broadcasted_iota(jnp.int32, (8, BLK), 0)

    def columns(step, carry):
        for u in range(SQUARE_STEP):
            j = step * SQUARE_STEP + u
            tile = nb[j]
            place, one, high, mid, low = square_rows(tile, centre, 3, 4)
            mass = jnp.where(eight == 5, jnp.broadcast_to(tile[6:7, :], (8, BLK)), 0.0)
            masses = [m.astype(jnp.float32) for m in pieces(mass)]
            stacked = jnp.concatenate(
                [
                    high + one + masses[0],
                    jnp.where(place, high, mid) + one + masses[1],
                    jnp.where(place, mid, low) + one + masses[2],
                    jnp.where(place, mid, 0.0),
                    jnp.where(place, high, 0.0),
                    jnp.where(place, low, 0.0),
                ],
                0,
            )
            turned = jnp.transpose(stacked, (1, 0)).astype(jnp.bfloat16)
            left[j, :, 0:SQUARE_ROWS] = turned
            table[j, 3] = jnp.dot(turned, spread, preferred_element_type=jnp.float32)
        return carry

    lax.fori_loop(0, NJ // SQUARE_STEP, columns, 0)

    def rows(step, carry):
        for u in range(SQUARE_STEP):
            i = step * SQUARE_STEP + u
            place, one, high, mid, low = square_rows(res[i], centre, 4, 3)
            twice = jnp.where(place, -2.0, 1.0)
            high, mid, low = high * twice, mid * twice, low * twice
            stacked = jnp.concatenate(
                [
                    high + one,
                    mid + one,
                    jnp.where(place, high, low) + one,
                    jnp.where(place, mid, 0.0),
                    jnp.where(place, low, 0.0),
                    jnp.where(place, high, 0.0),
                ],
                0,
            )
            right[i] = stacked.astype(jnp.bfloat16)
        return carry

    lax.fori_loop(0, RES // SQUARE_STEP, rows, 0)


def pieces(value):
    high = value.astype(jnp.bfloat16)
    rest = value - high.astype(jnp.float32)
    mid = rest.astype(jnp.bfloat16)
    low = (rest - mid.astype(jnp.float32)).astype(jnp.bfloat16)
    return high, mid, low


def write_columns(nb, table, fields):
    count = len(fields)
    row = lax.broadcasted_iota(jnp.int32, (32, count * BLK), 0)
    spot = lax.broadcasted_iota(jnp.int32, (32, count * BLK), 1) // BLK
    spread = jnp.zeros((32, count * BLK), jnp.float32)
    for n, (field, scale) in enumerate(fields):
        mine = (row == field) | (row == 8 + field) | (row == 16 + field)
        spread = jnp.where((spot == n) & mine, scale, spread)
    spread = spread.astype(jnp.bfloat16)

    def some(step, carry):
        for u in range(COLUMN_STEP):
            j = step * COLUMN_STEP + u
            high, mid, low = (p.astype(jnp.float32) for p in pieces(nb[j]))
            stacked = jnp.concatenate([high, mid, low, jnp.zeros((8, BLK), jnp.float32)], 0)
            turned = jnp.transpose(stacked, (1, 0)).astype(jnp.bfloat16)
            wide = jnp.dot(turned, spread, preferred_element_type=jnp.float32)
            for n in range(count):
                table[j, n] = wide[:, n * BLK : (n + 1) * BLK]
        return carry

    lax.fori_loop(0, NJ // COLUMN_STEP, some, 0)


def pieces(value):
    high = value.astype(jnp.bfloat16)
    rest = value - high.astype(jnp.float32)
    mid = rest.astype(jnp.bfloat16)
    low = (rest - mid.astype(jnp.float32)).astype(jnp.bfloat16)
    return high, mid, low


def write_columns(nb, table, fields):
    count = len(fields)
    row = lax.broadcasted_iota(jnp.int32, (32, count * BLK), 0)
    spot = lax.broadcasted_iota(jnp.int32, (32, count * BLK), 1) // BLK
    spread = jnp.zeros((32, count * BLK), jnp.float32)
    for n, (field, scale) in enumerate(fields):
        mine = (row == field) | (row == 8 + field) | (row == 16 + field)
        spread = jnp.where((spot == n) & mine, scale, spread)
    spread = spread.astype(jnp.bfloat16)

    def some(step, carry):
        for u in range(COLUMN_STEP):
            j = step * COLUMN_STEP + u
            high, mid, low = (p.astype(jnp.float32) for p in pieces(nb[j]))
            stacked = jnp.concatenate([high, mid, low, jnp.zeros((8, BLK), jnp.float32)], 0)
            turned = jnp.transpose(stacked, (1, 0)).astype(jnp.bfloat16)
            wide = jnp.dot(turned, spread, preferred_element_type=jnp.float32)
            for n in range(count):
                table[j, n] = wide[:, n * BLK : (n + 1) * BLK]
        return carry

    lax.fori_loop(0, NJ // COLUMN_STEP, some, 0)


def density_kernel(
    count_in, pairs_in, names_in, res_in, nb_in, dens_out, field_out, list_out, message_out, shell_out,
    count, pairs, names, res, nb, table, acc, origin, held, left, right, first, second, lists, sem, held_sem,
):
    members = names.shape[0]
    fetches = [
        pltpu.make_async_copy(source, target, sem.at[n])
        for n, (source, target) in enumerate(
            ((nb_in, nb), (res_in, res), (pairs_in, pairs), (count_in, count), (names_in, names))
        )
    ]
    for fetch in fetches:
        fetch.start()
    for fetch in fetches:
        fetch.wait()
    write_lists(count[0], pairs, res, nb, list_out)
    least, most = box_of(nb[...])
    least_res, most_res = box_of(res[...])
    least, most = jnp.minimum(least, least_res), jnp.maximum(most, most_res)
    centre = jnp.broadcast_to(0.5 * least + 0.5 * most, (8, BLK))
    spread = jnp.max((most - least)[0:3], 0, keepdims=True)
    list_out[6:7, :] = jnp.broadcast_to(jnp.where(spread <= NARROW, 1, 0), (1, PAIR_MAX))
    copy = pltpu.make_async_copy(list_out, lists, sem.at[5])
    copy.start()
    write_squares(res, nb, centre, left, right, table)
    x, y, z = (nb[:, f, :] * HALF for f in range(3))
    alone = jnp.sum(weight_of(shell_of(x * x + y * y + z * z)) * (4.0 * nb[:, 6, :]), 1, keepdims=True)
    origin[...] = jnp.zeros_like(origin)
    origin[:, 0, :] = jnp.broadcast_to(alone, (NJ, BLK))
    acc[...] = jnp.zeros_like(acc)
    copy.wait()
    steps = (lists[4, 0] + 2 * WIDE - 1) // (2 * WIDE)

    def shell_copy(step):
        rows = pl.ds(2 * WIDE * step, 2 * WIDE)
        return pltpu.make_async_copy(held.at[rows], shell_out.at[rows], held_sem.at[step])

    def whole(n, radius2_of):
        i = lists[0, n]
        j = lists[1, n]
        totals = [jnp.zeros((8, BLK), jnp.float32)] * 2
        for g in range(GROUPS):
            rows = pl.ds(8 * g, 8)
            shell = shell_of(radius2_of(i, j, rows))
            held[n, rows, :] = shell
            totals[g % 2] = totals[g % 2] + weight_of(shell) * table[j, 3, rows, :]
        acc[i] = acc[i] + (totals[0] + totals[1])

    @pl.when(lists[6, 0] == 1)
    def _():
        def squares(n, into):
            for u in range(WIDE):
                m = jnp.minimum(n + u, PAIR_MAX - 1)
                own = jnp.minimum(lists[0, m], RES - 1)
                columns = left[lists[1, m], :, 0:SQUARE_ROWS]
                into[u] = jnp.dot(columns, right[own], preferred_element_type=jnp.float32)

        def step_of(step, carry):
            n = 2 * WIDE * step
            squares(n + WIDE, second)
            for u in range(WIDE):
                whole(n + u, lambda i, j, rows: first[u, rows, :])
            squares(n + 2 * WIDE, first)
            for u in range(WIDE):
                whole(n + WIDE + u, lambda i, j, rows: second[u, rows, :])
            shell_copy(step).start()
            return carry

        squares(0, first)
        lax.fori_loop(0, steps, step_of, 0)

    @pl.when(lists[6, 0] == 0)
    def _():
        write_columns(nb, table, ((0, HALF), (1, HALF), (2, HALF), (6, 4.0)))

        def direct(i, j, rows):
            own = jnp.minimum(i, RES - 1)
            dx, dy, dz = (res[own, f : f + 1, :] * HALF - table[j, f, rows, :] for f in range(3))
            return dx * dx + dy * dy + dz * dz

        def step_of(step, carry):
            def part(quarter, carry):
                for u in range(STEP):
                    whole(2 * WIDE * step + STEP * quarter + u, direct)
                return carry

            lax.fori_loop(0, 2 * WIDE // STEP, part, 0)
            shell_copy(step).start()
            return carry

        lax.fori_loop(0, steps, step_of, 0)

    def blank(step, carry):
        for u in range(STEP):
            i = lists[2, STEP * step + u]
            acc[i] = acc[i] + origin[lists[3, STEP * step + u]]
        return carry

    lax.fori_loop(0, (lists[5, 0] + STEP - 1) // STEP, blank, 0)
    dens = jnp.sum(acc[0:RES], 1) * KERNEL_NORM
    dens_out[...] = dens
    inverse = 1.0 / jnp.maximum(dens, DENS_FLOOR)
    cube = dens * dens * dens
    field_out[:, 0, :] = STIFF * (cube * cube * dens - 1.0) * inverse * inverse
    field_out[:, 1, :] = res[:, 6, :] * inverse
    for d in range(members):
        for k in range(NEED):
            message_out[d, 2 * k : 2 * k + 2, :] = field_out[names[d, 0, k]]
    for k in range(GH):
        message_out[members, 2 * k : 2 * k + 2, :] = field_out[NSTAY - GH + k]
        message_out[members + 1, 2 * k : 2 * k + 2, :] = field_out[k]

    def settle(step, carry):
        shell_copy(step).wait()
        return carry

    lax.fori_loop(0, steps, settle, 0)


def two_pieces(value):
    high = value.astype(jnp.bfloat16)
    return high, (value - high.astype(jnp.float32)).astype(jnp.bfloat16)


def write_factors(nb, far, press, damp, centre):
    row = lax.broadcasted_iota(jnp.int32, (8, BLK), 0)
    upper = row < 3
    lower = (row >= 3) & (row < 6)

    def store(ref, j, tiles):
        for h in range(0, len(tiles), 2):
            pair = jnp.concatenate([tiles[h].astype(jnp.float32), tiles[h + 1].astype(jnp.float32)], 0)
            pair = pair.astype(jnp.bfloat16)
            rows = pl.ds(8 * h, 16)
            ref[j, rows, 0:BLK] = pair
            ref[j, rows, BLK : 2 * BLK] = pair

    def some(step, carry):
        for u in range(FACTOR_STEP):
            j = step * FACTOR_STEP + u
            tile = nb[j]
            mass = jnp.broadcast_to(tile[6:7, :], (8, BLK))
            scaled = tile * HALF
            middle = jnp.where(upper, jnp.broadcast_to(scaled[:, 0:1], (8, BLK)), 0.0)
            centre[j] = middle
            place = scaled - middle
            mass_q = mass * jnp.broadcast_to(far[pl.ds(2 * j, 1), :], (8, BLK))
            mass_s = mass * jnp.broadcast_to(far[pl.ds(2 * j + 1, 1), :], (8, BLK))
            first = jnp.where(upper, mass * place, jnp.where(row == 6, mass, jnp.where(row == 7, mass_q, 0.0)))
            second = jnp.where(upper, mass_q * place, 0.0)
            third = jnp.where(lower, mass_s * tile, jnp.where(row == 6, mass_s, 0.0))
            store(press, j, [p for both in zip(pieces(first), pieces(second)) for p in both])
            store(damp, j, [*pieces(third), jnp.zeros((8, BLK), jnp.bfloat16)])
        return carry

    lax.fori_loop(0, NJ // FACTOR_STEP, some, 0)


def force_kernel(
    lists_in, shells, res_in, nb_in, field_in, far_in, flag_in, out,
    lists, res, nb, field, far, flag, held, acc, origin, press, damp, centre, cubes, damps, sem, fetch_sem,
):
    fetches = [
        pltpu.make_async_copy(source, target, fetch_sem.at[n])
        for n, (source, target) in enumerate(
            ((lists_in, lists), (nb_in, nb), (far_in, far), (res_in, res), (field_in, field), (flag_in, flag))
        )
    ]

    def shell_copy(step):
        rows = pl.ds(WIDE * step, WIDE)
        return pltpu.make_async_copy(shells.at[rows], held.at[rows], sem.at[step])

    for fetch in fetches[0:3]:
        fetch.start()
    for step in range(AHEAD):
        shell_copy(step).start()
    for fetch in fetches[3:]:
        fetch.start()
    fetches[0].wait()
    steps = (lists[4, 0] + WIDE - 1) // WIDE

    def fetch(step, carry):
        shell_copy(step).start()
        return carry

    lax.fori_loop(AHEAD, steps, fetch, 0)
    fetches[1].wait()
    fetches[2].wait()
    write_factors(nb, far, press, damp, centre)
    acc[...] = jnp.zeros_like(acc)
    row = lax.broadcasted_iota(jnp.int32, (8, BLK), 0)
    upper = row < 3
    lower = (row >= 3) & (row < 6)
    scale = jnp.where(upper, HALF, 1.0)

    x, y, z = (nb[:, f, :] * HALF for f in range(3))
    radius2 = x * x + y * y + z * z
    shell = shell_of(radius2)
    cube = shell * shell * shell * nb[:, 6, :]
    drag = cube * radius2 / (radius2 + SOFT) * far[pl.ds(1, NJ, stride=2), :]
    push = cube * far[pl.ds(0, NJ, stride=2), :]
    origin[...] = jnp.zeros_like(origin)
    for f, place in enumerate((x, y, z)):
        origin[:, f, :] = jnp.broadcast_to(jnp.sum(cube * place, 1, keepdims=True), (NJ, BLK))
        origin[:, 8 + f, :] = jnp.broadcast_to(jnp.sum(push * place, 1, keepdims=True), (NJ, BLK))
        origin[:, 3 + f, :] = jnp.broadcast_to(jnp.sum(drag * nb[:, 3 + f, :], 1, keepdims=True), (NJ, BLK))

    def coefficients(i):
        q = jnp.broadcast_to(field[i, 0:1, :], (8, BLK))
        s = jnp.broadcast_to(field[i, 1:2, :], (8, BLK))
        return jnp.where(upper, q, jnp.where(lower, s, 0.0))

    def geometry(u, n):
        for g in range(GROUPS // 2):
            rows = pl.ds(16 * g, 16)
            shell = held[n, rows, :]
            ratio = 1.0 - shell
            radius2 = ratio * ratio
            cube = shell * shell * shell
            soft = lax.rsqrt(radius2 + SOFT)
            high, low = two_pieces(cube)
            cubes[u, rows, :] = high
            cubes[u, pl.ds(BLK + 16 * g, 16), :] = low
            high, low = two_pieces(cube * (radius2 * (soft * soft)))
            damps[u, rows, :] = high
            damps[u, pl.ds(BLK + 16 * g, 16), :] = low

    def sums_of(u, j):
        first = jnp.dot(press[j], cubes[u], preferred_element_type=jnp.float32)
        second = jnp.dot(damp[j], damps[u], preferred_element_type=jnp.float32)
        return first[0:16] + (first[16:32] + first[32:48]), second[0:8] + (second[8:16] + second[16:24])

    def whole(step, before):
        @pl.when(step < jnp.maximum(steps, AHEAD))
        def _():
            shell_copy(step).wait()

        sums = [sums_of(u, j) for u, (i, j) in enumerate(before)]
        after = []
        for u in range(WIDE):
            n = jnp.minimum(WIDE * step + u, PAIR_MAX - 1)
            geometry(u, n)
            after.append((lists[0, n], lists[1, n]))
        for u, (i, j) in enumerate(before):
            own = jnp.minimum(i, RES - 1)
            first, second = sums[u]
            place = res[own] * scale - centre[j]
            one, two = first[0:8], first[8:16]
            both = jnp.where(upper, jnp.broadcast_to(one[6:7], (8, BLK)), jnp.broadcast_to(second[6:7], (8, BLK)))
            only = jnp.where(upper, jnp.broadcast_to(one[7:8], (8, BLK)), 0.0)
            part = coefficients(own) * (place * both - (one + second)) + (place * only - two)
            acc[i] = acc[i] + part
        return tuple(after)

    for copy in fetches[3:]:
        copy.wait()
    nowhere = tuple((jnp.int32(RES), jnp.int32(0)) for _ in range(WIDE))
    lax.fori_loop(0, steps + 1, whole, nowhere)
    for step in range(1, AHEAD):

        @pl.when(step > steps)
        def _():
            shell_copy(step).wait()


    def blank(step, carry):
        for u in range(STEP):
            i = lists[2, STEP * step + u]
            j = lists[3, STEP * step + u]
            own = jnp.minimum(i, RES - 1)
            acc[i] = acc[i] - (coefficients(own) * origin[j, 0:8, :] + origin[j, 8:16, :])
        return carry

    lax.fori_loop(0, (lists[5, 0] + STEP - 1) // STEP, blank, 0)
    gravity = jnp.where(lax.broadcasted_iota(jnp.int32, (3, BLK), 0) == 2, -GRAVITY, 0.0)
    for b in range(RES):
        total = acc[b, 0:3, :] * PRESS_SCALE + acc[b, 3:6, :] * VISC_SCALE + gravity
        if b < NSTAY:
            total = total * (1.0 - flag[b : b + 1, :].astype(jnp.float32))
        out[:, b * BLK : (b + 1) * BLK] = total


def density_call(count, pairs, names, resident, neighbour):
    members = names.shape[0]
    return pl.pallas_call(
        density_kernel,
        out_shape=(
            jax.ShapeDtypeStruct((RES, BLK), jnp.float32),
            jax.ShapeDtypeStruct((RES, 2, BLK), jnp.float32),
            jax.ShapeDtypeStruct((8, PAIR_MAX), jnp.int32),
            jax.ShapeDtypeStruct((members + 2, 8, BLK), jnp.float32),
            jax.ShapeDtypeStruct((PAIR_MAX, BLK, BLK), jnp.float32),
        ),
        in_specs=[ANY] * 5,
        out_specs=(VMEM, VMEM, VMEM, VMEM, ANY),
        scratch_shapes=[
            pltpu.SMEM(count.shape, jnp.int32),
            pltpu.VMEM(pairs.shape, jnp.int32),
            pltpu.SMEM(names.shape, jnp.int32),
            pltpu.VMEM(resident.shape, jnp.float32),
            pltpu.VMEM(neighbour.shape, jnp.float32),
            pltpu.VMEM((NJ, 4, BLK, BLK), jnp.float32),
            pltpu.VMEM((RES + 1, 8, BLK), jnp.float32),
            pltpu.VMEM((NJ, 8, BLK), jnp.float32),
            pltpu.VMEM((PAIR_MAX, BLK, BLK), jnp.float32),
            pltpu.VMEM((NJ, BLK, BLK), jnp.bfloat16),
            pltpu.VMEM((RES, SQUARE_ROWS, BLK), jnp.bfloat16),
            pltpu.VMEM((WIDE, BLK, BLK), jnp.float32),
            pltpu.VMEM((WIDE, BLK, BLK), jnp.float32),
            pltpu.SMEM((8, PAIR_MAX), jnp.int32),
            pltpu.SemaphoreType.DMA((6,)),
            pltpu.SemaphoreType.DMA((PAIR_MAX // (2 * WIDE),)),
        ],
        compiler_params=pltpu.CompilerParams(vmem_limit_bytes=LIMIT),
    )(count, pairs, names, resident, neighbour)


def force_call(lists, shells, resident, neighbour, field, far, flag):
    return pl.pallas_call(
        force_kernel,
        out_shape=jax.ShapeDtypeStruct((3, RES * BLK), jnp.float32),
        in_specs=[ANY] * 7,
        out_specs=VMEM,
        scratch_shapes=[
            pltpu.SMEM(lists.shape, jnp.int32),
            pltpu.VMEM(resident.shape, jnp.float32),
            pltpu.VMEM(neighbour.shape, jnp.float32),
            pltpu.VMEM(field.shape, jnp.float32),
            pltpu.VMEM(far.shape, jnp.float32),
            pltpu.VMEM(flag.shape, jnp.int32),
            pltpu.VMEM((PAIR_MAX, BLK, BLK), jnp.float32),
            pltpu.VMEM((RES + 1, 8, BLK), jnp.float32),
            pltpu.VMEM((NJ, 16, BLK), jnp.float32),
            pltpu.VMEM((NJ, 48, 2 * BLK), jnp.bfloat16),
            pltpu.VMEM((NJ, 32, 2 * BLK), jnp.bfloat16),
            pltpu.VMEM((NJ, 8, BLK), jnp.float32),
            pltpu.VMEM((WIDE, 2 * BLK, BLK), jnp.bfloat16),
            pltpu.VMEM((WIDE, 2 * BLK, BLK), jnp.bfloat16),
            pltpu.SemaphoreType.DMA((PAIR_MAX // WIDE,)),
            pltpu.SemaphoreType.DMA((6,)),
        ],
        compiler_params=pltpu.CompilerParams(vmem_limit_bytes=LIMIT),
    )(lists, shells, resident, neighbour, field, far, flag)


def on_device(stay, leave, stay_flag, send_list, send_count, wanted, pair_tiles, pair_count):
    slabs = send_list.shape[1]
    members = wanted.shape[1]
    leaving = leave.reshape(7, slabs * SM, BLK).transpose(1, 0, 2)
    staying = stay.reshape(7, NSTAY, BLK).transpose(1, 0, 2)
    resident, neighbour, asked = migrate_call(
        slabs, members, send_list.transpose(0, 2, 1), send_count, wanted.transpose(0, 2, 1), leaving, staying
    )
    dens, field, lists, messages, shells = density_call(pair_count, pair_tiles[0], asked, resident, neighbour)
    far = field_call(slabs, members, messages)
    accel = force_call(lists, shells, resident, neighbour, field, far, stay_flag.reshape(NSTAY, BLK))
    return (dens.reshape(-1), accel)


def solution(mesh):
    in_specs = (
        P(None, ("slab", "grp")),
        P(None, ("slab", "grp")),
        P(("slab", "grp")),
        P(("slab", "grp"), None, None),
        P(("slab", "grp"), None),
        P(("slab", "grp"), None, None),
        P(("slab", "grp"), None, None),
        P(("slab", "grp")),
    )
    out_specs = (P(("slab", "grp")), P(None, ("slab", "grp")))
    return jax.shard_map(
        on_device, mesh=mesh, in_specs=in_specs, out_specs=out_specs, check_vma=False
    )
```
